32 devices in a mesh: dp: 4 (over x, core), blk: 8 (over z, y).
Axes of the slice: x: 2, y: 2, z: 4, core: 2. Of those that a mesh axis runs over, the one named last changes fastest.
Arguments:
- inputs: bfloat16 [4, 1024, 768], P('dp'), may hold values from -6 to 6
- memory: bfloat16 [4, 1024, 768], P('dp', 'blk'), may hold values from -6 to 6
- lengths: int32 [4], P('dp'), may hold values from 129 to 1024, as said below
- cotangent: bfloat16 [4, 1024, 768], P('dp'), may hold values from -6 to 6
- self_query: bfloat16 [768, 768], replicated, may hold values from -0.21875 to 0.21875
- self_key: bfloat16 [768, 768], replicated, may hold values from -0.21875 to 0.21875
- self_value: bfloat16 [768, 768], replicated, may hold values from -0.21875 to 0.21875
- self_out: bfloat16 [768, 768], replicated, may hold values from -2.5 to 2.5
- self_bias: bfloat16 [768, 3], replicated, may hold values from -1.796875 to 1.796875
- cross_query: bfloat16 [768, 768], replicated, may hold values from -0.21875 to 0.21875
- cross_key: bfloat16 [768, 768], replicated, may hold values from -0.21875 to 0.21875
- cross_value: bfloat16 [768, 768], replicated, may hold values from -0.21875 to 0.21875
- cross_out: bfloat16 [768, 768], replicated, may hold values from -3.5 to 3.5
- cross_bias: bfloat16 [768, 2], replicated, may hold values from -1.796875 to 1.796875
- cross_value_bias: bfloat16 [768], replicated, may hold values from -1.796875 to 1.796875
- norm_gain: bfloat16 [768, 3], replicated, may hold values from 0.5 to 1.5
- norm_bias: bfloat16 [768, 3], replicated, may hold values from -1.796875 to 1.796875
- ffn_in: bfloat16 [768, 3072], replicated, may hold values from -0.21875 to 0.21875
- ffn_in_bias: bfloat16 [3072], replicated, may hold values from -1.796875 to 1.796875
- ffn_out: bfloat16 [3072, 768], replicated, may hold values from -0.109375 to 0.109375
- ffn_out_bias: bfloat16 [768], replicated, may hold values from -1.796875 to 1.796875
Outputs:
- out: bfloat16 [4, 1024, 768], P('dp')
- input_grad: bfloat16 [4, 1024, 768], P('dp')
- memory_grad: bfloat16 [4, 1024, 768], P('dp', 'blk')
- grad_self_query: float32 [768, 768], P('dp')
- grad_self_key: float32 [768, 768], P('dp')
- grad_self_value: float32 [768, 768], P('dp')
- grad_self_out: float32 [768, 768], P('dp')
- grad_self_bias: float32 [768, 3], P('dp')
- grad_cross_query: float32 [768, 768], P('dp')
- grad_cross_key: float32 [768, 768], P('dp')
- grad_cross_value: float32 [768, 768], P('dp')
- grad_cross_out: float32 [768, 768], P('dp')
- grad_cross_bias: float32 [768, 2], P('dp')
- grad_cross_value_bias: float32 [768], P('dp')
- grad_norm_gain: float32 [768, 3], P('dp')
- grad_norm_bias: float32 [768, 3], P('dp')
- grad_ffn_in: float32 [768, 3072], P('dp')
- grad_ffn_in_bias: float32 [3072], P('dp')
- grad_ffn_out: float32 [3072, 768], P('dp')
- grad_ffn_out_bias: float32 [768], P('dp')
The draws below stay inside these ranges and needn't reach their ends.
Inputs may be any that keep to these rules, and one draw needn't show every extreme that they name: `lengths`: positions below an item's length are live. Of the 4 items one has length 1024; each other item's length lies in the upper half of a bucket of 256, 512 or 1024 positions.
All inputs are finite; a program needn't handle non-finite values.
Results may differ from the reference program's by a relative error of at most 0.035.
Values may be sent and summed in bfloat16 or wider, within the bound.
A program may use at most 256 MiB of HBM per device.

```python
import jax
import jax.numpy as jnp
from jax import lax

D = 768
HEADS = 12
HEAD = 64
FF = 3072
TGT = 1024
ITEMS = 1
BATCH = 4
SRC = 1024


def draw_lengths(key, part):
    key = jax.random.fold_in(key, 7)
    bucket_key, length_key, pick_key = jax.random.split(key, 3)
    buckets = jax.random.randint(bucket_key, (BATCH,), 0, 3)
    ceilings = jnp.where(buckets == 0, SRC // 4, jnp.where(buckets == 1, SRC // 2, SRC))
    lowest = ceilings // 2 + 1
    noise = jax.random.randint(length_key, (BATCH,), 0, 1 << 20)
    drawn = lowest + noise % (ceilings - lowest + 1)
    chosen = jax.random.randint(pick_key, (BATCH // ITEMS,), 0, ITEMS)
    indices = jnp.arange(BATCH)
    full_item = indices % ITEMS == chosen[indices // ITEMS]
    return jnp.where(full_item, SRC, drawn).astype(jnp.int32)


def shard_levels(stream_key, shape, shards, smallest, high):
    def one(dim, shards_of):
        draws = jax.random.uniform(jax.random.fold_in(jax.random.fold_in(stream_key, 6), dim), (shards_of,), jnp.float32, smallest / len(shards), high / len(shards))
        return jnp.repeat(jnp.exp(draws), shape[dim] // shards_of).reshape((-1,) + (1,) * (len(shape) - dim - 1))

    gain = one(*shards[0])
    for cut in shards[1:]:
        gain = gain * one(*cut)
    return gain


def scatter_about(own_key, shape, spread, reach, cuts=(), kind=jnp.bfloat16):
    level = shard_levels(own_key, shape, cuts, -0.22, 0.18) if cuts else 1.0
    values = jax.random.normal(own_key, shape, jnp.float32) * spread * level
    return jnp.minimum(jnp.maximum(values, -reach), reach).astype(kind)


def setup_inputs(seed: int = 0) -> dict:
    seeds = jax.random.split(jax.random.key(seed), 22)
    inputs = scatter_about(seeds[0], (BATCH, TGT, D), 1.0, 6.0, ((0, 4),))
    memory = scatter_about(seeds[1], (BATCH, SRC, D), 1.0, 6.0, ((0, 4), (1, 8)))
    lengths = draw_lengths(jax.random.fold_in(seeds[21], 71), 0)
    cotangent = scatter_about(seeds[3], (BATCH, TGT, D), 1.0, 6.0, ((0, 4),))
    self_query = scatter_about(seeds[4], (D, D), D ** -0.5, 0.21875)
    self_key = scatter_about(seeds[5], (D, D), D ** -0.5, 0.21875)
    self_value = scatter_about(seeds[6], (D, D), D ** -0.5, 0.21875)
    self_out = scatter_about(seeds[7], (D, D), (max(D // 128, 1)) ** -0.5, 2.5)
    self_bias = scatter_about(seeds[8], (D, 3), 0.3, 1.796875)
    cross_query = scatter_about(seeds[9], (D, D), D ** -0.5, 0.21875)
    cross_key = scatter_about(seeds[10], (D, D), D ** -0.5, 0.21875)
    cross_value = scatter_about(seeds[11], (D, D), D ** -0.5, 0.21875)
    cross_out = scatter_about(seeds[12], (D, D), (max(D // 256, 1)) ** -0.5, 3.5)
    cross_bias = scatter_about(seeds[13], (D, 2), 0.3, 1.796875)
    cross_value_bias = scatter_about(seeds[14], (D,), 0.3, 1.796875)
    norm_gain = jnp.clip(1.0 + 0.1 * jax.random.normal(seeds[15], (D, 3), jnp.float32), 0.5, 1.5).astype(jnp.bfloat16)
    norm_bias = scatter_about(seeds[16], (D, 3), 0.3, 1.796875)
    ffn_in = scatter_about(seeds[17], (D, FF), D ** -0.5, 0.21875)
    ffn_in_bias = scatter_about(seeds[18], (FF,), 0.3, 1.796875)
    ffn_out = scatter_about(seeds[19], (FF, D), FF ** -0.5, 0.109375)
    ffn_out_bias = scatter_about(seeds[20], (D,), 0.3, 1.796875)
    return {"inputs": inputs, "memory": memory, "lengths": lengths, "cotangent": cotangent, "self_query": self_query, "self_key": self_key, "self_value": self_value, "self_out": self_out, "self_bias": self_bias, "cross_query": cross_query, "cross_key": cross_key, "cross_value": cross_value, "cross_out": cross_out, "cross_bias": cross_bias, "cross_value_bias": cross_value_bias, "norm_gain": norm_gain, "norm_bias": norm_bias, "ffn_in": ffn_in, "ffn_in_bias": ffn_in_bias, "ffn_out": ffn_out, "ffn_out_bias": ffn_out_bias}


NEG = -1e+30
EPS = 1e-05
SCALE = 0.125

@jax.custom_vjp
def low(v):
    return lax.optimization_barrier(v.astype(jnp.bfloat16)).astype(jnp.float32)

@jax.custom_vjp
def low_back(v):
    return v

def low_keep(v):
    return (low(v), None)

def low_pass(kept, grad):
    return (grad,)

def back_keep(v):
    return (v, None)

def back_low(kept, grad):
    return (low(grad),)
low.defvjp(low_keep, low_pass)
low_back.defvjp(back_keep, back_low)

def both_ways(values):
    return low(low_back(values))

def matmul(left_side, right_side):
    return jnp.dot(left_side, right_side, precision=lax.Precision.HIGHEST)

def layer_norm(residual, gain_col, shift_col):
    average = lax.optimization_barrier(jnp.mean(residual, axis=-1, keepdims=True))
    centered = residual - average
    variance = lax.optimization_barrier(jnp.mean(centered * centered, axis=-1, keepdims=True))
    return centered * lax.rsqrt(variance + EPS) * gain_col + shift_col

def split_heads(values):
    return values.reshape(values.shape[0], HEADS, HEAD)

def attention(query_rows, key_rows, value_rows, allowed):
    block_rows = min(512, TGT)

    def one_block(row_start):
        picked = lax.dynamic_slice_in_dim(query_rows, row_start, block_rows, 0)
        scores = low_back(jnp.einsum('qhe,khe->hqk', picked, key_rows, precision=lax.Precision.HIGHEST))
        scores = jnp.where(allowed(row_start)[None, :, :], scores, NEG)
        totals = jax.nn.logsumexp(scores, axis=-1, keepdims=True)
        weights = low(jnp.exp(scores - totals))
        return jnp.einsum('hqk,khe->qhe', weights, value_rows, precision=lax.Precision.HIGHEST)
    starts = jnp.arange(TGT // block_rows, dtype=jnp.int32) * block_rows
    pieces = lax.map(jax.checkpoint(one_block), starts)
    return pieces.reshape(TGT, D)

def item_forward(tokens, source, length, params):
    self_query, self_key, self_value, self_out, self_bias, cross_query, cross_key, cross_value, cross_out, cross_bias, cross_value_bias, norm_gain, norm_bias, ffn_in, ffn_in_bias, ffn_out, ffn_out_bias = params
    block_rows = min(512, TGT)
    positions = jnp.arange(TGT, dtype=jnp.int32)
    sources = jnp.arange(SRC, dtype=jnp.int32)

    def causal(row_start):
        return positions[None, :] <= row_start + jnp.arange(block_rows, dtype=jnp.int32)[:, None]

    def within(row_start):
        return jnp.broadcast_to((sources < length)[None, :], (block_rows, SRC))
    query_self = both_ways((matmul(tokens, self_query) + self_bias[:, 0]) * SCALE)
    key_self = both_ways(matmul(tokens, self_key))
    value_self = both_ways(matmul(tokens, self_value) + self_bias[:, 1])
    self_attn = both_ways(attention(split_heads(query_self), split_heads(key_self), split_heads(value_self), causal))
    self_branch = low_back(matmul(self_attn, self_out) + self_bias[:, 2])
    hidden_one = layer_norm(tokens + self_branch, norm_gain[:, 0], norm_bias[:, 0])
    hidden_low = low(hidden_one)
    query_cross = both_ways((matmul(hidden_low, cross_query) + cross_bias[:, 0]) * SCALE)
    key_cross = both_ways(matmul(source, cross_key))
    value_cross = both_ways(matmul(source, cross_value) + cross_value_bias)
    cross_attn = both_ways(attention(split_heads(query_cross), split_heads(key_cross), split_heads(value_cross), within))
    cross_branch = low_back(matmul(cross_attn, cross_out) + cross_bias[:, 1])
    hidden_two = layer_norm(hidden_one + cross_branch, norm_gain[:, 1], norm_bias[:, 1])
    second_low = low(hidden_two)
    pre_act = low_back(matmul(second_low, ffn_in) + ffn_in_bias)
    activated = low(jax.nn.gelu(pre_act, approximate=False))
    ffn_branch = low_back(matmul(activated, ffn_out) + ffn_out_bias)
    return layer_norm(hidden_two + ffn_branch, norm_gain[:, 2], norm_bias[:, 2])

def reference(inputs, memory, lengths, cotangent, self_query, self_key, self_value, self_out, self_bias, cross_query, cross_key, cross_value, cross_out, cross_bias, cross_value_bias, norm_gain, norm_bias, ffn_in, ffn_in_bias, ffn_out, ffn_out_bias):
    params = tuple((weight.astype(jnp.float32) for weight in (self_query, self_key, self_value, self_out, self_bias, cross_query, cross_key, cross_value, cross_out, cross_bias, cross_value_bias, norm_gain, norm_bias, ffn_in, ffn_in_bias, ffn_out, ffn_out_bias)))

    def one_item(running, item_data):
        tokens, source, length, grad_out = item_data

        def forward(tokens_in, source_in, params_in):
            return item_forward(tokens_in, source_in, length, params_in)
        result, backward = jax.vjp(forward, tokens.astype(jnp.float32), source.astype(jnp.float32), params)
        grad_tokens, grad_source, grad_params = backward(grad_out.astype(jnp.float32))
        running = jax.tree.map(jnp.add, running, grad_params)
        return (running, (result.astype(jnp.bfloat16), grad_tokens.astype(jnp.bfloat16), grad_source.astype(jnp.bfloat16)))
    initial = jax.tree.map(jnp.zeros_like, params)
    totals, stacked = lax.scan(one_item, initial, (inputs, memory, lengths, cotangent))
    out_all, grad_in, grad_mem = stacked
    return (out_all, grad_in, grad_mem, totals[0], totals[1], totals[2], totals[3], totals[4], totals[5], totals[6], totals[7], totals[8], totals[9], totals[10], totals[11], totals[12], totals[13], totals[14], totals[15], totals[16])
```

```python
import functools

import jax
import jax.numpy as jnp
from jax import lax
from jax.experimental import pallas as pl
from jax.experimental.pallas import tpu as pltpu
from jax.sharding import PartitionSpec as P

D = 768
HEADS = 12
HEAD = 64
FF = 3072
TGT = 1024
ITEMS = 1


NEG = -1e30
EPS = 1e-05
SCALE = 0.125
BF = jnp.bfloat16
F32 = jnp.float32
MESH = pl.DeviceIdType.MESH
VMEM = pl.BlockSpec(memory_space=pltpu.VMEM)
SMEM = pl.BlockSpec(memory_space=pltpu.SMEM)
ANY = pl.BlockSpec(memory_space=pl.ANY)
LIMIT = 60 * 2**20


def dot(a, b):
    return jnp.dot(a, b, preferred_element_type=F32)


def dot_nt(a, b):
    return lax.dot_general(a, b, (((1,), (1,)), ((), ())), preferred_element_type=F32)


def dot_tn(a, b):
    return lax.dot_general(a, b, (((0,), (0,)), ((), ())), preferred_element_type=F32)


def lanes(shape):
    return lax.broadcasted_iota(jnp.int32, shape, 1)


def norm_parts(residual):
    centered = residual - jnp.mean(residual, axis=-1, keepdims=True)
    inv = lax.rsqrt(jnp.mean(centered * centered, axis=-1, keepdims=True) + EPS)
    return centered * inv, inv


def norm_grad(gradient, normed, inv, gain):
    scaled = gradient * gain
    return (
        scaled
        - jnp.mean(scaled, axis=-1, keepdims=True)
        - normed * jnp.mean(scaled * normed, axis=-1, keepdims=True)
    ) * inv


def gelu_parts(values):
    cdf = 0.5 * (1.0 + lax.erf(values * 0.7071067811865476))
    slope = cdf + values * (jnp.exp(-0.5 * values * values) * 0.3989422804014327)
    return values * cdf, slope


def col_sum(values):
    return jnp.sum(values, axis=0, keepdims=True)


class Gather:
    def __init__(self, buf, send, recv, slots):
        self.buf, self.send, self.recv, self.nz = buf, send, recv, slots // 2
        self.me = lax.axis_index("blk")
        self.y, self.z = self.me % 2, self.me // 2

    def _copy(self, slot, z, y, sem):
        return pltpu.make_async_remote_copy(
            src_ref=self.buf.at[slot],
            dst_ref=self.buf.at[slot],
            send_sem=self.send.at[sem],
            recv_sem=self.recv.at[sem],
            device_id=(lax.axis_index("dp"), z * 2 + y),
            device_id_type=MESH,
        )

    def _from(self, k):
        return ((self.z + self.nz - k) % self.nz) * 2 + self.y

    def start(self):
        for k in range(1, self.nz):
            self._copy(self.me, (self.z + k) % self.nz, self.y, k).start()
        self._copy(self.me, self.z, 1 - self.y, 0).start()

    def forward(self):
        for k in range(1, self.nz):
            self._copy(self._from(k), self.z, self.y, k).wait_recv()
            self._copy(self._from(k), self.z, 1 - self.y, self.nz + k).start()

    def finish(self):
        for k in range(1, self.nz):
            mirrored = ((self.z + self.nz - k) % self.nz) * 2 + 1 - self.y
            self._copy(mirrored, self.z, 1 - self.y, self.nz + k).wait_recv()
        self._copy(self.z * 2 + 1 - self.y, self.z, 1 - self.y, 0).wait_recv()
        for k in range(1, self.nz):
            self._copy(self.me, (self.z + k) % self.nz, self.y, k).wait_send()
            self._copy(self._from(k), self.z, 1 - self.y, self.nz + k).wait_send()
        self._copy(self.me, self.z, 1 - self.y, 0).wait_send()


def greet(blk_peers, dp_peers):
    dp, blk = lax.axis_index("dp"), lax.axis_index("blk")
    barrier = pltpu.get_barrier_semaphore()
    for k in range(1, blk_peers):
        pl.semaphore_signal(
            barrier, inc=1, device_id=(dp, (blk + k) % blk_peers), device_id_type=MESH
        )
    for k in range(1, dp_peers):
        pl.semaphore_signal(
            barrier, inc=1, device_id=((dp + k) % dp_peers, blk), device_id_type=MESH
        )
    pl.semaphore_wait(barrier, max(blk_peers - 1, 0) + max(dp_peers - 1, 0))


def call(body, name, ins, outs, scratch=(), collective_id=None, in_specs=None, out_specs=None):
    extra = {} if collective_id is None else {"collective_id": collective_id, "has_side_effects": True}
    return pl.pallas_call(
        body,
        out_shape=[jax.ShapeDtypeStruct(s, k) for s, k in outs],
        in_specs=in_specs or [VMEM] * len(ins),
        out_specs=out_specs or [VMEM] * len(outs),
        scratch_shapes=list(scratch),
        compiler_params=pltpu.CompilerParams(vmem_limit_bytes=LIMIT, **extra),
        name=name,
    )(*ins)


def pair_cols(p):
    return pl.ds(pl.multiple_of(p * 128, 128), 128)


def pick(own, block):
    return jnp.where(own, block, jnp.zeros_like(block))


def self_forward(
    nb, x, mem, wq, wk, wv, wo, bias, gain, shift,
    q, k, v, low, lse, r1, h1_low, mem_all, send, recv,
):
    greet(nb, 0)
    me = lax.axis_index("blk")
    gather = Gather(mem_all, send, recv, nb)
    mem_all[me] = mem[...]
    gather.start()

    @pl.loop(0, 4)
    def _(i):
        rows = pl.ds(pl.multiple_of(i * 256, 256), 256)
        block = x[rows, :]
        q[rows, :] = ((dot(block, wq[...]) + bias[0:1, :]) * SCALE).astype(BF)
        k[rows, :] = dot(block, wk[...]).astype(BF)
        v[rows, :] = (dot(block, wv[...]) + bias[1:2, :]).astype(BF)

    size = 256

    def one_pair(p):
        cols = pair_cols(p)
        for i in range(TGT // size):
            rows = slice(i * size, (i + 1) * size)
            left = slice(0, i * size)
            query = q[rows, cols]
            second = lanes((size, 128)) >= HEAD
            tri = lanes((size, size)) <= lax.broadcasted_iota(jnp.int32, (size, size), 0)
            found, kept = [], lse[rows, :]
            for a in (0, 1):
                own = pick(second == bool(a), query)
                s_diag = jnp.where(tri, dot_nt(own, k[rows, cols]), NEG)
                top = jnp.max(s_diag, -1, keepdims=True)
                if i:
                    s_left = dot_nt(own, k[left, cols])
                    top = jnp.maximum(top, jnp.max(s_left, -1, keepdims=True))
                e_diag = jnp.exp(s_diag - top)
                total = jnp.sum(e_diag, -1, keepdims=True)
                share = dot(e_diag.astype(BF), v[rows, cols])
                if i:
                    e_left = jnp.exp(s_left - top)
                    total = total + jnp.sum(e_left, -1, keepdims=True)
                    share = share + dot(e_left.astype(BF), v[left, cols])
                found.append(share / total)
                kept = jnp.where(lanes((size, 128)) == 2 * p + a, top + jnp.log(total), kept)
            low[rows, cols] = jnp.where(second, found[1], found[0]).astype(BF)
            lse[rows, :] = kept

    lse[...] = jnp.zeros_like(lse)
    pl.loop(0, 5)(one_pair)
    gather.forward()
    pl.loop(5, 6)(one_pair)

    @pl.loop(0, 4)
    def _(i):
        rows = pl.ds(pl.multiple_of(i * 256, 256), 256)
        resid = x[rows, :].astype(F32) + dot(low[rows, :], wo[...]) + bias[2:3, :]
        r1[rows, :] = resid
        normed, _ = norm_parts(resid)
        h1_low[rows, :] = (normed * gain[0:1, :] + shift[0:1, :]).astype(BF)

    gather.finish()


def row_part(
    length, r1, mem, cot, wq, wk, wv, wo, wi, wf, cbias, gain, shift, bi, bf,
    low, n3_low, co, cq_grad, so, stats, sums,
    key, value, probs, attn, slope, act,
):
    rows_own = r1.shape[0]

    @pl.loop(0, mem.shape[0] // 256)
    def _(i):
        rows = pl.ds(pl.multiple_of(i * 256, 256), 256)
        key[rows, :] = dot(mem[rows, :], wk[...]).astype(BF)
        value[rows, :] = (dot(mem[rows, :], wv[...]) + cbias[2:3, :]).astype(BF)

    n1, inv1 = norm_parts(r1[...])
    h1 = n1 * gain[0:1, :] + shift[0:1, :]
    query = ((dot(h1.astype(BF), wq[...]) + cbias[0:1, :]) * SCALE).astype(BF)
    total_rows = mem.shape[0]
    live = lanes((rows_own, total_rows)) < length[0]
    second = lanes((rows_own, 128)) >= HEAD
    stat = jnp.zeros((rows_own, 128), F32)
    for p in range(6):
        cols = slice(128 * p, 128 * p + 128)
        found = []
        for a in (0, 1):
            own = pick(second == bool(a), query[:, cols])
            s = jnp.where(live, dot_nt(own, key[:, cols]), NEG)
            top = jnp.max(s, -1, keepdims=True)
            e = jnp.exp(s - top)
            total = jnp.sum(e, -1, keepdims=True)
            pr = (e * (1.0 / total)).astype(BF)
            probs[2 * p + a] = pr
            found.append(dot(pr, value[:, cols]))
            stat = jnp.where(lanes((rows_own, 128)) == 2 * p + a, top + jnp.log(total), stat)
        attn[:, cols] = jnp.where(second, found[1], found[0])
    low[...] = attn[...].astype(BF)
    r2 = h1 + dot(low[...], wo[...]) + cbias[1:2, :]
    n2, inv2 = norm_parts(r2)
    h2 = n2 * gain[1:2, :] + shift[1:2, :]
    h2_low = h2.astype(BF)

    @pl.loop(0, FF // 512)
    def _(c):
        cols = pl.ds(pl.multiple_of(c * 512, 512), 512)
        pre = dot(h2_low, wi[:, cols]) + bi[:, cols]
        up, down = gelu_parts(pre)
        act[:, cols] = up.astype(BF)
        slope[:, cols] = down

    r3 = h2 + dot(act[...], wf[...]) + bf[...]
    n3, inv3 = norm_parts(r3)
    n3_low[...] = n3.astype(BF)
    stats[...] = jnp.where(lanes((rows_own, 128)) == HEADS, inv3, stat)

    g3 = cot[...].astype(F32)
    sums[...] = jnp.zeros_like(sums)
    sums[2:3, :] = col_sum(g3 * n3)
    sums[5:6, :] = col_sum(g3)
    grad_r3 = norm_grad(g3, n3, inv3, gain[2:3, :])
    z_low = grad_r3.astype(BF)
    sums[9:10, :] = col_sum(z_low.astype(F32))

    @pl.loop(0, FF // 512)
    def _(c):
        cols = pl.ds(pl.multiple_of(c * 512, 512), 512)
        act[:, cols] = (dot_nt(z_low, wf[cols, :]) * slope[:, cols]).astype(BF)

    grad_h2 = grad_r3 + dot_nt(act[...], wi[...])
    sums[1:2, :] = col_sum(grad_h2 * n2)
    sums[4:5, :] = col_sum(grad_h2)
    grad_r2 = norm_grad(grad_h2, n2, inv2, gain[1:2, :])
    co_low = grad_r2.astype(BF)
    co[...] = co_low
    sums[8:9, :] = col_sum(co_low.astype(F32))
    oc = dot_nt(co_low, wo[...]).astype(BF)
    product = oc.astype(F32) * attn[...]
    for p in range(6):
        cols = slice(128 * p, 128 * p + 128)
        found = []
        for a in (0, 1):
            sel = second == bool(a)
            delta = jnp.sum(jnp.where(sel, product[:, cols], 0.0), -1, keepdims=True)
            dp = dot_nt(pick(sel, oc[:, cols]), value[:, cols])
            ds = (probs[2 * p + a].astype(F32) * (dp - delta)).astype(BF)
            found.append(dot(ds, key[:, cols]))
        cq_grad[:, cols] = (
            jnp.where(second, found[1], found[0]).astype(BF).astype(F32) * SCALE
        ).astype(BF)
    cq_low = cq_grad[...]
    sums[7:8, :] = col_sum(cq_low.astype(F32))
    grad_h1 = grad_r2 + dot_nt(cq_low, wq[...])
    sums[0:1, :] = col_sum(grad_h1 * n1)
    sums[3:4, :] = col_sum(grad_h1)
    so_low = norm_grad(grad_h1, n1, inv1, gain[0:1, :]).astype(BF)
    so[...] = so_low
    sums[6:7, :] = col_sum(so_low.astype(F32))


def gather_rows(nb, *refs):
    n = (len(refs) - 2) // 2
    ins, outs, (send, recv) = refs[:n], refs[n : 2 * n], refs[2 * n :]
    greet(nb, 0)
    me = lax.axis_index("blk")
    gathers = []
    for i in range(n):
        outs[i][me] = ins[i][...]
        gathers.append(Gather(outs[i], send.at[i], recv.at[i], nb))
        gathers[i].start()
    for g in gathers:
        g.forward()
    for g in gathers:
        g.finish()


def self_backward(
    so, q, k, v, low, lse, left_t, wo, wq, wk, wv,
    input_grad, slab, sums,
    go, rights, dkt, dvt, qt, gt,
):
    size = 256

    @pl.loop(0, 4)
    def _(i):
        rows = pl.ds(pl.multiple_of(i * 256, 256), 256)
        go[rows, :] = dot_nt(so[rows, :], wo[...]).astype(BF)
        rights[3, rows, :] = so[rows, :]

    @pl.loop(0, 6)
    def _(p):
        cols = pair_cols(p)
        qt[...] = q[:, cols].T
        gt[...] = go[:, cols].T
        for i in range(TGT // size):
            rows = slice(i * size, (i + 1) * size)
            query, grad_out = q[rows, cols], go[rows, cols]
            second = lanes((size, 128)) >= HEAD
            tri = lanes((size, size)) <= lax.broadcasted_iota(jnp.int32, (size, size), 0)
            product = grad_out.astype(F32) * low[rows, cols].astype(F32)
            found, kept = [], lse[rows, :]
            for a in (0, 1):
                sel = second == bool(a)
                own_q, own_g = pick(sel, query), pick(sel, grad_out)
                top = jnp.sum(
                    jnp.where(lanes((size, 128)) == 2 * p + a, kept, 0.0), -1, keepdims=True
                )
                delta = jnp.sum(jnp.where(sel, product, 0.0), -1, keepdims=True)
                total = None
                head = slice(HEAD * a, HEAD * a + HEAD)
                for first, last in ((0, i * size), (i * size, (i + 1) * size)):
                    if first == last:
                        continue
                    keys = slice(first, last)
                    pr = jnp.exp(dot_nt(own_q, k[keys, cols]) - top)
                    if first == i * size:
                        pr = jnp.where(tri, pr, 0.0)
                    ds = (pr * (dot_nt(own_g, v[keys, cols]) - delta)).astype(BF)
                    part = dot(ds, k[keys, cols])
                    total = part if total is None else total + part
                    part_k = dot(qt[head, rows], ds)
                    part_v = dot(gt[head, rows], pr.astype(BF))
                    if first == i * size:
                        dkt[head, keys] = part_k
                        dvt[head, keys] = part_v
                    else:
                        dkt[head, keys] += part_k
                        dvt[head, keys] += part_v
                found.append(total)
            rights[0, rows, cols] = (
                jnp.where(second, found[1], found[0]).astype(BF).astype(F32) * SCALE
            ).astype(BF)
        rights[1, :, cols] = dkt[...].T.astype(BF)
        rights[2, :, cols] = dvt[...].T.astype(BF)

    sums[...] = jnp.zeros_like(sums)

    @pl.loop(0, 4)
    def _(i):
        rows = pl.ds(pl.multiple_of(i * 256, 256), 256)
        sq, sk, sv = rights[0, rows, :], rights[1, rows, :], rights[2, rows, :]
        input_grad[rows, :] = (
            so[rows, :].astype(F32)
            + dot_nt(sq, wq[...])
            + dot_nt(sk, wk[...])
            + dot_nt(sv, wv[...])
        ).astype(BF)
        sums[0:1, :] += col_sum(sq.astype(F32))
        sums[1:2, :] += col_sum(sv.astype(F32))

    me = lax.axis_index("blk")
    right = rights.at[me // 2]
    cols = pl.ds(pl.multiple_of((me % 2) * 384, 128), 384)

    @pl.loop(0, 3)
    def _(i):
        rows = pl.ds(pl.multiple_of(i * 256, 256), 256)
        slab[rows, :] = dot(left_t[rows, :], right[:, cols]).astype(BF)


def column_part(
    nb, length, r1, h1_low, low, stats, co, n3, cot, mem,
    wq, wk, wv, wo, wi, wf, cbias, gain, shift, bi,
    out, slab_in, slab_out, dk, dv, mem_grad, sums, bias_in,
    h2_low, z_low, query, oc, prod, lse_t, delta_t, act, pre_low, wi_own, wf_own, key, value, sem,
):
    me = lax.axis_index("blk")
    copies = []
    for t in range(3):
        off = pl.multiple_of(768 * ((me + t) % 4) + 128 * (2 * t + me // 4), 128)
        copies.append(
            pltpu.make_async_copy(
                wi.at[:, pl.ds(off, 128)], wi_own.at[:, pl.ds(128 * t, 128)], sem.at[2 * t]
            )
        )
        copies.append(
            pltpu.make_async_copy(
                wf.at[pl.ds(off, 128), :], wf_own.at[pl.ds(128 * t, 128), :], sem.at[2 * t + 1]
            )
        )
    for c in copies:
        c.start()

    @pl.loop(0, 4)
    def _(i):
        rows = pl.ds(pl.multiple_of(i * 256, 256), 256)
        n1, _ = norm_parts(r1[rows, :])
        h1 = n1 * gain[0:1, :] + shift[0:1, :]
        r2 = h1 + dot(low[rows, :], wo[...]) + cbias[1:2, :]
        n2, _ = norm_parts(r2)
        h2_low[rows, :] = (n2 * gain[1:2, :] + shift[1:2, :]).astype(BF)
        normed = n3[rows, :].astype(F32)
        out[rows, :] = (normed * gain[2:3, :] + shift[2:3, :]).astype(BF)
        inv3 = jnp.sum(
            jnp.where(lanes((256, 128)) == HEADS, stats[rows, :], 0.0), -1, keepdims=True
        )
        z_low[rows, :] = norm_grad(
            cot[rows, :].astype(F32), normed, inv3, gain[2:3, :]
        ).astype(BF)
        query[rows, :] = ((dot(h1_low[rows, :], wq[...]) + cbias[0:1, :]) * SCALE).astype(BF)
        grad_out = dot_nt(co[rows, :], wo[...]).astype(BF)
        oc[rows, :] = grad_out
        prod[rows, :] = grad_out.astype(F32) * low[rows, :].astype(F32)

    lse_t[...] = stats[...].T
    member = (
        lax.broadcasted_iota(jnp.int32, (16, D), 1) // HEAD
        == lax.broadcasted_iota(jnp.int32, (16, D), 0)
    )
    member = jnp.where(member, 1.0, 0.0).astype(BF)
    big = prod[...].astype(BF)
    small = (prod[...] - big.astype(F32)).astype(BF)
    delta_t[...] = dot_nt(member, big) + dot_nt(member, small)

    for c in copies:
        c.wait()
    off = [pl.multiple_of(768 * ((me + t) % 4) + 128 * (2 * t + me // 4), 128) for t in range(3)]
    bias = jnp.concatenate([bi[:, pl.ds(o, 128)] for o in off], axis=1)
    total = jnp.zeros((1, 384), F32)
    for i in range(4):
        rows = slice(i * 256, (i + 1) * 256)
        up, slope = gelu_parts(dot(h2_low[rows, :], wi_own[...]) + bias)
        act[rows, :] = up.astype(BF)
        low_grad = (dot_nt(z_low[rows, :], wf_own[...]) * slope).astype(BF)
        pre_low[rows, :] = low_grad
        total = total + col_sum(low_grad.astype(F32))
    bias_in[...] = jnp.zeros_like(bias_in)
    for t in range(3):
        bias_in[:, pl.ds(off[t], 128)] = total[:, 128 * t : 128 * t + 128]

    @pl.loop(0, 3)
    def _(i):
        rows = pl.ds(pl.multiple_of(i * 256, 256), 256)
        slab_in[rows, :] = dot_tn(h2_low[:, rows], pre_low[...]).astype(BF)

    for t in range(3):
        slab_out[t] = dot_tn(act[:, 128 * t : 128 * t + 128], z_low[...]).astype(BF)
    slab_out[3] = jnp.zeros_like(slab_out[3])

    own_rows = mem.shape[0]
    key[...] = dot(mem[...], wk[...]).astype(BF)
    value[...] = (dot(mem[...], wv[...]) + cbias[2:3, :]).astype(BF)
    position = me * own_rows + lax.broadcasted_iota(jnp.int32, (own_rows, 1), 0)
    live = position < length[0]
    second = lanes((own_rows, 128)) >= HEAD

    @pl.loop(0, 6)
    def _(p):
        cols = pair_cols(p)
        found_k, found_v = [], []
        for a in (0, 1):
            sel = second == bool(a)
            s = dot_nt(pick(sel, key[:, cols]), query[:, cols])
            pr = jnp.where(live, jnp.exp(s - lse_t[pl.ds(2 * p + a, 1), :]), 0.0)
            dp = dot_nt(pick(sel, value[:, cols]), oc[:, cols])
            ds = (pr * (dp - delta_t[pl.ds(2 * p + a, 1), :])).astype(BF)
            found_k.append(dot(ds, query[:, cols]))
            found_v.append(dot(pr.astype(BF), oc[:, cols]))
        dk[:, cols] = jnp.where(second, found_k[1], found_k[0]).astype(BF)
        dv[:, cols] = jnp.where(second, found_v[1], found_v[0]).astype(BF)

    mem_grad[...] = (dot_nt(dk[...], wk[...]) + dot_nt(dv[...], wv[...])).astype(BF)
    sums[...] = col_sum(dv[...].astype(F32))


def reduce_part(
    nb, ndp, slab_self, slab_in, slab_out, rights, left_t,
    f_self, f_cross, f_in, f_out,
    right, slab_cross, got, got_out, ag, ag_out, x_send, x_recv, d_send, d_recv, g_send, g_recv,
):
    greet(nb, ndp)
    dp, me = lax.axis_index("dp"), lax.axis_index("blk")
    quarter = D // ndp

    def trade(k, target, origin):
        return pltpu.make_async_remote_copy(
            src_ref=rights.at[target // 2, :, pl.ds(pl.multiple_of((target % 2) * 384, 128), 384)],
            dst_ref=right.at[origin],
            send_sem=x_send.at[k],
            recv_sem=x_recv.at[k],
            device_id=(dp, target),
            device_id_type=MESH,
        )

    for k in range(1, nb):
        trade(k, (me + k) % nb, me).start()
    right[me] = rights[me // 2, :, pl.ds(pl.multiple_of((me % 2) * 384, 128), 384)]

    def share(g, slab, k):
        peer = (dp + k) % ndp
        return pltpu.make_async_remote_copy(
            src_ref=slab.at[pl.ds(pl.multiple_of(peer * quarter, 16), quarter), :],
            dst_ref=got.at[g, k],
            send_sem=d_send.at[g, k],
            recv_sem=d_recv.at[g, k],
            device_id=(peer, me),
            device_id_type=MESH,
        )

    def share_out(k):
        peer = (dp + k) % ndp
        return pltpu.make_async_remote_copy(
            src_ref=slab_out.at[(peer - me + nb) % 4],
            dst_ref=got_out.at[k],
            send_sem=d_send.at[3, k],
            recv_sem=d_recv.at[3, k],
            device_id=(peer, me),
            device_id_type=MESH,
        )

    slabs = (slab_self, slab_cross, slab_in)
    for g in (0, 2):
        for k in range(1, ndp):
            share(g, slabs[g], k).start()
    for k in range(1, ndp):
        share_out(k).start()

    own = pl.ds(pl.multiple_of(dp * quarter, 16), quarter)
    gathers = [Gather(ag.at[g], g_send.at[g], g_recv.at[g], nb) for g in range(3)]
    gathers.append(Gather(ag_out, g_send.at[3], g_recv.at[3], nb))

    def settle(g):
        for k in range(1, ndp):
            share(g, slabs[g], k).wait()
        total = slabs[g][own, :].astype(F32)
        for k in range(1, ndp):
            total = total + got[g, k].astype(F32)
        ag[g, me] = total.astype(BF)
        gathers[g].start()

    settle(0)
    settle(2)
    for k in range(1, ndp):
        share_out(k).wait()
    total = slab_out[(dp - me + nb) % 4].astype(F32)
    for k in range(1, ndp):
        total = total + got_out[k].astype(F32)
    ag_out[me] = total.astype(BF)
    gathers[3].start()

    for k in range(1, nb):
        trade(k, (me + k) % nb, (me + nb - k) % nb).wait_recv()

    @pl.loop(0, 3)
    def _(i):
        rows = pl.ds(pl.multiple_of(i * 256, 256), 256)
        slab_cross[rows, :] = dot(left_t[rows, :], right[...].reshape(TGT, 384)).astype(BF)

    for k in range(1, ndp):
        share(1, slab_cross, k).start()
    settle(1)
    order = (0, 2, 3, 1)
    for g in order:
        gathers[g].forward()
    for g in order:
        gathers[g].finish()
        if g == 3:
            for b in range(nb):
                t = (dp - b + nb) % 4

                @pl.when(t < 3)
                def _():
                    f_out[pl.ds(pl.multiple_of(128 * (2 * t + b // 4), 128), 128), :] = ag_out[b].astype(F32)
        elif g == 2:
            for b in range(nb):
                for t in range(3):
                    col = 768 * ((b + t) % 4) + 128 * (2 * t + b // 4)
                    f_in[:, col : col + 128] = ag[2, b, :, 128 * t : 128 * t + 128].astype(F32)
        else:
            dst = f_self if g == 0 else f_cross
            for b in range(nb):
                dst[b // 2, :, 384 * (b % 2) : 384 * (b % 2) + 384] = ag[g, b].astype(F32)
    for k in range(1, nb):
        trade(k, (me + k) % nb, me).wait_send()


def shared_work(
    nb, ndp,
    inputs, memory, lengths, cotangent, self_query, self_key, self_value, self_out, self_bias,
    cross_query, cross_key, cross_value, cross_out, cross_bias, cross_value_bias,
    norm_gain, norm_bias, ffn_in, ffn_in_bias, ffn_out, ffn_out_bias,
):
    own_rows = TGT // nb
    me = lax.axis_index("blk")
    x, mem, cot = inputs[0], memory[0], cotangent[0]
    mrows = mem.shape[0]
    gain, shift = norm_gain.astype(F32).T, norm_bias.astype(F32).T
    sbias = self_bias.astype(F32).T
    cbias = jnp.concatenate([cross_bias.astype(F32).T, cross_value_bias.astype(F32)[None]], 0)
    bi, bf = ffn_in_bias.astype(F32)[None], ffn_out_bias.astype(F32)[None]
    wide = (TGT, D)
    own = (own_rows, D)
    dma = pltpu.SemaphoreType.DMA

    q, k, v, low, lse, r1, h1_low, mem_all = call(
        functools.partial(self_forward, nb),
        "self_forward",
        (x, mem, self_query, self_key, self_value, self_out, sbias, gain, shift),
        [(wide, BF)] * 4 + [((TGT, 128), F32), (wide, F32), (wide, BF), ((nb, mrows, D), BF)],
        [dma((nb,)), dma((nb,))],
        collective_id=0,
    )
    mem_flat = mem_all.reshape(nb * mrows, D)
    cut = lambda a: lax.dynamic_slice_in_dim(a, me * own_rows, own_rows, 0)
    c_low, n3_low, co, cq, so, stats, sums = call(
        row_part,
        "row_part",
        (lengths, cut(r1), mem_flat, cut(cot), cross_query, cross_key, cross_value, cross_out,
         ffn_in, ffn_out, cbias, gain, shift, bi, bf),
        [(own, BF)] * 5 + [((own_rows, 128), F32), ((16, D), F32)],
        [
            pltpu.VMEM((nb * mrows, D), BF),
            pltpu.VMEM((nb * mrows, D), BF),
            pltpu.VMEM((HEADS, own_rows, nb * mrows), BF),
            pltpu.VMEM(own, F32),
            pltpu.VMEM((own_rows, FF), F32),
            pltpu.VMEM((own_rows, FF), BF),
        ],
        in_specs=[SMEM] + [VMEM] * 14,
    )
    gathered = call(
        functools.partial(gather_rows, nb),
        "gather_rows",
        (so, c_low, stats, co, n3_low),
        [((nb,) + own, BF)] * 2 + [((nb, own_rows, 128), F32)] + [((nb,) + own, BF)] * 2,
        [dma((5, nb)), dma((5, nb))],
        collective_id=1,
    )
    so_all, c_low_all, stats_all, co_all, n3_all = [a.reshape(TGT, -1) for a in gathered]
    left_self = jnp.where(me < 6, x, low).T
    input_grad, slab_self, sums_self = call(
        self_backward,
        "self_backward",
        (so_all, q, k, v, low, lse, left_self, self_out, self_query, self_key, self_value),
        [(wide, BF), ((D, 384), BF), ((8, D), F32)],
        [
            pltpu.VMEM(wide, BF),
            pltpu.VMEM((4,) + wide, BF),
            pltpu.VMEM((128, TGT), F32),
            pltpu.VMEM((128, TGT), F32),
            pltpu.VMEM((128, TGT), BF),
            pltpu.VMEM((128, TGT), BF),
        ],
    )
    out, slab_in, slab_out, dk, dv, mem_grad, sums_v, bias_in = call(
        functools.partial(column_part, nb),
        "column_part",
        (lengths, r1, h1_low, c_low_all, stats_all, co_all, n3_all, cot, mem,
         cross_query, cross_key, cross_value, cross_out, ffn_in, ffn_out, cbias, gain, shift, bi),
        [(wide, BF), ((D, 384), BF), ((4, 128, D), BF), ((mrows, D), BF), ((mrows, D), BF),
         ((mrows, D), BF), ((1, D), F32), ((1, FF), F32)],
        [
            pltpu.VMEM(wide, BF), pltpu.VMEM(wide, BF), pltpu.VMEM(wide, BF), pltpu.VMEM(wide, BF),
            pltpu.VMEM(wide, F32), pltpu.VMEM((128, TGT), F32), pltpu.VMEM((16, TGT), F32),
            pltpu.VMEM((TGT, 384), BF), pltpu.VMEM((TGT, 384), BF),
            pltpu.VMEM((D, 384), BF), pltpu.VMEM((384, D), BF),
            pltpu.VMEM((mrows, D), BF), pltpu.VMEM((mrows, D), BF), dma((6,)),
        ],
        in_specs=[SMEM] + [VMEM] * 12 + [ANY, ANY] + [VMEM] * 4,
    )
    left_cross = jnp.where(
        me < 4, mem_flat, jnp.where(me < 6, h1_low, c_low_all)
    ).T
    quarter = D // ndp
    f_self, f_cross, f_in, f_out = call(
        functools.partial(reduce_part, nb, ndp),
        "reduce_part",
        (slab_self, slab_in, slab_out, jnp.stack([dk, dv, cq, co]), left_cross),
        [((4, quarter, D), F32), ((4, quarter, D), F32), ((quarter, FF), F32), ((FF // ndp, D), F32)],
        [
            pltpu.VMEM((nb, own_rows, 384), BF),
            pltpu.VMEM((D, 384), BF),
            pltpu.VMEM((3, ndp, quarter, 384), BF),
            pltpu.VMEM((ndp, 128, D), BF),
            pltpu.VMEM((3, nb, quarter, 384), BF),
            pltpu.VMEM((nb, 128, D), BF),
            dma((nb,)), dma((nb,)), dma((4, ndp)), dma((4, ndp)), dma((4, nb)), dma((4, nb)),
        ],
        collective_id=2,
    )
    part = jnp.concatenate(
        [sums[:10], sums_self[:2] * (1.0 / nb), sums_v, bias_in.reshape(4, D)], axis=0
    )
    part = lax.psum(part, ("dp", "blk"))
    dp = lax.axis_index("dp")
    mine = lax.dynamic_slice_in_dim(part, dp * quarter, quarter, 1)
    in_bias = lax.dynamic_slice_in_dim(part[13:], dp, 1, 0)[0]
    return (
        out[None],
        input_grad[None],
        mem_grad[None],
        f_self[0], f_self[1], f_self[2], f_self[3],
        jnp.stack([mine[10], mine[11], mine[6]], 1),
        f_cross[2], f_cross[0], f_cross[1], f_cross[3],
        jnp.stack([mine[7], mine[8]], 1),
        mine[12],
        mine[0:3].T,
        mine[3:6].T,
        f_in,
        in_bias,
        f_out,
        mine[9],
    )


def merged(array, axis, join):
    gathered = jax.tree.map(
        lambda a, kind: lax.all_gather(a.astype(kind), axis), array, (jnp.bfloat16, jnp.bfloat16)
    )

    def take(source):
        return jax.tree.map(
            lambda a, own: lax.dynamic_index_in_dim(a, source, 0, False).astype(own.dtype),
            gathered,
            array,
        )

    return lax.fori_loop(
        1, lax.axis_size(axis), lambda source, state: join(state, take(source)), take(0)
    )


def layer_norm(residual, gain_col, shift_col):
    average = jnp.mean(residual, axis=-1, keepdims=True)
    centered = residual - average
    variance = jnp.mean(centered * centered, axis=-1, keepdims=True)
    return centered * lax.rsqrt(variance + EPS) * gain_col + shift_col


def exact_gelu(values):
    return jax.nn.gelu(values, approximate=False)


def project(left_side, weight):
    return jnp.dot(left_side, weight, preferred_element_type=jnp.float32)


def project_back(gradient, weight):
    return lax.dot_general(
        gradient, weight, (((1,), (1,)), ((), ())), preferred_element_type=jnp.float32
    )


def weight_grad(left_side, gradient):
    return lax.dot_general(
        left_side, gradient, (((0,), (0,)), ((), ())), preferred_element_type=jnp.float32
    )


def column_sum(gradient):
    return jnp.sum(gradient.astype(jnp.float32), axis=0)


def split_heads(values):
    return values.reshape(values.shape[:-1] + (HEADS, HEAD))


def combine_totals(earlier, latter):
    top_a, sum_a = earlier
    top_b, sum_b = latter
    top_score = jnp.maximum(top_a, top_b)
    return (top_score, sum_a * jnp.exp(top_a - top_score) + sum_b * jnp.exp(top_b - top_score))


def self_scores(query_rows, key_rows, row_start, block_rows):
    scores = jnp.einsum("qhe,khe->hqk", query_rows, key_rows, preferred_element_type=jnp.float32)
    row_pos = row_start + jnp.arange(block_rows)[:, None]
    col_pos = jnp.arange(key_rows.shape[0])[None, :]
    return jnp.where((col_pos <= row_pos)[None], scores, NEG)


def copied_work(
    inputs,
    memory,
    lengths,
    cotangent,
    self_query,
    self_key,
    self_value,
    self_out,
    self_bias,
    cross_query,
    cross_key,
    cross_value,
    cross_out,
    cross_bias,
    cross_value_bias,
    norm_gain,
    norm_bias,
    ffn_in,
    ffn_in_bias,
    ffn_out,
    ffn_out_bias,
):
    all_rows = ITEMS * TGT
    block_rows = min(512, TGT)
    mem_rows = memory.shape[1]
    self_bias_f = self_bias.astype(jnp.float32)
    cross_bias_f = cross_bias.astype(jnp.float32)
    gains = norm_gain.astype(jnp.float32)
    shifts = norm_bias.astype(jnp.float32)
    flat_in = inputs.reshape(all_rows, D)
    query_self = split_heads(
        ((project(flat_in, self_query) + self_bias_f[:, 0]) * SCALE)
        .astype(jnp.bfloat16)
        .reshape(ITEMS, TGT, D)
    )
    key_self = split_heads(project(flat_in, self_key).astype(jnp.bfloat16).reshape(ITEMS, TGT, D))
    value_self = split_heads(
        (project(flat_in, self_value) + self_bias_f[:, 1])
        .astype(jnp.bfloat16)
        .reshape(ITEMS, TGT, D)
    )
    item_index = 0
    attn_blocks = []
    lse_blocks = []
    for row_start in range(0, TGT, block_rows):
        row_end = row_start + block_rows
        scores = self_scores(
            query_self[item_index, row_start:row_end],
            key_self[item_index, :row_end],
            row_start,
            block_rows,
        )
        top_score = jnp.max(scores, axis=-1, keepdims=True)
        log_total = top_score + jnp.log(
            jnp.sum(jnp.exp(scores - top_score), axis=-1, keepdims=True)
        )
        probs_low = jnp.exp(scores - log_total).astype(jnp.bfloat16)
        attn_blocks.append(
            jnp.einsum(
                "hqk,khe->qhe",
                probs_low,
                value_self[item_index, :row_end],
                preferred_element_type=jnp.float32,
            )
        )
        lse_blocks.append(log_total)
    attn_items = [jnp.concatenate(attn_blocks, axis=0)]
    lse_self = [lse_blocks]
    self_attn = jnp.stack(attn_items, axis=0)
    self_low = self_attn.astype(jnp.bfloat16).reshape(all_rows, D)
    resid_one = flat_in.astype(jnp.float32) + project(self_low, self_out) + self_bias_f[:, 2]
    hidden_one, norm1_back = jax.vjp(layer_norm, resid_one, gains[:, 0], shifts[:, 0])
    hidden_low = hidden_one.astype(jnp.bfloat16)
    query_cross = split_heads(
        ((project(hidden_low, cross_query) + cross_bias_f[:, 0]) * SCALE)
        .astype(jnp.bfloat16)
        .reshape(ITEMS, TGT, D)
    )
    flat_mem = memory.reshape(ITEMS * mem_rows, D)
    key_cross = split_heads(
        project(flat_mem, cross_key).astype(jnp.bfloat16).reshape(ITEMS, mem_rows, D)
    )
    value_cross = split_heads(
        (project(flat_mem, cross_value) + cross_value_bias.astype(jnp.float32))
        .astype(jnp.bfloat16)
        .reshape(ITEMS, mem_rows, D)
    )
    position = lax.axis_index("blk") * mem_rows + jnp.arange(mem_rows)
    live_mask = position[None, :] < lengths[:, None]

    def cross_scores():
        raw_scores = jnp.einsum(
            "bqhe,bkhe->bhqk", query_cross, key_cross, preferred_element_type=jnp.float32
        )
        return jnp.where(live_mask[:, None, None, :], raw_scores, NEG)

    scores = cross_scores()
    top_local = jnp.max(scores, axis=-1)
    sum_local = jnp.sum(jnp.exp(scores - top_local[..., None]), axis=-1)
    top_all, sum_all = merged((top_local, sum_local), "blk", combine_totals)
    cross_lse = top_all + jnp.log(sum_all)
    probs_low = jnp.exp(scores - cross_lse[..., None]).astype(jnp.bfloat16)
    share_out = jnp.einsum(
        "bhqk,bkhe->bqhe", probs_low, value_cross, preferred_element_type=jnp.float32
    ).reshape(all_rows, D)
    cot_flat = cotangent.reshape(all_rows, D)
    attn_rows = lax.psum(share_out, "blk")
    cross_low = attn_rows.astype(jnp.bfloat16)
    resid_two = hidden_one + project(cross_low, cross_out) + cross_bias_f[:, 1]
    hidden_two, norm2_back = jax.vjp(layer_norm, resid_two, gains[:, 1], shifts[:, 1])
    second_low = hidden_two.astype(jnp.bfloat16)
    pre_act = project(second_low, ffn_in) + ffn_in_bias.astype(jnp.float32)
    activated, gelu_back = jax.vjp(exact_gelu, pre_act)
    act_low = activated.astype(jnp.bfloat16)
    resid_three = hidden_two + project(act_low, ffn_out) + ffn_out_bias.astype(jnp.float32)
    result, norm3_back = jax.vjp(layer_norm, resid_three, gains[:, 2], shifts[:, 2])
    result_low = result.astype(jnp.bfloat16)
    grad_r3, grad_gain3, grad_shift3 = norm3_back(cot_flat.astype(jnp.float32))
    z_low = grad_r3.astype(jnp.bfloat16)
    g_ffn_out = weight_grad(act_low, z_low)
    g_ffn_out_bias = column_sum(z_low)
    (grad_pre,) = gelu_back(project_back(z_low, ffn_out))
    pre_low = grad_pre.astype(jnp.bfloat16)
    g_ffn_in = weight_grad(second_low, pre_low)
    g_ffn_in_bias = column_sum(pre_low)
    grad_h2 = grad_r3 + project_back(pre_low, ffn_in)
    grad_r2, grad_gain2, grad_shift2 = norm2_back(grad_h2)
    co_low = grad_r2.astype(jnp.bfloat16)
    g_cross_out = weight_grad(cross_low, co_low)
    g_co_bias = column_sum(co_low)
    oc_low = project_back(co_low, cross_out).astype(jnp.bfloat16)
    out_rows = result_low.reshape(ITEMS, TGT, D)
    grad_oc = split_heads(oc_low.reshape(ITEMS, TGT, D))
    cross_delta = jnp.transpose(
        jnp.sum(
            grad_oc.astype(jnp.float32) * split_heads(attn_rows.reshape(ITEMS, TGT, D)), axis=-1
        ),
        (0, 2, 1),
    )
    scores = cross_scores()
    prob_full = jnp.exp(scores - cross_lse[..., None])
    grad_probs = jnp.einsum(
        "bqhe,bkhe->bhqk", grad_oc, value_cross, preferred_element_type=jnp.float32
    )
    grad_scores = (prob_full * (grad_probs - cross_delta[..., None])).astype(jnp.bfloat16)
    query_share = jnp.einsum(
        "bhqk,bkhe->bqhe", grad_scores, key_cross, preferred_element_type=jnp.float32
    ).reshape(all_rows, D)
    key_low = (
        jnp.einsum("bhqk,bqhe->bkhe", grad_scores, query_cross, preferred_element_type=jnp.float32)
        .astype(jnp.bfloat16)
        .reshape(ITEMS * mem_rows, D)
    )
    value_low = (
        jnp.einsum(
            "bhqk,bqhe->bkhe",
            prob_full.astype(jnp.bfloat16),
            grad_oc,
            preferred_element_type=jnp.float32,
        )
        .astype(jnp.bfloat16)
        .reshape(ITEMS * mem_rows, D)
    )
    grad_cq = lax.psum(query_share, "blk")
    cq_low = (grad_cq * SCALE).astype(jnp.bfloat16)
    g_cross_query = weight_grad(hidden_one.astype(jnp.bfloat16), cq_low)
    g_cq_bias = column_sum(cq_low)
    grad_h1_rows = grad_r2 + project_back(cq_low, cross_query)
    g_cross_key_dev = weight_grad(flat_mem, key_low)
    g_cross_value_dev = weight_grad(flat_mem, value_low)
    g_cv_bias_dev = column_sum(value_low)
    memory_grad = (
        (project_back(key_low, cross_key) + project_back(value_low, cross_value))
        .astype(jnp.bfloat16)
        .reshape(ITEMS, mem_rows, D)
    )
    g_cross_key, g_cross_value, g_cv_bias = lax.psum(
        (g_cross_key_dev, g_cross_value_dev, g_cv_bias_dev), "blk"
    )
    grad_r1, grad_gain1, grad_shift1 = norm1_back(grad_h1_rows)
    so_low = grad_r1.astype(jnp.bfloat16)
    g_self_out = weight_grad(self_low, so_low)
    g_so_bias = column_sum(so_low)
    grad_os = split_heads(
        project_back(so_low, self_out).astype(jnp.bfloat16).reshape(ITEMS, TGT, D)
    )
    item_index = 0
    key_grad = jnp.zeros((TGT, HEADS, HEAD), jnp.float32)
    value_grad = jnp.zeros((TGT, HEADS, HEAD), jnp.float32)
    query_blocks = []
    for row_start in range(0, TGT, block_rows):
        row_end = row_start + block_rows
        query_rows = query_self[item_index, row_start:row_end]
        key_rows = key_self[item_index, :row_end]
        scores = self_scores(query_rows, key_rows, row_start, block_rows)
        prob_full = jnp.exp(scores - lse_self[item_index][row_start // block_rows])
        grad_out = grad_os[item_index, row_start:row_end]
        row_delta = jnp.transpose(
            jnp.sum(
                grad_out.astype(jnp.float32) * self_attn[item_index, row_start:row_end], axis=-1
            )
        )
        grad_probs = jnp.einsum(
            "qhe,khe->hqk",
            grad_out,
            value_self[item_index, :row_end],
            preferred_element_type=jnp.float32,
        )
        grad_scores = (prob_full * (grad_probs - row_delta[:, :, None])).astype(jnp.bfloat16)
        query_blocks.append(
            jnp.einsum("hqk,khe->qhe", grad_scores, key_rows, preferred_element_type=jnp.float32)
        )
        key_grad = key_grad.at[:row_end].add(
            jnp.einsum("hqk,qhe->khe", grad_scores, query_rows, preferred_element_type=jnp.float32)
        )
        value_grad = value_grad.at[:row_end].add(
            jnp.einsum(
                "hqk,qhe->khe",
                prob_full.astype(jnp.bfloat16),
                grad_out,
                preferred_element_type=jnp.float32,
            )
        )
    query_items = [jnp.concatenate(query_blocks, axis=0)]
    key_items = [key_grad]
    value_items = [value_grad]
    sq_low = (jnp.stack(query_items, 0).astype(jnp.bfloat16) * jnp.bfloat16(SCALE)).reshape(
        all_rows, D
    )
    sk_low = jnp.stack(key_items, 0).astype(jnp.bfloat16).reshape(all_rows, D)
    sv_low = jnp.stack(value_items, 0).astype(jnp.bfloat16).reshape(all_rows, D)
    g_self_query = weight_grad(flat_in, sq_low)
    g_self_key = weight_grad(flat_in, sk_low)
    g_self_value = weight_grad(flat_in, sv_low)
    g_sq_bias = column_sum(sq_low)
    g_sv_bias = column_sum(sv_low)
    input_grad = (
        (
            grad_r1
            + project_back(sq_low, self_query)
            + project_back(sk_low, self_key)
            + project_back(sv_low, self_value)
        )
        .astype(jnp.bfloat16)
        .reshape(ITEMS, TGT, D)
    )
    g_self_bias = jnp.stack([g_sq_bias, g_sv_bias, g_so_bias], axis=1)
    g_cross_bias = jnp.stack([g_cq_bias, g_co_bias], axis=1)
    g_norm_gain = jnp.stack([grad_gain1, grad_gain2, grad_gain3], axis=1)
    g_norm_bias = jnp.stack([grad_shift1, grad_shift2, grad_shift3], axis=1)
    summed = (
        lax.psum_scatter(
            g_self_query.astype(jnp.bfloat16), "dp", scatter_dimension=0, tiled=True
        ).astype(jnp.float32),
        lax.psum_scatter(
            g_self_key.astype(jnp.bfloat16), "dp", scatter_dimension=0, tiled=True
        ).astype(jnp.float32),
        lax.psum_scatter(
            g_self_value.astype(jnp.bfloat16), "dp", scatter_dimension=0, tiled=True
        ).astype(jnp.float32),
        lax.psum_scatter(
            g_self_out.astype(jnp.bfloat16), "dp", scatter_dimension=0, tiled=True
        ).astype(jnp.float32),
        lax.psum_scatter(
            g_cross_query.astype(jnp.bfloat16), "dp", scatter_dimension=0, tiled=True
        ).astype(jnp.float32),
        lax.psum_scatter(
            g_cross_key.astype(jnp.bfloat16), "dp", scatter_dimension=0, tiled=True
        ).astype(jnp.float32),
        lax.psum_scatter(
            g_cross_value.astype(jnp.bfloat16), "dp", scatter_dimension=0, tiled=True
        ).astype(jnp.float32),
        lax.psum_scatter(
            g_cross_out.astype(jnp.bfloat16), "dp", scatter_dimension=0, tiled=True
        ).astype(jnp.float32),
        lax.psum_scatter(
            g_ffn_in.astype(jnp.bfloat16), "dp", scatter_dimension=0, tiled=True
        ).astype(jnp.float32),
        lax.psum_scatter(
            g_ffn_out.astype(jnp.bfloat16), "dp", scatter_dimension=0, tiled=True
        ).astype(jnp.float32),
        lax.psum_scatter(
            g_self_bias.astype(jnp.bfloat16), "dp", scatter_dimension=0, tiled=True
        ).astype(jnp.float32),
        lax.psum_scatter(
            g_cross_bias.astype(jnp.bfloat16), "dp", scatter_dimension=0, tiled=True
        ).astype(jnp.float32),
        lax.psum_scatter(
            g_cv_bias.astype(jnp.bfloat16), "dp", scatter_dimension=0, tiled=True
        ).astype(jnp.float32),
        lax.psum_scatter(
            g_norm_gain.astype(jnp.bfloat16), "dp", scatter_dimension=0, tiled=True
        ).astype(jnp.float32),
        lax.psum_scatter(
            g_norm_bias.astype(jnp.bfloat16), "dp", scatter_dimension=0, tiled=True
        ).astype(jnp.float32),
        lax.psum_scatter(
            g_ffn_in_bias.astype(jnp.bfloat16), "dp", scatter_dimension=0, tiled=True
        ).astype(jnp.float32),
        lax.psum_scatter(
            g_ffn_out_bias.astype(jnp.bfloat16), "dp", scatter_dimension=0, tiled=True
        ).astype(jnp.float32),
    )
    (
        s_query,
        s_key,
        s_value,
        s_out,
        c_query,
        c_key,
        c_value,
        c_out,
        f_in,
        f_out,
        r_self_bias,
        r_cross_bias,
        r_cv_bias,
        r_gain,
        r_shift,
        r_in_bias,
        r_out_bias,
    ) = summed
    return (
        out_rows,
        input_grad,
        memory_grad,
        s_query,
        s_key,
        s_value,
        s_out,
        r_self_bias,
        c_query,
        c_key,
        c_value,
        c_out,
        r_cross_bias,
        r_cv_bias,
        r_gain,
        r_shift,
        f_in,
        r_in_bias,
        f_out,
        r_out_bias,
    )


def solution(mesh):
    nb, ndp = mesh.shape["blk"], mesh.shape["dp"]
    body = copied_work
    if (nb, ndp) == (8, 4):
        body = functools.partial(shared_work, nb, ndp)
    return jax.shard_map(
        body,
        mesh=mesh,
        in_specs=(
            P("dp", None, None),
            P("dp", "blk", None),
            P("dp"),
            P("dp", None, None),
            P(),
            P(),
            P(),
            P(),
            P(),
            P(),
            P(),
            P(),
            P(),
            P(),
            P(),
            P(),
            P(),
            P(),
            P(),
            P(),
            P(),
        ),
        out_specs=(
            P("dp", None, None),
            P("dp", None, None),
            P("dp", "blk", None),
            P("dp", None),
            P("dp", None),
            P("dp", None),
            P("dp", None),
            P("dp", None),
            P("dp", None),
            P("dp", None),
            P("dp", None),
            P("dp", None),
            P("dp", None),
            P("dp"),
            P("dp", None),
            P("dp", None),
            P("dp", None),
            P("dp"),
            P("dp", None),
            P("dp"),
        ),
        check_vma=False,
    )
```

```python
import functools

import jax
import jax.numpy as jnp
from jax import lax
from jax.experimental import pallas as pl
from jax.experimental.pallas import tpu as pltpu
from jax.sharding import PartitionSpec as P

D = 768
HEADS = 12
HEAD = 64
FF = 3072
TGT = 1024
ITEMS = 1


NEG = -1e30
EPS = 1e-05
SCALE = 0.125
BF = jnp.bfloat16
F32 = jnp.float32
MESH = pl.DeviceIdType.MESH
VMEM = pl.BlockSpec(memory_space=pltpu.VMEM)
SMEM = pl.BlockSpec(memory_space=pltpu.SMEM)
ANY = pl.BlockSpec(memory_space=pl.ANY)
LIMIT = 62 * 2**20


def dot(a, b):
    return jnp.dot(a, b, preferred_element_type=F32)


def dot_nt(a, b):
    return lax.dot_general(a, b, (((1,), (1,)), ((), ())), preferred_element_type=F32)


def dot_tn(a, b):
    return lax.dot_general(a, b, (((0,), (0,)), ((), ())), preferred_element_type=F32)


def lanes(shape):
    return lax.broadcasted_iota(jnp.int32, shape, 1)


def norm_parts(residual):
    centered = residual - jnp.mean(residual, axis=-1, keepdims=True)
    inv = lax.rsqrt(jnp.mean(centered * centered, axis=-1, keepdims=True) + EPS)
    return centered * inv, inv


def norm_grad(gradient, normed, inv, gain):
    scaled = gradient * gain
    return (
        scaled
        - jnp.mean(scaled, axis=-1, keepdims=True)
        - normed * jnp.mean(scaled * normed, axis=-1, keepdims=True)
    ) * inv


def gelu_parts(values):
    cdf = 0.5 * (1.0 + lax.erf(values * 0.7071067811865476))
    slope = cdf + values * (jnp.exp(-0.5 * values * values) * 0.3989422804014327)
    return values * cdf, slope


def col_sum(values):
    return jnp.sum(values, axis=0, keepdims=True)


class Gather:
    def __init__(self, buf, send, recv, live=None):
        self.buf, self.send, self.recv = buf, send, recv
        self.me = lax.axis_index("blk")
        self.y, self.z = self.me % 2, self.me // 2
        self.others = (1 + self.z % 2, (2 + 3 * self.z) % 5, 3 * (1 - self.z // 2))
        self.live = live
        self.inner = self.z % 3 != 0

    def _do(self, slot, act, also=None):
        wanted = [c for c in (also, self.live and self.live(slot)) if c is not None]
        if not wanted:
            act()
        else:
            pl.when(wanted[0] if len(wanted) == 1 else jnp.logical_and(*wanted))(act)

    def _copy(self, slot, z, y, sem):
        return pltpu.make_async_remote_copy(
            src_ref=self.buf.at[slot],
            dst_ref=self.buf.at[slot],
            send_sem=self.send.at[sem],
            recv_sem=self.recv.at[slot],
            device_id=(lax.axis_index("dp"), z * 2 + y),
            device_id_type=MESH,
        )

    def _along(self, z):
        return self._copy(self.me, z, self.y, z)

    def _across(self, z):
        return self._copy(2 * z + self.y, self.z, 1 - self.y, 4 + z)

    def _pass_on(self, z):
        return self._copy(2 * z + self.y, self.others[1], self.y, 8 + z)

    def _arrived(self, slot):
        self._do(slot, lambda: self._copy(slot, self.z, 1 - self.y, 0).wait_recv())

    def start(self):
        def act():
            self._across(self.z).start()
            for z in self.others[:2]:
                self._along(z).start()

        self._do(self.me, act)

    def forward(self, *which):
        for n in which or (0, 1, 2):
            z = self.others[n]
            slot = 2 * z + self.y
            self._arrived(slot)
            self._do(slot, lambda: self._across(z).start())
            if n != 1:
                self._do(slot, lambda: self._pass_on(z).start(), self.inner)

    def finish(self):
        self._arrived(2 * self.z + 1 - self.y)
        for z in self.others:
            self._arrived(2 * z + 1 - self.y)

        def act():
            self._across(self.z).wait_send()
            for z in self.others[:2]:
                self._along(z).wait_send()

        self._do(self.me, act)
        for n, z in enumerate(self.others):
            self._do(2 * z + self.y, lambda: self._across(z).wait_send())
            if n != 1:
                self._do(2 * z + self.y, lambda: self._pass_on(z).wait_send(), self.inner)


def greet(blk_peers, dp_peers):
    dp, blk = lax.axis_index("dp"), lax.axis_index("blk")
    barrier = pltpu.get_barrier_semaphore()
    for k in range(1, blk_peers):
        pl.semaphore_signal(
            barrier, inc=1, device_id=(dp, (blk + k) % blk_peers), device_id_type=MESH
        )
    for k in range(1, dp_peers):
        pl.semaphore_signal(
            barrier, inc=1, device_id=((dp + k) % dp_peers, blk), device_id_type=MESH
        )
    pl.semaphore_wait(barrier, max(blk_peers - 1, 0) + max(dp_peers - 1, 0))


def call(body, name, ins, outs, scratch=(), collective_id=None, in_specs=None, out_specs=None):
    extra = {} if collective_id is None else {"collective_id": collective_id, "has_side_effects": True}
    return pl.pallas_call(
        body,
        out_shape=[jax.ShapeDtypeStruct(s, k) for s, k in outs],
        in_specs=in_specs or [VMEM] * len(ins),
        out_specs=out_specs or [VMEM] * len(outs),
        scratch_shapes=list(scratch),
        compiler_params=pltpu.CompilerParams(vmem_limit_bytes=LIMIT, **extra),
        name=name,
    )(*ins)


def pair_cols(p):
    return pl.ds(pl.multiple_of(p * 128, 128), 128)


def pick(own, block):
    return jnp.where(own, block, jnp.zeros_like(block))


class Refs:
    def __init__(self, names, refs):
        for name, ref in zip(names, refs, strict=True):
            setattr(self, name, ref)


def two(i):
    return pl.ds(2 * i, 2)


def rows_of(ref, i):
    return ref[two(i)].reshape(256, ref.shape[-1])


def span(i, size=256):
    return pl.ds(pl.multiple_of(i * size, size), size)


def head_col(block, h):
    return jnp.sum(jnp.where(lanes(block.shape) == h, block, 0.0), -1, keepdims=True)


def triangle(size):
    return lanes((size, size)) <= lax.broadcasted_iota(jnp.int32, (size, size), 0)


LAYER_IN = (
    "length", "mem", "x", "cot", "sq", "sk", "sv", "so_w", "wq", "wk", "wv", "wo", "wi", "wf",
    "gain", "shift", "sbias", "cbias", "vecs",
)
LAYER_OUT = ("n3_out", "input_grad", "mem_grad", "ag_o", "ag_out_o", "vec_out", "h1_o", "e_o")
LAYER_SCRATCH = (
    "par", "bi", "v_x", "v_sq", "v_sk", "v_sv", "v_so", "v_wq", "v_wo", "v_q", "v_k", "v_v", "v_low",
    "inv", "attn_own", "r1_own", "query", "mem_all", "low_all", "n3_all", "so_all", "co_all",
    "stats_all", "trade_src", "right", "slab_self", "slab_cross", "slab_in", "slab_out", "got",
    "got_out", "ag", "ag_out", "vec", "vq", "vgot", "vall", "load_sem", "x_send", "x_recv",
    "d_send", "d_recv", "g_send", "g_recv", "v_send", "v_recv",
)
GAIN, SHIFT, SBIAS, CBIAS, VBIAS, FBIAS = 0, 3, 6, 9, 11, 12


def self_half(slot):
    m = slot // 2
    return (slot % 2 + m * (m - 2) * (m - 3) // 2) % 2


def is_late(slot):
    return jnp.logical_and(slot < 6, self_half(slot) == 1)


def is_early(slot):
    return jnp.logical_or(slot >= 6, self_half(slot) == 0)


def hidden_offsets(me):
    return [pl.multiple_of(D * ((me + t) % 4) + 128 * (2 * t + me // 4), 128) for t in range(3)]


def layer_part(nb, ndp, *refs):
    r = Refs(LAYER_IN + LAYER_OUT + LAYER_SCRATCH, refs)
    dp, me = lax.axis_index("dp"), lax.axis_index("blk")
    own_rows = TGT // nb
    quarter = D // ndp
    mrows = r.mem.shape[0]
    total_rows = nb * mrows
    wide = (TGT, D)
    free = iter(range(64))

    def load(src, dst):
        copy = pltpu.make_async_copy(src, dst, r.load_sem.at[next(free)])
        copy.start()
        return copy

    def par(row):
        return r.par[row : row + 1, :]

    gathers = [
        Gather(buf, r.g_send.at[n], r.g_recv.at[n])
        for n, buf in enumerate((r.mem_all, r.low_all, r.n3_all, r.so_all, r.co_all, r.stats_all))
    ]
    g_mem, g_low, g_n3, g_so, g_co, g_stats = gathers
    g_groups = [
        Gather(r.ag.at[g], r.g_send.at[6 + g], r.g_recv.at[6 + g], live)
        for g, live in enumerate((is_late, None, None))
    ]
    g_early = Gather(r.ag.at[0], r.g_send.at[6], r.g_recv.at[6], is_early)
    g_groups.append(
        Gather(
            r.ag_out, r.g_send.at[9], r.g_recv.at[9], lambda slot: (dp - slot + nb) % 4 < 3
        )
    )

    slabs = (r.slab_self, r.slab_cross, r.slab_in)

    def share(g, k):
        peer = (dp + k) % ndp
        if g == 3:
            src, dst = r.slab_out.at[(peer - me + nb) % 4], r.got_out.at[k]
        else:
            src = slabs[g].at[pl.ds(pl.multiple_of(peer * quarter, 16), quarter), :]
            dst = r.got.at[g, k]
        return pltpu.make_async_remote_copy(
            src_ref=src, dst_ref=dst, send_sem=r.d_send.at[g, k], recv_sem=r.d_recv.at[g, k],
            device_id=(peer, me), device_id_type=MESH,
        )

    def share_start(g):
        for k in range(1, ndp):
            share(g, k).start()

    def settle(g, gather=None):
        for k in range(1, ndp):
            share(g, k).wait()
        if g == 3:
            total = r.slab_out[(dp - me + nb) % 4].astype(F32)
            for k in range(1, ndp):
                total = total + r.got_out[k].astype(F32)
            r.ag_out[me] = total.astype(BF)
        else:
            total = slabs[g][pl.ds(pl.multiple_of(dp * quarter, 16), quarter), :].astype(F32)
            for k in range(1, ndp):
                total = total + r.got[g, k].astype(F32)
            r.ag[g, me] = total.astype(BF)
        (gather or g_groups[g]).start()

    c_mem = load(r.mem, r.mem_all.at[me])
    c_x = load(r.x, r.v_x)
    c_qkv = [load(s, d) for s, d in ((r.sq, r.v_sq), (r.sk, r.v_sk), (r.sv, r.v_sv))]
    c_more = [load(s, d) for s, d in ((r.so_w, r.v_so), (r.wq, r.v_wq), (r.wo, r.v_wo))]
    r.par[0:3, :] = r.gain[...].astype(F32)
    r.par[3:6, :] = r.shift[...].astype(F32)
    r.par[6:9, :] = r.sbias[...].astype(F32)
    r.par[9:11, :] = r.cbias[...].astype(F32)
    r.par[11:13, :] = r.vecs[0:2, :]
    for c in range(4):
        r.bi[:, D * c : D * c + D] = r.vecs[2 + c : 3 + c, :]
    greet(nb, ndp)
    c_mem.wait()
    g_mem.start()
    c_x.wait()
    for c in c_qkv:
        c.wait()

    @pl.loop(0, 4)
    def _(i):
        rows = span(i)
        block = r.v_x[rows, :]
        r.v_q[rows, :] = ((dot(block, r.v_sq[...]) + par(SBIAS)) * SCALE).astype(BF)
        r.v_k[rows, :] = dot(block, r.v_sk[...]).astype(BF)
        r.v_v[rows, :] = (dot(block, r.v_sv[...]) + par(SBIAS + 1)).astype(BF)

    own = span(me, own_rows)
    second_own = lanes((own_rows, 128)) >= HEAD
    reach = lanes((own_rows, TGT)) - lax.broadcasted_iota(jnp.int32, (own_rows, TGT), 0)
    seen = reach <= me * own_rows

    @pl.loop(0, 6)
    def _(p):
        cols = pair_cols(p)
        found = []
        for a in (0, 1):
            head = pick(second_own == bool(a), r.v_q[own, cols])
            s = jnp.where(seen, dot_nt(head, r.v_k[:, cols]), NEG)
            e = jnp.exp(s - jnp.max(s, -1, keepdims=True))
            found.append(dot(e.astype(BF), r.v_v[:, cols]) / jnp.sum(e, -1, keepdims=True))
        r.attn_own[:, cols] = jnp.where(second_own, found[1], found[0]).astype(BF)

    g_mem.forward(0)
    for c in c_more:
        c.wait()
    r.r1_own[...] = r.v_x[own, :].astype(F32) + dot(r.attn_own[...], r.v_so[...]) + par(SBIAS + 2)

    r.inv[...] = jnp.zeros_like(r.inv)

    def pairs(first, last, between):
        def body(ebuf, esem):
            def keep(p):
                return pltpu.make_async_copy(ebuf.at[p % 2], r.e_o.at[p], esem.at[p % 2])

            size = 256

            def one_pair(p):
                slot = ebuf.at[p % 2]
                cols = pair_cols(p)
                for i in range(TGT // size):
                    rows = slice(i * size, (i + 1) * size)
                    place = i * (i + 1) // 2
                    second = lanes((size, 128)) >= HEAD
                    found, kept = [], r.inv[rows, :]
                    for a in (0, 1):
                        head = pick(second == bool(a), r.v_q[rows, cols])
                        last = (i + 1) * size
                        s = dot_nt(head, r.v_k[0:last, cols])
                        s_diag = jnp.where(triangle(size), s[:, i * size :], NEG)
                        s = jnp.concatenate([s[:, : i * size], s_diag], 1) if i else s_diag
                        e = jnp.exp(s - jnp.max(s, -1, keepdims=True))
                        total = jnp.sum(e, -1, keepdims=True)
                        e_low = e.astype(BF)
                        for j in range(i + 1):
                            slot[a, place + j] = e_low[:, j * size : (j + 1) * size]
                        part = dot(e_low, r.v_v[0:last, cols])
                        inverse = 1.0 / total
                        found.append(part * inverse)
                        kept = jnp.where(lanes((size, 128)) == 2 * p + a, inverse, kept)
                    r.v_low[rows, cols] = jnp.where(second, found[1], found[0]).astype(BF)
                    r.inv[rows, :] = kept
                keep(p).start()

            @pl.loop(first, last)
            def _(p):
                @pl.when(p >= first + 2)
                def _():
                    keep(p - 2).wait()

                one_pair(p)
                between(p)

            for p in range(max(first, last - 2), last):
                keep(p).wait()

        pl.run_scoped(
            body, pltpu.VMEM((2, 2, 10, 256, 256), BF), pltpu.SemaphoreType.DMA((2,))
        )

    def pass_memory(p):
        pl.when(p == 0)(lambda: g_mem.forward(1))
        pl.when(p == 1)(lambda: g_mem.forward(2))

    pairs(0, 3, pass_memory)

    def row_part(wi, wf, wk, wv, key, value, probs, slope, act, attn, cotv):
        c_kv = [load(r.wk, wk), load(r.wv, wv)]
        c_wi, c_cot, c_wf = load(r.wi, wi), load(r.cot.at[own, :], cotv), load(r.wf, wf)
        n1, inv1 = norm_parts(r.r1_own[...])
        h1 = n1 * par(GAIN) + par(SHIFT)
        query = ((dot(h1.astype(BF), r.v_wq[...]) + par(CBIAS)) * SCALE).astype(BF)
        for c in c_kv:
            c.wait()
        g_mem.finish()

        @pl.loop(0, total_rows // 256)
        def _(i):
            block = rows_of(r.mem_all, i)
            key[span(i), :] = dot(block, wk[...]).astype(BF)
            value[span(i), :] = (dot(block, wv[...]) + par(VBIAS)).astype(BF)

        live = lanes((own_rows, total_rows)) < r.length[0]
        stat = jnp.zeros((own_rows, 128), F32)
        for p in range(6):
            cols = slice(128 * p, 128 * p + 128)
            found = []
            for a in (0, 1):
                head = pick(second_own == bool(a), query[:, cols])
                s = jnp.where(live, dot_nt(head, key[:, cols]), NEG)
                top = jnp.max(s, -1, keepdims=True)
                e = jnp.exp(s - top)
                total = jnp.sum(e, -1, keepdims=True)
                pr = (e * (1.0 / total)).astype(BF)
                probs[2 * p + a] = pr
                found.append(dot(pr, value[:, cols]))
                stat = jnp.where(lanes((own_rows, 128)) == 2 * p + a, top + jnp.log(total), stat)
            attn[:, cols] = jnp.where(second_own, found[1], found[0])
        low = attn[...].astype(BF)
        r.low_all[me] = low
        g_low.start()
        r2 = h1 + dot(low, r.v_wo[...]) + par(CBIAS + 1)
        n2, inv2 = norm_parts(r2)
        h2 = n2 * par(GAIN + 1) + par(SHIFT + 1)
        h2_low = h2.astype(BF)
        c_wi.wait()

        @pl.loop(0, FF // 512)
        def _(c):
            cols = span(c, 512)
            up, down = gelu_parts(dot(h2_low, wi[:, cols]) + r.bi[:, cols])
            act[:, cols] = up.astype(BF)
            slope[:, cols] = down

        c_wf.wait()
        r3 = h2 + dot(act[...], wf[...]) + par(FBIAS)
        n3, inv3 = norm_parts(r3)
        r.n3_all[me] = n3.astype(BF)
        r.stats_all[me] = jnp.where(lanes((own_rows, 128)) == HEADS, inv3, stat).T[0:16, :]
        g_stats.start()
        g_n3.start()

        c_cot.wait()
        g3 = cotv[...].astype(F32)
        vec = r.vec
        vec[...] = jnp.zeros_like(vec)
        vec[2:3, :] = col_sum(g3 * n3)
        vec[5:6, :] = col_sum(g3)
        grad_r3 = norm_grad(g3, n3, inv3, par(GAIN + 2))
        z_low = grad_r3.astype(BF)
        vec[9:10, :] = col_sum(z_low.astype(F32))

        @pl.loop(0, FF // 512)
        def _(c):
            cols = span(c, 512)
            act[:, cols] = (dot_nt(z_low, wf[cols, :]) * slope[:, cols]).astype(BF)

        grad_h2 = grad_r3 + dot_nt(act[...], wi[...])
        vec[1:2, :] = col_sum(grad_h2 * n2)
        vec[4:5, :] = col_sum(grad_h2)
        grad_r2 = norm_grad(grad_h2, n2, inv2, par(GAIN + 1))
        co_low = grad_r2.astype(BF)
        r.co_all[me] = co_low
        vec[8:9, :] = col_sum(co_low.astype(F32))
        oc = dot_nt(co_low, r.v_wo[...]).astype(BF)
        product = oc.astype(F32) * attn[...]
        for p in range(6):
            cols = slice(128 * p, 128 * p + 128)
            found = []
            for a in (0, 1):
                sel = second_own == bool(a)
                delta = jnp.sum(jnp.where(sel, product[:, cols], 0.0), -1, keepdims=True)
                dprob = dot_nt(pick(sel, oc[:, cols]), value[:, cols])
                ds = (probs[2 * p + a].astype(F32) * (dprob - delta)).astype(BF)
                found.append(dot(ds, key[:, cols]))
            r.trade_src[2, :, cols] = (
                jnp.where(second_own, found[1], found[0]).astype(BF).astype(F32) * SCALE
            ).astype(BF)
        cq_low = r.trade_src[2]
        vec[7:8, :] = col_sum(cq_low.astype(F32))
        grad_h1 = grad_r2 + dot_nt(cq_low, r.v_wq[...])
        vec[0:1, :] = col_sum(grad_h1 * n1)
        vec[3:4, :] = col_sum(grad_h1)
        so_low = norm_grad(grad_h1, n1, inv1, par(GAIN)).astype(BF)
        r.so_all[me] = so_low
        vec[6:7, :] = col_sum(so_low.astype(F32))
        g_so.start()
        g_low.forward()

    memory_block = pltpu.VMEM((total_rows, D), BF)
    square = pltpu.VMEM((D, D), BF)
    pl.run_scoped(
        row_part,
        pltpu.VMEM((D, FF), BF), pltpu.VMEM((FF, D), BF), square, square, memory_block, memory_block,
        pltpu.VMEM((HEADS, own_rows, total_rows), BF),
        pltpu.VMEM((own_rows, FF), F32), pltpu.VMEM((own_rows, FF), BF),
        pltpu.VMEM((own_rows, D), F32), pltpu.VMEM((own_rows, D), BF),
    )

    def pass_n3(p):
        pl.when(p == 4)(lambda: g_n3.forward(0))
        pl.when(p == 5)(lambda: g_n3.forward(1))

    pairs(3, 6, pass_n3)
    g_co.start()

    def hidden_scope(h2_low, z_low, act, slope, wi_own, wf_own):
        offsets = hidden_offsets(me)
        c_cot = load(r.cot, z_low)
        own_w = [
            load(r.wi.at[:, pl.ds(off, 128)], wi_own.at[:, pl.ds(128 * t, 128)])
            for t, off in enumerate(offsets)
        ] + [
            load(r.wf.at[pl.ds(off, 128), :], wf_own.at[pl.ds(128 * t, 128), :])
            for t, off in enumerate(offsets)
        ]

        def hidden_forward(r1v, h1v):
            @pl.loop(0, 4)
            def _(i):
                rows = span(i)
                resid = (
                    r.v_x[rows, :].astype(F32) + dot(r.v_low[rows, :], r.v_so[...]) + par(SBIAS + 2)
                )
                n1, _ = norm_parts(resid)
                h1 = n1 * par(GAIN) + par(SHIFT)
                r1v[rows, :] = h1
                h1v[rows, :] = h1.astype(BF)
                r.query[rows, :] = (
                    (dot(h1.astype(BF), r.v_wq[...]) + par(CBIAS)) * SCALE
                ).astype(BF)

            c_h1 = load(h1v, r.h1_o)
            g_low.finish()
            g_n3.forward(2)
            g_stats.forward()
            g_so.forward(0)

            @pl.loop(0, 4)
            def _(i):
                r2 = r1v[span(i), :] + dot(rows_of(r.low_all, i), r.v_wo[...]) + par(CBIAS + 1)
                n2, _ = norm_parts(r2)
                h2_low[two(i)] = (
                    (n2 * par(GAIN + 1) + par(SHIFT + 1)).astype(BF).reshape(2, 128, D)
                )

            g_so.forward(1)
            c_h1.wait()

        pl.run_scoped(hidden_forward, pltpu.VMEM(wide, F32), pltpu.VMEM(wide, BF))
        for c in own_w:
            c.wait()
        bias = jnp.concatenate([r.bi[:, pl.ds(off, 128)] for off in offsets], axis=1)

        @pl.loop(0, 4)
        def _(i):
            up, down = gelu_parts(dot(rows_of(h2_low, i), wi_own[...]) + bias)
            act[span(i), :] = up.astype(BF)
            slope[span(i), :] = down

        def hidden_backward():
            g_stats.finish()
            g_n3.finish()
            g_so.forward(2)
            c_cot.wait()

            @pl.loop(0, 4)
            def _(i):
                normed = rows_of(r.n3_all, i).astype(F32)
                tile = r.stats_all[two(i)]
                inv3 = jnp.concatenate(
                    [
                        jnp.concatenate([tile[b], jnp.zeros((112, 128), F32)], 0).T[:, HEADS : HEADS + 1]
                        for b in (0, 1)
                    ],
                    0,
                )
                z_low[span(i), :] = norm_grad(
                    z_low[span(i), :].astype(F32), normed, inv3, par(GAIN + 2)
                ).astype(BF)

            for t in range(3):
                r.slab_out[t] = dot_tn(act[:, 128 * t : 128 * t + 128], z_low[...]).astype(BF)
            r.slab_out[3] = jnp.zeros_like(r.slab_out[3])
            share_start(3)

            @pl.loop(0, 4)
            def _(i):
                rows = span(i)
                act[rows, :] = (dot_nt(z_low[rows, :], wf_own[...]) * slope[rows, :]).astype(BF)

            total = col_sum(act[...].astype(F32))
            for t in range(3):
                lane = pl.ds(pl.multiple_of(128 * (2 * t + me // 4), 128), 128)
                which = lax.broadcasted_iota(jnp.int32, (4, 128), 0) == (me + t) % 4
                r.vec[13:17, lane] = jnp.where(which, total[:, 128 * t : 128 * t + 128], 0.0)

            @pl.loop(0, 3)
            def _(c):
                cols = span(c)
                r.slab_in[cols, :] = dot_tn(
                    h2_low[:, :, cols].reshape(TGT, 256), act[...]
                ).astype(BF)

            share_start(2)

        hidden_backward()

    pl.run_scoped(
        hidden_scope,
        pltpu.VMEM((nb, own_rows, D), BF), pltpu.VMEM(wide, BF),
        pltpu.VMEM((TGT, 384), BF), pltpu.VMEM((TGT, 384), F32),
        pltpu.VMEM((D, 384), BF), pltpu.VMEM((384, D), BF),
    )
    c_n3 = load(r.n3_all, r.n3_out)

    def trade(k, target, origin):
        source = (target // 2 + 2) % 3
        return pltpu.make_async_remote_copy(
            src_ref=r.trade_src.at[source, :, pl.ds(pl.multiple_of((target % 2) * 384, 128), 384)],
            dst_ref=r.right.at[origin],
            send_sem=r.x_send.at[k], recv_sem=r.x_recv.at[k],
            device_id=(dp, target), device_id_type=MESH,
        )

    def trade_start(first, last):
        for k in range(1, nb):
            target = (me + k) % nb
            wanted = jnp.logical_and(target >= first, target < last)
            pl.when(wanted)(lambda: trade(k, target, me).start())

    def vshare(k):
        peer = (dp + k) % ndp
        return pltpu.make_async_remote_copy(
            src_ref=r.vq.at[peer], dst_ref=r.vgot.at[k],
            send_sem=r.v_send.at[0, k], recv_sem=r.v_recv.at[0, k],
            device_id=(peer, me), device_id_type=MESH,
        )

    def vspread(k, origin):
        return pltpu.make_async_remote_copy(
            src_ref=r.vall.at[origin], dst_ref=r.vall.at[origin],
            send_sem=r.v_send.at[1, k], recv_sem=r.v_recv.at[1, k],
            device_id=(dp, (me + k) % nb), device_id_type=MESH,
        )

    def vectors_start():
        vec = r.vec[...]
        r.vq[...] = jnp.zeros_like(r.vq)
        for q in range(ndp):
            r.vq[q, 0:16, 0:quarter] = vec[0:16, quarter * q : quarter * q + quarter]
            for s in range(ndp):
                r.vq[q, 16 + s : 17 + s, 0:quarter] = vec[
                    13 + q : 14 + q, quarter * s : quarter * s + quarter
                ]
        for k in range(1, ndp):
            vshare(k).start()

    def vectors_spread():
        for k in range(1, ndp):
            vshare(k).wait()
        total = r.vq[dp]
        for k in range(1, ndp):
            total = total + r.vgot[k]
        r.vall[me] = total
        for k in range(1, nb):
            vspread(k, me).start()

    def self_part(go, gs, rights, dkt, dvt, qt, gt, left, ebuf, esem):
        size = 256

        def fetch(p):
            return pltpu.make_async_copy(r.e_o.at[p], ebuf.at[p % 2], esem.at[p % 2])

        fetch(0).start()
        g_so.finish()

        @pl.loop(0, 4)
        def _(i):
            go[span(i), :] = dot_nt(rows_of(r.so_all, i), r.v_so[...]).astype(BF)

        def one_pair(p):
            @pl.when(p + 1 < 6)
            def _():
                fetch(p + 1).start()

            cols = pair_cols(p)
            second = lanes((size, 128)) >= HEAD
            deltas = []
            for i in range(TGT // size):
                rows = slice(i * size, (i + 1) * size)
                invs = [head_col(r.inv[rows, :], 2 * p + a) for a in (0, 1)]
                scaled = go[rows, cols].astype(F32) * jnp.where(second, invs[1], invs[0])
                gs[rows, :] = scaled.astype(BF)
                product = scaled * r.v_low[rows, cols].astype(F32)
                deltas.append(
                    [
                        jnp.sum(jnp.where(second == bool(a), product, 0.0), -1, keepdims=True)
                        for a in (0, 1)
                    ]
                )
            qt[...] = r.v_q[:, cols].T
            gt[...] = gs[...].T
            fetch(p).wait()
            slot = ebuf.at[p % 2]
            for i in reversed(range(TGT // size)):
                rows = slice(i * size, (i + 1) * size)
                found = []
                for a in (0, 1):
                    own_g = pick(second == bool(a), gs[rows, :])
                    head = slice(HEAD * a, HEAD * a + HEAD)
                    last = (i + 1) * size
                    place = i * (i + 1) // 2
                    e = jnp.concatenate([slot[a, place + j] for j in range(i + 1)], 1)
                    dprob = dot_nt(own_g, r.v_v[0:last, cols])
                    ds = (e.astype(F32) * (dprob - deltas[i][a])).astype(BF)
                    found.append(dot(ds, r.v_k[0:last, cols]))
                    part_k = dot(qt[head, rows], ds)
                    part_v = dot(gt[head, rows], e)
                    if last == TGT:
                        dkt[head, :] = part_k
                        dvt[head, :] = part_v
                    else:
                        dkt[head, 0:last] += part_k
                        dvt[head, 0:last] += part_v
                rights[0, rows, cols] = (
                    jnp.where(second, found[1], found[0]).astype(BF).astype(F32) * SCALE
                ).astype(BF)
            rights[1, :, cols] = dkt[...].T.astype(BF)
            rights[2, :, cols] = dvt[...].T.astype(BF)

        left_sem = r.load_sem.at[next(free)]
        square_block = pltpu.VMEM((mrows, D), BF)

        def memory_part(wk, wv, key, value, oc, lse_t, delta_t):
            c_kv = [load(r.wk, wk), load(r.wv, wv)]

            @pl.when(jnp.logical_and(me >= 2, me < 6))
            def _():
                pltpu.make_async_copy(r.mem_all, left, left_sem).start()

            for b in range(nb):
                rows = pl.ds(own_rows * b, own_rows)

                @pl.when(me < 2)
                def _():
                    pltpu.make_async_copy(r.h1_o.at[rows, :], left.at[b], left_sem).start()

            @pl.when(me >= 6)
            def _():
                pltpu.make_async_copy(r.low_all, left, left_sem).start()

            g_co.finish()
            member = jnp.where(
                lax.broadcasted_iota(jnp.int32, (16, D), 1) // HEAD
                == lax.broadcasted_iota(jnp.int32, (16, D), 0),
                1.0,
                0.0,
            ).astype(BF)
            for i in range(4):
                rows = slice(256 * i, 256 * i + 256)
                grad_out = dot_nt(rows_of(r.co_all, i), r.v_wo[...]).astype(BF)
                oc[rows, :] = grad_out
                product = grad_out.astype(F32) * rows_of(r.low_all, i).astype(F32)
                big = product.astype(BF)
                small = (product - big.astype(F32)).astype(BF)
                delta_t[:, rows] = dot_nt(member, big) + dot_nt(member, small)
                lse_t[:, rows] = jnp.concatenate([r.stats_all[2 * i], r.stats_all[2 * i + 1]], 1)
            for c in c_kv:
                c.wait()
            key[...] = dot(r.mem_all[me], wk[...]).astype(BF)
            value[...] = (dot(r.mem_all[me], wv[...]) + par(VBIAS)).astype(BF)
            position = me * mrows + lax.broadcasted_iota(jnp.int32, (mrows, 1), 0)
            live = position < r.length[0]
            second = lanes((mrows, 128)) >= HEAD

            @pl.loop(0, 6)
            def _(p):
                cols = pair_cols(p)
                found_k, found_v = [], []
                for a in (0, 1):
                    sel = second == bool(a)
                    s = dot_nt(pick(sel, key[:, cols]), r.query[:, cols])
                    pr = jnp.where(live, jnp.exp(s - lse_t[pl.ds(2 * p + a, 1), :]), 0.0)
                    dprob = dot_nt(pick(sel, value[:, cols]), oc[:, cols])
                    ds = (pr * (dprob - delta_t[pl.ds(2 * p + a, 1), :])).astype(BF)
                    found_k.append(dot(ds, r.query[:, cols]))
                    found_v.append(dot(pr.astype(BF), oc[:, cols]))
                r.trade_src[0, :, cols] = jnp.where(second, found_k[1], found_k[0]).astype(BF)
                r.trade_src[1, :, cols] = jnp.where(second, found_v[1], found_v[0]).astype(BF)

            trade_start(2, 6)
            dk, dv = r.trade_src[0], r.trade_src[1]
            r.mem_grad[...] = (dot_nt(dk, wk[...]) + dot_nt(dv, wv[...])).astype(BF)
            r.vec[12:13, :] = col_sum(dv.astype(F32))

        half = pl.ds(pl.multiple_of((me % 2) * 384, 128), 384)

        def form_cross():
            @pl.when(me < 6)
            def _():
                r.right[me] = r.trade_src[(me // 2 + 2) % 3, :, half]
                for k in range(1, nb):
                    trade(k, (me + k) % nb, (me + nb - k) % nb).wait_recv()

            @pl.when(me >= 6)
            def _():
                r.right[...] = r.co_all[:, :, half]

            pltpu.make_async_copy(r.mem_all, left, left_sem).wait()

            @pl.loop(0, 3)
            def _(c):
                r.slab_cross[span(c), :] = dot_tn(
                    left[:, :, span(c)].reshape(TGT, 256), r.right[...].reshape(TGT, 384)
                ).astype(BF)

            share_start(1)

        self_cols = pl.ds(pl.multiple_of(self_half(me) * 384, 128), 384)

        def self_slab_qkv():
            @pl.loop(0, 3)
            def _(c):
                r.slab_self[span(c), :] = dot_tn(
                    r.v_x[:, span(c)], rights[me // 2, :, self_cols]
                ).astype(BF)

        def self_early():
            @pl.when(jnp.logical_and(is_early(me), me < 6))
            def _():
                self_slab_qkv()

            @pl.when(me >= 6)
            def _():
                @pl.loop(0, 3)
                def _(c):
                    r.slab_self[span(c), :] = dot_tn(
                        r.v_low[:, span(c)], r.so_all[:, :, self_cols].reshape(TGT, 384)
                    ).astype(BF)

            pl.when(is_early(me))(lambda: share_start(0))

        def run_memory():
            pl.run_scoped(
                memory_part,
                square, square, square_block, square_block,
                pltpu.VMEM(wide, BF), pltpu.VMEM((16, TGT), F32), pltpu.VMEM((16, TGT), F32),
            )

        @pl.loop(0, 6)
        def _(p):
            @pl.when(p == 0)
            def _():
                g_co.forward()
                trade_start(0, 2)

            @pl.when(p == 2)
            def _():
                settle(3)
                run_memory()

            @pl.when(p == 3)
            def _():
                settle(2)
                self_early()

            @pl.when(p == 4)
            def _():
                g_groups[3].forward()
                pl.when(is_early(me))(lambda: settle(0, g_early))

            @pl.when(p == 5)
            def _():
                form_cross()
                g_groups[2].forward()

            one_pair(p)

        @pl.when(is_late(me))
        def _():
            self_slab_qkv()
            share_start(0)

        settle(1)
        g_early.forward()
        pl.when(is_late(me))(lambda: settle(0))

        @pl.loop(0, 4)
        def _(i):
            rows = span(i)
            sq, sk, sv = rights[0, rows, :], rights[1, rows, :], rights[2, rows, :]
            go[rows, :] = (
                rows_of(r.so_all, i).astype(F32)
                + dot_nt(sq, r.v_sq[...])
                + dot_nt(sk, r.v_sk[...])
                + dot_nt(sv, r.v_sv[...])
            ).astype(BF)
            r.vec[10:11, :] += col_sum(sq.astype(F32)) * (1.0 / nb)
            r.vec[11:12, :] += col_sum(sv.astype(F32)) * (1.0 / nb)

        c_grad = load(go, r.input_grad)
        vectors_start()
        g_groups[1].forward()
        g_groups[0].forward()
        vectors_spread()
        c_grad.wait()


    pl.run_scoped(
        self_part,
        pltpu.VMEM(wide, BF), pltpu.VMEM((TGT, 128), BF), pltpu.VMEM((3,) + wide, BF),
        pltpu.VMEM((128, TGT), F32), pltpu.VMEM((128, TGT), F32),
        pltpu.VMEM((128, TGT), BF), pltpu.VMEM((128, TGT), BF), pltpu.VMEM((nb, own_rows, D), BF),
        pltpu.VMEM((2, 2, 10, 256, 256), BF), pltpu.SemaphoreType.DMA((2,)),
    )

    outs = []

    def collect(g):
        g_groups[g].finish()
        outs.append(load(r.ag_out, r.ag_out_o) if g == 3 else load(r.ag.at[g], r.ag_o.at[g]))

    collect(3)
    collect(2)
    g_early.finish()
    collect(1)
    collect(0)
    for k in range(1, nb):
        vspread(k, (me + nb - k) % nb).wait_recv()
    total = r.vall[0]
    for b in range(1, nb):
        total = total + r.vall[b]
    r.vec_out[...] = total
    for k in range(1, nb):
        target = (me + k) % nb
        pl.when(target < 6)(lambda: trade(k, target, me).wait_send())
        vspread(k, me).wait_send()
    for c in outs:
        c.wait()
    c_n3.wait()


FINISH_IN = ("n3", "grad_in", "mem_in", "ag", "ag_out", "vec", "gain", "shift")
FINISH_OUT = (
    "out", "input_grad", "mem_grad", "s_q", "s_k", "s_v", "s_o", "c_k", "c_v", "c_q", "c_o", "f_in",
    "f_out", "self_bias", "cross_bias", "cv", "d_gain", "d_shift", "in_bias", "out_bias",
)
FINISH_SCRATCH = ("v_ag", "v_ag_out", "v_n3", "v_f", "v_in", "v_out", "v_y", "v_grad", "v_mem", "sem")


def finish_part(nb, ndp, *refs):
    r = Refs(FINISH_IN + FINISH_OUT + FINISH_SCRATCH, refs)
    dp = lax.axis_index("dp")
    quarter = D // ndp
    free = iter(range(32))

    def move(src, dst):
        copy = pltpu.make_async_copy(src, dst, r.sem.at[next(free)])
        copy.start()
        return copy

    c_ag = [move(r.ag.at[g], r.v_ag.at[g]) for g in range(3)]
    c_out, c_n3 = move(r.ag_out, r.v_ag_out), move(r.n3, r.v_n3)
    c_grad, c_mem = move(r.grad_in, r.v_grad), move(r.mem_in, r.v_mem)
    done = []
    vec = r.vec
    for ref, rows in (
        (r.self_bias, (10, 11, 6)), (r.cross_bias, (7, 8)), (r.d_gain, (0, 1, 2)),
        (r.d_shift, (3, 4, 5)), (r.cv, (12,)), (r.out_bias, (9,)),
    ):
        for n, row in enumerate(rows):
            ref[n : n + 1, :] = vec[row : row + 1, 0:quarter]
    for s in range(ndp):
        r.in_bias[:, quarter * s : quarter * s + quarter] = vec[16 + s : 17 + s, 0:quarter]
    for g, dsts in ((0, (r.s_q, r.s_k, r.s_v, r.s_o)), (1, (r.c_q, r.c_k, r.c_v, r.c_o))):
        c_ag[g].wait()
        for n, dst in enumerate(dsts):
            for b in (2 * n, 2 * n + 1):
                h = self_half(b) if g == 0 else b % 2
                half = slice(384 * h, 384 * h + 384)
                r.v_f[4 * g + n, :, half] = r.v_ag[g, b].astype(F32)
            done.append(move(r.v_f.at[4 * g + n], dst))
    c_grad.wait()
    c_mem.wait()
    done += [move(r.v_grad, r.input_grad), move(r.v_mem, r.mem_grad)]
    c_ag[2].wait()
    for b in range(nb):
        for t in range(3):
            col = D * ((b + t) % 4) + 128 * (2 * t + b // 4)
            r.v_in[:, col : col + 128] = r.v_ag[2, b, :, 128 * t : 128 * t + 128].astype(F32)
    done.append(move(r.v_in, r.f_in))
    c_out.wait()
    for b in range(nb):
        t = (dp - b + nb) % 4

        @pl.when(t < 3)
        def _():
            place = pl.ds(pl.multiple_of(128 * (2 * t + b // 4), 128), 128)
            r.v_out[place, :] = r.v_ag_out[b].astype(F32)

    done.append(move(r.v_out, r.f_out))
    c_n3.wait()
    gain, shift = r.gain[...].astype(F32)[2:3, :], r.shift[...].astype(F32)[2:3, :]

    @pl.loop(0, nb)
    def _(b):
        r.v_y[b] = (r.v_n3[b].astype(F32) * gain + shift).astype(BF)

    done.append(move(r.v_y, r.out))
    for c in done:
        c.wait()


def shared_work(
    nb, ndp,
    inputs, memory, lengths, cotangent, self_query, self_key, self_value, self_out, self_bias,
    cross_query, cross_key, cross_value, cross_out, cross_bias, cross_value_bias,
    norm_gain, norm_bias, ffn_in, ffn_in_bias, ffn_out, ffn_out_bias,
):
    own_rows = TGT // nb
    x, mem, cot = inputs[0], memory[0], cotangent[0]
    mrows = mem.shape[0]
    quarter = D // ndp
    gain, shift = norm_gain.T, norm_bias.T
    vecs = (
        jnp.concatenate([cross_value_bias, ffn_out_bias, ffn_in_bias]).reshape(6, D).astype(F32)
    )
    wide, own, square, block = (TGT, D), (own_rows, D), (D, D), (nb, own_rows, D)
    dma = pltpu.SemaphoreType.DMA
    vm = pltpu.VMEM
    n3, grad_in, mem_grad, ag, ag_out, vec, _, _ = call(
        functools.partial(layer_part, nb, ndp),
        "layer_part",
        (lengths, mem, x, cot, self_query, self_key, self_value, self_out, cross_query, cross_key,
         cross_value, cross_out, ffn_in, ffn_out, gain, shift, self_bias.T, cross_bias.T, vecs),
        [(block, BF), (wide, BF), ((mrows, D), BF), ((3, nb, quarter, 384), BF), ((nb, 128, D), BF),
         ((24, 256), F32), (wide, BF), ((6, 2, 10, 256, 256), BF)],
        [vm((16, D), F32), vm((1, FF), F32), vm(wide, BF)]
        + [vm(square, BF)] * 6
        + [vm(wide, BF)] * 4
        + [vm((TGT, 128), F32), vm(own, BF), vm(own, F32), vm(wide, BF), vm((nb, mrows, D), BF)]
        + [vm(block, BF)] * 4
        + [vm((nb, 16, own_rows), F32), vm((3, own_rows, D), BF), vm((nb, own_rows, 384), BF)]
        + [vm((D, 384), BF)] * 3
        + [vm((4, 128, D), BF), vm((3, ndp, quarter, 384), BF), vm((ndp, 128, D), BF),
           vm((3, nb, quarter, 384), BF), vm((nb, 128, D), BF),
           vm((24, D), F32), vm((ndp, 24, 256), F32), vm((ndp, 24, 256), F32), vm((nb, 24, 256), F32)]
        + [dma((64,)), dma((nb,)), dma((nb,)), dma((4, ndp)), dma((4, ndp)), dma((10, 12)),
           dma((10, nb)), dma((2, nb)), dma((2, nb))],
        collective_id=0,
        in_specs=[SMEM] + [ANY] * 13 + [VMEM] * 5,
        out_specs=[ANY] * 2 + [VMEM] + [ANY] * 2 + [VMEM] + [ANY] * 2,
    )
    weight = ((quarter, D), F32)
    (
        out, input_grad, memory_grad, s_q, s_k, s_v, s_o, c_k, c_v, c_q, c_o, f_in, f_out,
        g_self_bias, g_cross_bias, g_cv, g_gain, g_shift, g_in_bias, g_out_bias,
    ) = call(
        functools.partial(finish_part, nb, ndp),
        "finish_part",
        (n3, grad_in, mem_grad, ag, ag_out, vec, gain, shift),
        [(block, BF), (wide, BF), ((mrows, D), BF)]
        + [weight] * 8
        + [((quarter, FF), F32), ((FF // ndp, D), F32), ((3, quarter), F32), ((2, quarter), F32),
           ((1, quarter), F32), ((3, quarter), F32), ((3, quarter), F32), ((1, FF // ndp), F32),
           ((1, quarter), F32)],
        [vm((3, nb, quarter, 384), BF), vm((nb, 128, D), BF), vm(block, BF),
         vm((8, quarter, D), F32), vm((quarter, FF), F32), vm((FF // ndp, D), F32), vm(block, BF),
         vm(wide, BF), vm((mrows, D), BF), dma((32,))],
        in_specs=[ANY] * 5 + [VMEM] * 3,
        out_specs=[ANY] * 13 + [VMEM] * 7,
    )
    return (
        out.reshape(1, TGT, D), input_grad[None], memory_grad[None],
        s_q, s_k, s_v, s_o, g_self_bias.T, c_q, c_k, c_v, c_o, g_cross_bias.T, g_cv.reshape(quarter),
        g_gain.T, g_shift.T, f_in, g_in_bias.reshape(FF // ndp), f_out, g_out_bias.reshape(quarter),
    )


def merged(array, axis, join):
    gathered = jax.tree.map(
        lambda a, kind: lax.all_gather(a.astype(kind), axis), array, (jnp.bfloat16, jnp.bfloat16)
    )

    def take(source):
        return jax.tree.map(
            lambda a, own: lax.dynamic_index_in_dim(a, source, 0, False).astype(own.dtype),
            gathered,
            array,
        )

    return lax.fori_loop(
        1, lax.axis_size(axis), lambda source, state: join(state, take(source)), take(0)
    )


def layer_norm(residual, gain_col, shift_col):
    average = jnp.mean(residual, axis=-1, keepdims=True)
    centered = residual - average
    variance = jnp.mean(centered * centered, axis=-1, keepdims=True)
    return centered * lax.rsqrt(variance + EPS) * gain_col + shift_col


def exact_gelu(values):
    return jax.nn.gelu(values, approximate=False)


def project(left_side, weight):
    return jnp.dot(left_side, weight, preferred_element_type=jnp.float32)


def project_back(gradient, weight):
    return lax.dot_general(
        gradient, weight, (((1,), (1,)), ((), ())), preferred_element_type=jnp.float32
    )


def weight_grad(left_side, gradient):
    return lax.dot_general(
        left_side, gradient, (((0,), (0,)), ((), ())), preferred_element_type=jnp.float32
    )


def column_sum(gradient):
    return jnp.sum(gradient.astype(jnp.float32), axis=0)


def split_heads(values):
    return values.reshape(values.shape[:-1] + (HEADS, HEAD))


def combine_totals(earlier, latter):
    top_a, sum_a = earlier
    top_b, sum_b = latter
    top_score = jnp.maximum(top_a, top_b)
    return (top_score, sum_a * jnp.exp(top_a - top_score) + sum_b * jnp.exp(top_b - top_score))


def self_scores(query_rows, key_rows, row_start, block_rows):
    scores = jnp.einsum("qhe,khe->hqk", query_rows, key_rows, preferred_element_type=jnp.float32)
    row_pos = row_start + jnp.arange(block_rows)[:, None]
    col_pos = jnp.arange(key_rows.shape[0])[None, :]
    return jnp.where((col_pos <= row_pos)[None], scores, NEG)


def copied_work(
    inputs,
    memory,
    lengths,
    cotangent,
    self_query,
    self_key,
    self_value,
    self_out,
    self_bias,
    cross_query,
    cross_key,
    cross_value,
    cross_out,
    cross_bias,
    cross_value_bias,
    norm_gain,
    norm_bias,
    ffn_in,
    ffn_in_bias,
    ffn_out,
    ffn_out_bias,
):
    all_rows = ITEMS * TGT
    block_rows = min(512, TGT)
    mem_rows = memory.shape[1]
    self_bias_f = self_bias.astype(jnp.float32)
    cross_bias_f = cross_bias.astype(jnp.float32)
    gains = norm_gain.astype(jnp.float32)
    shifts = norm_bias.astype(jnp.float32)
    flat_in = inputs.reshape(all_rows, D)
    query_self = split_heads(
        ((project(flat_in, self_query) + self_bias_f[:, 0]) * SCALE)
        .astype(jnp.bfloat16)
        .reshape(ITEMS, TGT, D)
    )
    key_self = split_heads(project(flat_in, self_key).astype(jnp.bfloat16).reshape(ITEMS, TGT, D))
    value_self = split_heads(
        (project(flat_in, self_value) + self_bias_f[:, 1])
        .astype(jnp.bfloat16)
        .reshape(ITEMS, TGT, D)
    )
    item_index = 0
    attn_blocks = []
    lse_blocks = []
    for row_start in range(0, TGT, block_rows):
        row_end = row_start + block_rows
        scores = self_scores(
            query_self[item_index, row_start:row_end],
            key_self[item_index, :row_end],
            row_start,
            block_rows,
        )
        top_score = jnp.max(scores, axis=-1, keepdims=True)
        log_total = top_score + jnp.log(
            jnp.sum(jnp.exp(scores - top_score), axis=-1, keepdims=True)
        )
        probs_low = jnp.exp(scores - log_total).astype(jnp.bfloat16)
        attn_blocks.append(
            jnp.einsum(
                "hqk,khe->qhe",
                probs_low,
                value_self[item_index, :row_end],
                preferred_element_type=jnp.float32,
            )
        )
        lse_blocks.append(log_total)
    attn_items = [jnp.concatenate(attn_blocks, axis=0)]
    lse_self = [lse_blocks]
    self_attn = jnp.stack(attn_items, axis=0)
    self_low = self_attn.astype(jnp.bfloat16).reshape(all_rows, D)
    resid_one = flat_in.astype(jnp.float32) + project(self_low, self_out) + self_bias_f[:, 2]
    hidden_one, norm1_back = jax.vjp(layer_norm, resid_one, gains[:, 0], shifts[:, 0])
    hidden_low = hidden_one.astype(jnp.bfloat16)
    query_cross = split_heads(
        ((project(hidden_low, cross_query) + cross_bias_f[:, 0]) * SCALE)
        .astype(jnp.bfloat16)
        .reshape(ITEMS, TGT, D)
    )
    flat_mem = memory.reshape(ITEMS * mem_rows, D)
    key_cross = split_heads(
        project(flat_mem, cross_key).astype(jnp.bfloat16).reshape(ITEMS, mem_rows, D)
    )
    value_cross = split_heads(
        (project(flat_mem, cross_value) + cross_value_bias.astype(jnp.float32))
        .astype(jnp.bfloat16)
        .reshape(ITEMS, mem_rows, D)
    )
    position = lax.axis_index("blk") * mem_rows + jnp.arange(mem_rows)
    live_mask = position[None, :] < lengths[:, None]

    def cross_scores():
        raw_scores = jnp.einsum(
            "bqhe,bkhe->bhqk", query_cross, key_cross, preferred_element_type=jnp.float32
        )
        return jnp.where(live_mask[:, None, None, :], raw_scores, NEG)

    scores = cross_scores()
    top_local = jnp.max(scores, axis=-1)
    sum_local = jnp.sum(jnp.exp(scores - top_local[..., None]), axis=-1)
    top_all, sum_all = merged((top_local, sum_local), "blk", combine_totals)
    cross_lse = top_all + jnp.log(sum_all)
    probs_low = jnp.exp(scores - cross_lse[..., None]).astype(jnp.bfloat16)
    share_out = jnp.einsum(
        "bhqk,bkhe->bqhe", probs_low, value_cross, preferred_element_type=jnp.float32
    ).reshape(all_rows, D)
    cot_flat = cotangent.reshape(all_rows, D)
    attn_rows = lax.psum(share_out, "blk")
    cross_low = attn_rows.astype(jnp.bfloat16)
    resid_two = hidden_one + project(cross_low, cross_out) + cross_bias_f[:, 1]
    hidden_two, norm2_back = jax.vjp(layer_norm, resid_two, gains[:, 1], shifts[:, 1])
    second_low = hidden_two.astype(jnp.bfloat16)
    pre_act = project(second_low, ffn_in) + ffn_in_bias.astype(jnp.float32)
    activated, gelu_back = jax.vjp(exact_gelu, pre_act)
    act_low = activated.astype(jnp.bfloat16)
    resid_three = hidden_two + project(act_low, ffn_out) + ffn_out_bias.astype(jnp.float32)
    result, norm3_back = jax.vjp(layer_norm, resid_three, gains[:, 2], shifts[:, 2])
    result_low = result.astype(jnp.bfloat16)
    grad_r3, grad_gain3, grad_shift3 = norm3_back(cot_flat.astype(jnp.float32))
    z_low = grad_r3.astype(jnp.bfloat16)
    g_ffn_out = weight_grad(act_low, z_low)
    g_ffn_out_bias = column_sum(z_low)
    (grad_pre,) = gelu_back(project_back(z_low, ffn_out))
    pre_low = grad_pre.astype(jnp.bfloat16)
    g_ffn_in = weight_grad(second_low, pre_low)
    g_ffn_in_bias = column_sum(pre_low)
    grad_h2 = grad_r3 + project_back(pre_low, ffn_in)
    grad_r2, grad_gain2, grad_shift2 = norm2_back(grad_h2)
    co_low = grad_r2.astype(jnp.bfloat16)
    g_cross_out = weight_grad(cross_low, co_low)
    g_co_bias = column_sum(co_low)
    oc_low = project_back(co_low, cross_out).astype(jnp.bfloat16)
    out_rows = result_low.reshape(ITEMS, TGT, D)
    grad_oc = split_heads(oc_low.reshape(ITEMS, TGT, D))
    cross_delta = jnp.transpose(
        jnp.sum(
            grad_oc.astype(jnp.float32) * split_heads(attn_rows.reshape(ITEMS, TGT, D)), axis=-1
        ),
        (0, 2, 1),
    )
    scores = cross_scores()
    prob_full = jnp.exp(scores - cross_lse[..., None])
    grad_probs = jnp.einsum(
        "bqhe,bkhe->bhqk", grad_oc, value_cross, preferred_element_type=jnp.float32
    )
    grad_scores = (prob_full * (grad_probs - cross_delta[..., None])).astype(jnp.bfloat16)
    query_share = jnp.einsum(
        "bhqk,bkhe->bqhe", grad_scores, key_cross, preferred_element_type=jnp.float32
    ).reshape(all_rows, D)
    key_low = (
        jnp.einsum("bhqk,bqhe->bkhe", grad_scores, query_cross, preferred_element_type=jnp.float32)
        .astype(jnp.bfloat16)
        .reshape(ITEMS * mem_rows, D)
    )
    value_low = (
        jnp.einsum(
            "bhqk,bqhe->bkhe",
            prob_full.astype(jnp.bfloat16),
            grad_oc,
            preferred_element_type=jnp.float32,
        )
        .astype(jnp.bfloat16)
        .reshape(ITEMS * mem_rows, D)
    )
    grad_cq = lax.psum(query_share, "blk")
    cq_low = (grad_cq * SCALE).astype(jnp.bfloat16)
    g_cross_query = weight_grad(hidden_one.astype(jnp.bfloat16), cq_low)
    g_cq_bias = column_sum(cq_low)
    grad_h1_rows = grad_r2 + project_back(cq_low, cross_query)
    g_cross_key_dev = weight_grad(flat_mem, key_low)
    g_cross_value_dev = weight_grad(flat_mem, value_low)
    g_cv_bias_dev = column_sum(value_low)
    memory_grad = (
        (project_back(key_low, cross_key) + project_back(value_low, cross_value))
        .astype(jnp.bfloat16)
        .reshape(ITEMS, mem_rows, D)
    )
    g_cross_key, g_cross_value, g_cv_bias = lax.psum(
        (g_cross_key_dev, g_cross_value_dev, g_cv_bias_dev), "blk"
    )
    grad_r1, grad_gain1, grad_shift1 = norm1_back(grad_h1_rows)
    so_low = grad_r1.astype(jnp.bfloat16)
    g_self_out = weight_grad(self_low, so_low)
    g_so_bias = column_sum(so_low)
    grad_os = split_heads(
        project_back(so_low, self_out).astype(jnp.bfloat16).reshape(ITEMS, TGT, D)
    )
    item_index = 0
    key_grad = jnp.zeros((TGT, HEADS, HEAD), jnp.float32)
    value_grad = jnp.zeros((TGT, HEADS, HEAD), jnp.float32)
    query_blocks = []
    for row_start in range(0, TGT, block_rows):
        row_end = row_start + block_rows
        query_rows = query_self[item_index, row_start:row_end]
        key_rows = key_self[item_index, :row_end]
        scores = self_scores(query_rows, key_rows, row_start, block_rows)
        prob_full = jnp.exp(scores - lse_self[item_index][row_start // block_rows])
        grad_out = grad_os[item_index, row_start:row_end]
        row_delta = jnp.transpose(
            jnp.sum(
                grad_out.astype(jnp.float32) * self_attn[item_index, row_start:row_end], axis=-1
            )
        )
        grad_probs = jnp.einsum(
            "qhe,khe->hqk",
            grad_out,
            value_self[item_index, :row_end],
            preferred_element_type=jnp.float32,
        )
        grad_scores = (prob_full * (grad_probs - row_delta[:, :, None])).astype(jnp.bfloat16)
        query_blocks.append(
            jnp.einsum("hqk,khe->qhe", grad_scores, key_rows, preferred_element_type=jnp.float32)
        )
        key_grad = key_grad.at[:row_end].add(
            jnp.einsum("hqk,qhe->khe", grad_scores, query_rows, preferred_element_type=jnp.float32)
        )
        value_grad = value_grad.at[:row_end].add(
            jnp.einsum(
                "hqk,qhe->khe",
                prob_full.astype(jnp.bfloat16),
                grad_out,
                preferred_element_type=jnp.float32,
            )
        )
    query_items = [jnp.concatenate(query_blocks, axis=0)]
    key_items = [key_grad]
    value_items = [value_grad]
    sq_low = (jnp.stack(query_items, 0).astype(jnp.bfloat16) * jnp.bfloat16(SCALE)).reshape(
        all_rows, D
    )
    sk_low = jnp.stack(key_items, 0).astype(jnp.bfloat16).reshape(all_rows, D)
    sv_low = jnp.stack(value_items, 0).astype(jnp.bfloat16).reshape(all_rows, D)
    g_self_query = weight_grad(flat_in, sq_low)
    g_self_key = weight_grad(flat_in, sk_low)
    g_self_value = weight_grad(flat_in, sv_low)
    g_sq_bias = column_sum(sq_low)
    g_sv_bias = column_sum(sv_low)
    input_grad = (
        (
            grad_r1
            + project_back(sq_low, self_query)
            + project_back(sk_low, self_key)
            + project_back(sv_low, self_value)
        )
        .astype(jnp.bfloat16)
        .reshape(ITEMS, TGT, D)
    )
    g_self_bias = jnp.stack([g_sq_bias, g_sv_bias, g_so_bias], axis=1)
    g_cross_bias = jnp.stack([g_cq_bias, g_co_bias], axis=1)
    g_norm_gain = jnp.stack([grad_gain1, grad_gain2, grad_gain3], axis=1)
    g_norm_bias = jnp.stack([grad_shift1, grad_shift2, grad_shift3], axis=1)
    summed = (
        lax.psum_scatter(
            g_self_query.astype(jnp.bfloat16), "dp", scatter_dimension=0, tiled=True
        ).astype(jnp.float32),
        lax.psum_scatter(
            g_self_key.astype(jnp.bfloat16), "dp", scatter_dimension=0, tiled=True
        ).astype(jnp.float32),
        lax.psum_scatter(
            g_self_value.astype(jnp.bfloat16), "dp", scatter_dimension=0, tiled=True
        ).astype(jnp.float32),
        lax.psum_scatter(
            g_self_out.astype(jnp.bfloat16), "dp", scatter_dimension=0, tiled=True
        ).astype(jnp.float32),
        lax.psum_scatter(
            g_cross_query.astype(jnp.bfloat16), "dp", scatter_dimension=0, tiled=True
        ).astype(jnp.float32),
        lax.psum_scatter(
            g_cross_key.astype(jnp.bfloat16), "dp", scatter_dimension=0, tiled=True
        ).astype(jnp.float32),
        lax.psum_scatter(
            g_cross_value.astype(jnp.bfloat16), "dp", scatter_dimension=0, tiled=True
        ).astype(jnp.float32),
        lax.psum_scatter(
            g_cross_out.astype(jnp.bfloat16), "dp", scatter_dimension=0, tiled=True
        ).astype(jnp.float32),
        lax.psum_scatter(
            g_ffn_in.astype(jnp.bfloat16), "dp", scatter_dimension=0, tiled=True
        ).astype(jnp.float32),
        lax.psum_scatter(
            g_ffn_out.astype(jnp.bfloat16), "dp", scatter_dimension=0, tiled=True
        ).astype(jnp.float32),
        lax.psum_scatter(
            g_self_bias.astype(jnp.bfloat16), "dp", scatter_dimension=0, tiled=True
        ).astype(jnp.float32),
        lax.psum_scatter(
            g_cross_bias.astype(jnp.bfloat16), "dp", scatter_dimension=0, tiled=True
        ).astype(jnp.float32),
        lax.psum_scatter(
            g_cv_bias.astype(jnp.bfloat16), "dp", scatter_dimension=0, tiled=True
        ).astype(jnp.float32),
        lax.psum_scatter(
            g_norm_gain.astype(jnp.bfloat16), "dp", scatter_dimension=0, tiled=True
        ).astype(jnp.float32),
        lax.psum_scatter(
            g_norm_bias.astype(jnp.bfloat16), "dp", scatter_dimension=0, tiled=True
        ).astype(jnp.float32),
        lax.psum_scatter(
            g_ffn_in_bias.astype(jnp.bfloat16), "dp", scatter_dimension=0, tiled=True
        ).astype(jnp.float32),
        lax.psum_scatter(
            g_ffn_out_bias.astype(jnp.bfloat16), "dp", scatter_dimension=0, tiled=True
        ).astype(jnp.float32),
    )
    (
        s_query,
        s_key,
        s_value,
        s_out,
        c_query,
        c_key,
        c_value,
        c_out,
        f_in,
        f_out,
        r_self_bias,
        r_cross_bias,
        r_cv_bias,
        r_gain,
        r_shift,
        r_in_bias,
        r_out_bias,
    ) = summed
    return (
        out_rows,
        input_grad,
        memory_grad,
        s_query,
        s_key,
        s_value,
        s_out,
        r_self_bias,
        c_query,
        c_key,
        c_value,
        c_out,
        r_cross_bias,
        r_cv_bias,
        r_gain,
        r_shift,
        f_in,
        r_in_bias,
        f_out,
        r_out_bias,
    )


def solution(mesh):
    nb, ndp = mesh.shape["blk"], mesh.shape["dp"]
    body = copied_work
    if (nb, ndp) == (8, 4):
        body = functools.partial(shared_work, nb, ndp)
    return jax.shard_map(
        body,
        mesh=mesh,
        in_specs=(
            P("dp", None, None),
            P("dp", "blk", None),
            P("dp"),
            P("dp", None, None),
            P(),
            P(),
            P(),
            P(),
            P(),
            P(),
            P(),
            P(),
            P(),
            P(),
            P(),
            P(),
            P(),
            P(),
            P(),
            P(),
            P(),
        ),
        out_specs=(
            P("dp", None, None),
            P("dp", None, None),
            P("dp", "blk", None),
            P("dp", None),
            P("dp", None),
            P("dp", None),
            P("dp", None),
            P("dp", None),
            P("dp", None),
            P("dp", None),
            P("dp", None),
            P("dp", None),
            P("dp", None),
            P("dp"),
            P("dp", None),
            P("dp", None),
            P("dp", None),
            P("dp"),
            P("dp", None),
            P("dp"),
        ),
        check_vma=False,
    )
```

```python
import functools

import jax
import jax.numpy as jnp
from jax import lax
from jax.experimental import pallas as pl
from jax.experimental.pallas import tpu as pltpu
from jax.sharding import PartitionSpec as P

D = 768
HEADS = 12
HEAD = 64
FF = 3072
TGT = 1024
ITEMS = 1


NEG = -1e30
EPS = 1e-05
SCALE = 0.125
BF = jnp.bfloat16
F32 = jnp.float32
MESH = pl.DeviceIdType.MESH
VMEM = pl.BlockSpec(memory_space=pltpu.VMEM)
SMEM = pl.BlockSpec(memory_space=pltpu.SMEM)
ANY = pl.BlockSpec(memory_space=pl.ANY)
LIMIT = 62 * 2**20


def dot(a, b):
    return jnp.dot(a, b, preferred_element_type=F32)


def dot_nt(a, b):
    return lax.dot_general(a, b, (((1,), (1,)), ((), ())), preferred_element_type=F32)


def dot_tn(a, b):
    return lax.dot_general(a, b, (((0,), (0,)), ((), ())), preferred_element_type=F32)


def lanes(shape):
    return lax.broadcasted_iota(jnp.int32, shape, 1)


def norm_parts(residual):
    centered = residual - jnp.mean(residual, axis=-1, keepdims=True)
    inv = lax.rsqrt(jnp.mean(centered * centered, axis=-1, keepdims=True) + EPS)
    return centered * inv, inv


def norm_grad(gradient, normed, inv, gain):
    scaled = gradient * gain
    return (
        scaled
        - jnp.mean(scaled, axis=-1, keepdims=True)
        - normed * jnp.mean(scaled * normed, axis=-1, keepdims=True)
    ) * inv


def gelu_parts(values):
    cdf = 0.5 * (1.0 + lax.erf(values * 0.7071067811865476))
    slope = cdf + values * (jnp.exp(-0.5 * values * values) * 0.3989422804014327)
    return values * cdf, slope


def col_sum(values):
    return jnp.sum(values, axis=0, keepdims=True)


class Gather:
    def __init__(self, buf, send, recv, live=None):
        self.buf, self.send, self.recv = buf, send, recv
        self.me = lax.axis_index("blk")
        self.y, self.z = self.me % 2, self.me // 2
        self.others = (1 + self.z % 2, (2 + 3 * self.z) % 5, 3 * (1 - self.z // 2))
        self.paired = self.z + 1 - 2 * (self.z % 2)
        self.live = live
        self.inner = self.z % 3 != 0
        self.end = self.z % 3 == 0
        self.half = buf.shape[1] // 2

    def _do(self, slot, act, also=None):
        wanted = [c for c in (also, self.live and self.live(slot)) if c is not None]
        if not wanted:
            act()
        else:
            pl.when(wanted[0] if len(wanted) == 1 else jnp.logical_and(*wanted))(act)

    def _copy(self, slot, z, y, sem, recv=None, part=None):
        ref = self.buf.at[slot]
        if part is not None:
            ref = ref.at[pl.ds(part * self.half, self.half), :]
        return pltpu.make_async_remote_copy(
            src_ref=ref,
            dst_ref=ref,
            send_sem=self.send.at[sem],
            recv_sem=self.recv.at[slot if recv is None else recv],
            device_id=(lax.axis_index("dp"), z * 2 + y),
            device_id_type=MESH,
        )

    def _along(self, z):
        return self._copy(self.me, z, self.y, z)

    def _across(self, z, part=None):
        return self._copy(2 * z + self.y, self.z, 1 - self.y, 4 + z, part=part)

    def _pass_on(self, z):
        return self._copy(2 * z + self.y, self.others[1], self.y, 8 + z)

    def _mirror(self, z):
        return 2 * z + 1 - self.y

    def _pass_mirror(self):
        return self._copy(self._mirror(self.z), self.paired, self.y, 12, 8, 1)

    def _arrived(self, slot, part=None, recv=None, also=None):
        copy = self._copy(slot, self.z, 1 - self.y, 0, recv, part)
        self._do(slot, lambda: copy.wait_recv(), also)

    def _by_pair(self, n, half, whole):
        if n == 2:
            whole()
        else:
            pl.when(self.end if n == 0 else self.inner)(half)
            pl.when(self.inner if n == 0 else self.end)(whole)

    def start(self):
        def act():
            self._across(self.z).start()
            for z in self.others[:2]:
                self._along(z).start()

        self._do(self.me, act)

    def _forward(self, inner, which):
        for n in which or (0, 1, 2):
            z = self.others[n]
            slot = 2 * z + self.y
            if n == 0:
                mirror = self._mirror(self.z)
                self._arrived(mirror)
                self._do(mirror, lambda: self._pass_mirror().start())
            self._arrived(slot)
            part = 0 if n == int(inner) else None
            self._do(slot, lambda: self._across(z, part).start())
            if inner and n != 1:
                self._do(slot, lambda: self._pass_on(z).start())

    def inner_forward(self, *which):
        pl.when(self.inner)(lambda: self._forward(True, which))

    def end_forward(self, *which):
        pl.when(self.end)(lambda: self._forward(False, which))

    def finish(self):
        for n, z in enumerate(self.others):
            slot = self._mirror(z)

            def half():
                self._arrived(slot, 0)
                self._arrived(slot, 1, 8)

            self._by_pair(n, half, lambda: self._arrived(slot))

        def act():
            self._across(self.z).wait_send()
            for z in self.others[:2]:
                self._along(z).wait_send()

        self._do(self.me, act)
        self._do(self._mirror(self.z), lambda: self._pass_mirror().wait_send())
        for n, z in enumerate(self.others):
            slot = 2 * z + self.y
            self._do(
                slot,
                lambda: self._by_pair(
                    n, lambda: self._across(z, 0).wait_send(), lambda: self._across(z).wait_send()
                ),
            )
            if n != 1:
                self._do(slot, lambda: self._pass_on(z).wait_send(), self.inner)


def greet(blk_peers, dp_peers):
    dp, blk = lax.axis_index("dp"), lax.axis_index("blk")
    barrier = pltpu.get_barrier_semaphore()
    for k in range(1, blk_peers):
        pl.semaphore_signal(
            barrier, inc=1, device_id=(dp, (blk + k) % blk_peers), device_id_type=MESH
        )
    for k in range(1, dp_peers):
        pl.semaphore_signal(
            barrier, inc=1, device_id=((dp + k) % dp_peers, blk), device_id_type=MESH
        )
    pl.semaphore_wait(barrier, max(blk_peers - 1, 0) + max(dp_peers - 1, 0))


def call(body, name, ins, outs, scratch=(), collective_id=None, in_specs=None, out_specs=None):
    extra = {} if collective_id is None else {"collective_id": collective_id, "has_side_effects": True}
    return pl.pallas_call(
        body,
        out_shape=[jax.ShapeDtypeStruct(s, k) for s, k in outs],
        in_specs=in_specs or [VMEM] * len(ins),
        out_specs=out_specs or [VMEM] * len(outs),
        scratch_shapes=list(scratch),
        compiler_params=pltpu.CompilerParams(vmem_limit_bytes=LIMIT, **extra),
        name=name,
    )(*ins)


def pair_cols(p):
    return pl.ds(pl.multiple_of(p * 128, 128), 128)


def pick(own, block):
    return jnp.where(own, block, jnp.zeros_like(block))


class Refs:
    def __init__(self, names, refs):
        for name, ref in zip(names, refs, strict=True):
            setattr(self, name, ref)


def two(i):
    return pl.ds(2 * i, 2)


def rows_of(ref, i):
    return ref[two(i)].reshape(256, ref.shape[-1])


def span(i, size=256):
    return pl.ds(pl.multiple_of(i * size, size), size)


def head_col(block, h):
    return jnp.sum(jnp.where(lanes(block.shape) == h, block, 0.0), -1, keepdims=True)


def triangle(size):
    return lanes((size, size)) <= lax.broadcasted_iota(jnp.int32, (size, size), 0)


LAYER_IN = (
    "length", "mem", "x", "cot", "sq", "sk", "sv", "so_w", "wq", "wk", "wv", "wo", "wi", "wf",
    "gain", "shift", "sbias", "cbias", "vecs",
)
LAYER_OUT = ("n3_out", "input_grad", "mem_grad", "ag_o", "ag_out_o", "vec_out", "h1_o", "e_o")
LAYER_SCRATCH = (
    "par", "bi", "v_x", "v_sq", "v_sk", "v_sv", "v_so", "v_wq", "v_wo", "v_q", "v_k", "v_v", "v_low",
    "inv", "attn_own", "r1_own", "query", "mem_all", "low_all", "n3_all", "so_all", "co_all",
    "stats_all", "trade_src", "right", "slab_self", "slab_cross", "slab_in", "slab_out", "got",
    "got_out", "ag", "ag_out", "vec", "vq", "vgot", "vall", "load_sem", "x_send", "x_recv",
    "d_send", "d_recv", "g_send", "g_recv", "v_send", "v_recv",
)
GAIN, SHIFT, SBIAS, CBIAS, VBIAS, FBIAS = 0, 3, 6, 9, 11, 12


def self_half(slot):
    m = slot // 2
    return (slot % 2 + m * (m - 2) * (m - 3) // 2) % 2


def is_late(slot):
    return jnp.logical_and(slot < 6, self_half(slot) == 1)


def is_early(slot):
    return jnp.logical_or(slot >= 6, self_half(slot) == 0)


def hidden_offsets(me):
    return [pl.multiple_of(D * ((me + t) % 4) + 128 * (2 * t + me // 4), 128) for t in range(3)]


def layer_part(nb, ndp, *refs):
    r = Refs(LAYER_IN + LAYER_OUT + LAYER_SCRATCH, refs)
    dp, me = lax.axis_index("dp"), lax.axis_index("blk")
    own_rows = TGT // nb
    quarter = D // ndp
    mrows = r.mem.shape[0]
    total_rows = nb * mrows
    wide = (TGT, D)
    free = iter(range(64))

    def load(src, dst):
        copy = pltpu.make_async_copy(src, dst, r.load_sem.at[next(free)])
        copy.start()
        return copy

    def par(row):
        return r.par[row : row + 1, :]

    gathers = [
        Gather(buf, r.g_send.at[n], r.g_recv.at[n])
        for n, buf in enumerate((r.mem_all, r.low_all, r.n3_all, r.so_all, r.co_all, r.stats_all))
    ]
    g_mem, g_low, g_n3, g_so, g_co, g_stats = gathers
    g_groups = [
        Gather(r.ag.at[g], r.g_send.at[6 + g], r.g_recv.at[6 + g], live)
        for g, live in enumerate((is_late, None, None))
    ]
    g_early = Gather(r.ag.at[0], r.g_send.at[6], r.g_recv.at[6], is_early)
    g_groups.append(
        Gather(
            r.ag_out, r.g_send.at[9], r.g_recv.at[9], lambda slot: (dp - slot + nb) % 4 < 3
        )
    )

    slabs = (r.slab_self, r.slab_cross, r.slab_in)

    def share(g, k):
        peer = (dp + k) % ndp
        if g == 3:
            src, dst = r.slab_out.at[(peer - me + nb) % 4], r.got_out.at[k]
        else:
            src = slabs[g].at[pl.ds(pl.multiple_of(peer * quarter, 16), quarter), :]
            dst = r.got.at[g, k]
        return pltpu.make_async_remote_copy(
            src_ref=src, dst_ref=dst, send_sem=r.d_send.at[g, k], recv_sem=r.d_recv.at[g, k],
            device_id=(peer, me), device_id_type=MESH,
        )

    def share_start(g):
        for k in range(1, ndp):
            share(g, k).start()

    def settle(g, gather=None):
        for k in range(1, ndp):
            share(g, k).wait()
        if g == 3:
            total = r.slab_out[(dp - me + nb) % 4].astype(F32)
            for k in range(1, ndp):
                total = total + r.got_out[k].astype(F32)
            r.ag_out[me] = total.astype(BF)
        else:
            total = slabs[g][pl.ds(pl.multiple_of(dp * quarter, 16), quarter), :].astype(F32)
            for k in range(1, ndp):
                total = total + r.got[g, k].astype(F32)
            r.ag[g, me] = total.astype(BF)
        (gather or g_groups[g]).start()

    c_mem = load(r.mem, r.mem_all.at[me])
    c_x = load(r.x, r.v_x)
    c_qkv = [load(s, d) for s, d in ((r.sq, r.v_sq), (r.sk, r.v_sk), (r.sv, r.v_sv))]
    c_more = [load(s, d) for s, d in ((r.so_w, r.v_so), (r.wq, r.v_wq), (r.wo, r.v_wo))]
    r.par[0:3, :] = r.gain[...].astype(F32)
    r.par[3:6, :] = r.shift[...].astype(F32)
    r.par[6:9, :] = r.sbias[...].astype(F32)
    r.par[9:11, :] = r.cbias[...].astype(F32)
    r.par[11:13, :] = r.vecs[0:2, :]
    for c in range(4):
        r.bi[:, D * c : D * c + D] = r.vecs[2 + c : 3 + c, :]
    greet(nb, ndp)
    c_mem.wait()
    g_mem.start()
    c_x.wait()
    for c in c_qkv:
        c.wait()

    @pl.loop(0, 4)
    def _(i):
        rows = span(i)
        block = r.v_x[rows, :]
        r.v_q[rows, :] = ((dot(block, r.v_sq[...]) + par(SBIAS)) * SCALE).astype(BF)
        r.v_k[rows, :] = dot(block, r.v_sk[...]).astype(BF)
        r.v_v[rows, :] = (dot(block, r.v_sv[...]) + par(SBIAS + 1)).astype(BF)

    own = span(me, own_rows)
    second_own = lanes((own_rows, 128)) >= HEAD
    reach = lanes((own_rows, TGT)) - lax.broadcasted_iota(jnp.int32, (own_rows, TGT), 0)
    seen = reach <= me * own_rows

    @pl.loop(0, 6)
    def _(p):
        cols = pair_cols(p)
        found = []
        for a in (0, 1):
            head = pick(second_own == bool(a), r.v_q[own, cols])
            s = jnp.where(seen, dot_nt(head, r.v_k[:, cols]), NEG)
            e = jnp.exp(s - jnp.max(s, -1, keepdims=True))
            found.append(dot(e.astype(BF), r.v_v[:, cols]) / jnp.sum(e, -1, keepdims=True))
        r.attn_own[:, cols] = jnp.where(second_own, found[1], found[0]).astype(BF)

    g_mem.inner_forward(0)
    g_mem.end_forward(0)
    for c in c_more:
        c.wait()
    r.r1_own[...] = r.v_x[own, :].astype(F32) + dot(r.attn_own[...], r.v_so[...]) + par(SBIAS + 2)

    r.inv[...] = jnp.zeros_like(r.inv)

    def pairs(first, last, between):
        def body(ebuf, esem):
            def keep(p):
                return pltpu.make_async_copy(ebuf.at[p % 2], r.e_o.at[p], esem.at[p % 2])

            size = 256

            def one_pair(p):
                slot = ebuf.at[p % 2]
                cols = pair_cols(p)
                for i in range(TGT // size):
                    rows = slice(i * size, (i + 1) * size)
                    place = i * (i + 1) // 2
                    second = lanes((size, 128)) >= HEAD
                    found, kept = [], r.inv[rows, :]
                    for a in (0, 1):
                        head = pick(second == bool(a), r.v_q[rows, cols])
                        last = (i + 1) * size
                        s = dot_nt(head, r.v_k[0:last, cols])
                        s_diag = jnp.where(triangle(size), s[:, i * size :], NEG)
                        s = jnp.concatenate([s[:, : i * size], s_diag], 1) if i else s_diag
                        e = jnp.exp(s - jnp.max(s, -1, keepdims=True))
                        total = jnp.sum(e, -1, keepdims=True)
                        e_low = e.astype(BF)
                        for j in range(i + 1):
                            slot[a, place + j] = e_low[:, j * size : (j + 1) * size]
                        part = dot(e_low, r.v_v[0:last, cols])
                        inverse = 1.0 / total
                        found.append(part * inverse)
                        kept = jnp.where(lanes((size, 128)) == 2 * p + a, inverse, kept)
                    r.v_low[rows, cols] = jnp.where(second, found[1], found[0]).astype(BF)
                    r.inv[rows, :] = kept
                keep(p).start()

            @pl.loop(first, last)
            def _(p):
                @pl.when(p >= first + 2)
                def _():
                    keep(p - 2).wait()

                one_pair(p)
                between(p)

            for p in range(max(first, last - 2), last):
                keep(p).wait()

        pl.run_scoped(
            body, pltpu.VMEM((2, 2, 10, 256, 256), BF), pltpu.SemaphoreType.DMA((2,))
        )

    def pass_memory(p):
        pl.when(p == 0)(lambda: g_mem.inner_forward(1, 2))
        pl.when(p == 1)(lambda: g_mem.end_forward(1))

    pairs(0, 2, pass_memory)

    def row_part(wi, wf, wk, wv, key, value, probs, slope, act, attn, cotv):
        c_kv = [load(r.wk, wk), load(r.wv, wv)]
        c_wi, c_cot, c_wf = load(r.wi, wi), load(r.cot.at[own, :], cotv), load(r.wf, wf)
        n1, inv1 = norm_parts(r.r1_own[...])
        h1 = n1 * par(GAIN) + par(SHIFT)
        query = ((dot(h1.astype(BF), r.v_wq[...]) + par(CBIAS)) * SCALE).astype(BF)
        for c in c_kv:
            c.wait()
        g_mem.end_forward(2)
        g_mem.finish()

        @pl.loop(0, total_rows // 256)
        def _(i):
            block = rows_of(r.mem_all, i)
            key[span(i), :] = dot(block, wk[...]).astype(BF)
            value[span(i), :] = (dot(block, wv[...]) + par(VBIAS)).astype(BF)

        live = lanes((own_rows, total_rows)) < r.length[0]
        stat = jnp.zeros((own_rows, 128), F32)
        for p in range(6):
            cols = slice(128 * p, 128 * p + 128)
            found = []
            for a in (0, 1):
                head = pick(second_own == bool(a), query[:, cols])
                s = jnp.where(live, dot_nt(head, key[:, cols]), NEG)
                top = jnp.max(s, -1, keepdims=True)
                e = jnp.exp(s - top)
                total = jnp.sum(e, -1, keepdims=True)
                pr = (e * (1.0 / total)).astype(BF)
                probs[2 * p + a] = pr
                found.append(dot(pr, value[:, cols]))
                stat = jnp.where(lanes((own_rows, 128)) == 2 * p + a, top + jnp.log(total), stat)
            attn[:, cols] = jnp.where(second_own, found[1], found[0])
        low = attn[...].astype(BF)
        r.low_all[me] = low
        g_low.start()
        r2 = h1 + dot(low, r.v_wo[...]) + par(CBIAS + 1)
        n2, inv2 = norm_parts(r2)
        h2 = n2 * par(GAIN + 1) + par(SHIFT + 1)
        h2_low = h2.astype(BF)
        c_wi.wait()

        @pl.loop(0, FF // 512)
        def _(c):
            cols = span(c, 512)
            up, down = gelu_parts(dot(h2_low, wi[:, cols]) + r.bi[:, cols])
            act[:, cols] = up.astype(BF)
            slope[:, cols] = down

        c_wf.wait()
        r3 = h2 + dot(act[...], wf[...]) + par(FBIAS)
        n3, inv3 = norm_parts(r3)
        r.n3_all[me] = n3.astype(BF)
        r.stats_all[me] = jnp.where(lanes((own_rows, 128)) == HEADS, inv3, stat).T[0:16, :]
        g_stats.start()
        g_n3.start()
        g_low.inner_forward(0)
        c_cot.wait()
        g3 = cotv[...].astype(F32)
        vec = r.vec
        vec[...] = jnp.zeros_like(vec)
        vec[2:3, :] = col_sum(g3 * n3)
        vec[5:6, :] = col_sum(g3)
        grad_r3 = norm_grad(g3, n3, inv3, par(GAIN + 2))
        z_low = grad_r3.astype(BF)
        vec[9:10, :] = col_sum(z_low.astype(F32))

        @pl.loop(0, FF // 512)
        def _(c):
            cols = span(c, 512)
            act[:, cols] = (dot_nt(z_low, wf[cols, :]) * slope[:, cols]).astype(BF)

        grad_h2 = grad_r3 + dot_nt(act[...], wi[...])
        vec[1:2, :] = col_sum(grad_h2 * n2)
        vec[4:5, :] = col_sum(grad_h2)
        grad_r2 = norm_grad(grad_h2, n2, inv2, par(GAIN + 1))
        co_low = grad_r2.astype(BF)
        g_low.inner_forward(1, 2)
        g_low.end_forward(0)
        r.co_all[me] = co_low
        vec[8:9, :] = col_sum(co_low.astype(F32))
        oc = dot_nt(co_low, r.v_wo[...]).astype(BF)
        product = oc.astype(F32) * attn[...]
        for p in range(6):
            cols = slice(128 * p, 128 * p + 128)
            found = []
            for a in (0, 1):
                sel = second_own == bool(a)
                delta = jnp.sum(jnp.where(sel, product[:, cols], 0.0), -1, keepdims=True)
                dprob = dot_nt(pick(sel, oc[:, cols]), value[:, cols])
                ds = (probs[2 * p + a].astype(F32) * (dprob - delta)).astype(BF)
                found.append(dot(ds, key[:, cols]))
            r.trade_src[2, :, cols] = (
                jnp.where(second_own, found[1], found[0]).astype(BF).astype(F32) * SCALE
            ).astype(BF)
        cq_low = r.trade_src[2]
        vec[7:8, :] = col_sum(cq_low.astype(F32))
        grad_h1 = grad_r2 + dot_nt(cq_low, r.v_wq[...])
        vec[0:1, :] = col_sum(grad_h1 * n1)
        vec[3:4, :] = col_sum(grad_h1)
        so_low = norm_grad(grad_h1, n1, inv1, par(GAIN)).astype(BF)
        r.so_all[me] = so_low
        vec[6:7, :] = col_sum(so_low.astype(F32))
        g_so.start()

    memory_block = pltpu.VMEM((total_rows, D), BF)
    square = pltpu.VMEM((D, D), BF)
    pl.run_scoped(
        row_part,
        pltpu.VMEM((D, FF), BF), pltpu.VMEM((FF, D), BF), square, square, memory_block, memory_block,
        pltpu.VMEM((HEADS, own_rows, total_rows), BF),
        pltpu.VMEM((own_rows, FF), F32), pltpu.VMEM((own_rows, FF), BF),
        pltpu.VMEM((own_rows, D), F32), pltpu.VMEM((own_rows, D), BF),
    )

    def pass_rows(p):
        @pl.when(p == 2)
        def _():
            g_low.end_forward(1, 2)
            g_n3.inner_forward(0)

        @pl.when(p == 3)
        def _():
            g_n3.inner_forward(1, 2)
            g_n3.end_forward(0)

        @pl.when(p == 4)
        def _():
            g_co.start()
            g_so.inner_forward(0)
            g_n3.end_forward(1)

        @pl.when(p == 5)
        def _():
            g_so.inner_forward(1, 2)
            g_n3.end_forward(2)
            g_so.end_forward(0)

    pairs(2, 6, pass_rows)

    def hidden_scope(h2_low, z_low, act, slope, wi_own, wf_own):
        offsets = hidden_offsets(me)
        c_cot = load(r.cot, z_low)
        own_w = [
            load(r.wi.at[:, pl.ds(off, 128)], wi_own.at[:, pl.ds(128 * t, 128)])
            for t, off in enumerate(offsets)
        ] + [
            load(r.wf.at[pl.ds(off, 128), :], wf_own.at[pl.ds(128 * t, 128), :])
            for t, off in enumerate(offsets)
        ]

        def hidden_forward(r1v, h1v):
            @pl.loop(0, 4)
            def _(i):
                rows = span(i)
                resid = (
                    r.v_x[rows, :].astype(F32) + dot(r.v_low[rows, :], r.v_so[...]) + par(SBIAS + 2)
                )
                n1, _ = norm_parts(resid)
                h1 = n1 * par(GAIN) + par(SHIFT)
                r1v[rows, :] = h1
                h1v[rows, :] = h1.astype(BF)
                r.query[rows, :] = (
                    (dot(h1.astype(BF), r.v_wq[...]) + par(CBIAS)) * SCALE
                ).astype(BF)

            c_h1 = load(h1v, r.h1_o)
            g_stats.inner_forward()
            g_co.inner_forward(0)
            g_so.end_forward(1)
            g_low.finish()

            @pl.loop(0, 4)
            def _(i):
                r2 = r1v[span(i), :] + dot(rows_of(r.low_all, i), r.v_wo[...]) + par(CBIAS + 1)
                n2, _ = norm_parts(r2)
                h2_low[two(i)] = (
                    (n2 * par(GAIN + 1) + par(SHIFT + 1)).astype(BF).reshape(2, 128, D)
                )

            g_co.inner_forward(1, 2)
            g_so.end_forward(2)
            c_h1.wait()

        pl.run_scoped(hidden_forward, pltpu.VMEM(wide, F32), pltpu.VMEM(wide, BF))
        for c in own_w:
            c.wait()
        bias = jnp.concatenate([r.bi[:, pl.ds(off, 128)] for off in offsets], axis=1)

        @pl.loop(0, 4)
        def _(i):
            up, down = gelu_parts(dot(rows_of(h2_low, i), wi_own[...]) + bias)
            act[span(i), :] = up.astype(BF)
            slope[span(i), :] = down

        def hidden_backward():
            g_stats.end_forward()
            g_co.end_forward(0)
            g_stats.finish()
            g_n3.finish()
            c_cot.wait()

            @pl.loop(0, 4)
            def _(i):
                normed = rows_of(r.n3_all, i).astype(F32)
                tile = r.stats_all[two(i)]
                inv3 = jnp.concatenate(
                    [
                        jnp.concatenate([tile[b], jnp.zeros((112, 128), F32)], 0).T[:, HEADS : HEADS + 1]
                        for b in (0, 1)
                    ],
                    0,
                )
                z_low[span(i), :] = norm_grad(
                    z_low[span(i), :].astype(F32), normed, inv3, par(GAIN + 2)
                ).astype(BF)

            g_co.end_forward(1)
            for t in range(3):
                r.slab_out[t] = dot_tn(act[:, 128 * t : 128 * t + 128], z_low[...]).astype(BF)
            r.slab_out[3] = jnp.zeros_like(r.slab_out[3])
            share_start(3)

            @pl.loop(0, 4)
            def _(i):
                rows = span(i)
                act[rows, :] = (dot_nt(z_low[rows, :], wf_own[...]) * slope[rows, :]).astype(BF)

            g_co.end_forward(2)
            total = col_sum(act[...].astype(F32))
            for t in range(3):
                lane = pl.ds(pl.multiple_of(128 * (2 * t + me // 4), 128), 128)
                which = lax.broadcasted_iota(jnp.int32, (4, 128), 0) == (me + t) % 4
                r.vec[13:17, lane] = jnp.where(which, total[:, 128 * t : 128 * t + 128], 0.0)

            @pl.loop(0, 3)
            def _(c):
                cols = span(c)
                r.slab_in[cols, :] = dot_tn(
                    h2_low[:, :, cols].reshape(TGT, 256), act[...]
                ).astype(BF)

            share_start(2)

        hidden_backward()

    pl.run_scoped(
        hidden_scope,
        pltpu.VMEM((nb, own_rows, D), BF), pltpu.VMEM(wide, BF),
        pltpu.VMEM((TGT, 384), BF), pltpu.VMEM((TGT, 384), F32),
        pltpu.VMEM((D, 384), BF), pltpu.VMEM((384, D), BF),
    )
    c_n3 = load(r.n3_all, r.n3_out)

    def trade(k, target, origin):
        source = (target // 2 + 2) % 3
        return pltpu.make_async_remote_copy(
            src_ref=r.trade_src.at[source, :, pl.ds(pl.multiple_of((target % 2) * 384, 128), 384)],
            dst_ref=r.right.at[origin],
            send_sem=r.x_send.at[k], recv_sem=r.x_recv.at[k],
            device_id=(dp, target), device_id_type=MESH,
        )

    def inner_slot(slot):
        return jnp.logical_and(slot >= 2, slot < 6)

    def trade_start(wanted):
        for k in range(1, nb):
            target = (me + k) % nb
            pl.when(wanted(target))(lambda: trade(k, target, me).start())

    def vshare(k):
        peer = (dp + k) % ndp
        return pltpu.make_async_remote_copy(
            src_ref=r.vq.at[peer], dst_ref=r.vgot.at[k],
            send_sem=r.v_send.at[0, k], recv_sem=r.v_recv.at[0, k],
            device_id=(peer, me), device_id_type=MESH,
        )

    def vspread(k, origin):
        return pltpu.make_async_remote_copy(
            src_ref=r.vall.at[origin], dst_ref=r.vall.at[origin],
            send_sem=r.v_send.at[1, k], recv_sem=r.v_recv.at[1, k],
            device_id=(dp, (me + k) % nb), device_id_type=MESH,
        )

    def vectors_start():
        vec = r.vec[...]
        r.vq[...] = jnp.zeros_like(r.vq)
        for q in range(ndp):
            r.vq[q, 0:16, 0:quarter] = vec[0:16, quarter * q : quarter * q + quarter]
            for s in range(ndp):
                r.vq[q, 16 + s : 17 + s, 0:quarter] = vec[
                    13 + q : 14 + q, quarter * s : quarter * s + quarter
                ]
        for k in range(1, ndp):
            vshare(k).start()

    def vectors_spread():
        for k in range(1, ndp):
            vshare(k).wait()
        total = r.vq[dp]
        for k in range(1, ndp):
            total = total + r.vgot[k]
        r.vall[me] = total
        for k in range(1, nb):
            vspread(k, me).start()

    def self_part(go, gs, rights, dkt, dvt, qt, gt, left, ebuf, esem):
        size = 256

        def fetch(p):
            return pltpu.make_async_copy(r.e_o.at[p], ebuf.at[p % 2], esem.at[p % 2])

        fetch(0).start()
        g_so.finish()

        @pl.loop(0, 4)
        def _(i):
            go[span(i), :] = dot_nt(rows_of(r.so_all, i), r.v_so[...]).astype(BF)

        def one_pair(p):
            @pl.when(p + 1 < 6)
            def _():
                fetch(p + 1).start()

            cols = pair_cols(p)
            second = lanes((size, 128)) >= HEAD
            deltas = []
            for i in range(TGT // size):
                rows = slice(i * size, (i + 1) * size)
                invs = [head_col(r.inv[rows, :], 2 * p + a) for a in (0, 1)]
                scaled = go[rows, cols].astype(F32) * jnp.where(second, invs[1], invs[0])
                gs[rows, :] = scaled.astype(BF)
                product = scaled * r.v_low[rows, cols].astype(F32)
                deltas.append(
                    [
                        jnp.sum(jnp.where(second == bool(a), product, 0.0), -1, keepdims=True)
                        for a in (0, 1)
                    ]
                )
            qt[...] = r.v_q[:, cols].T
            gt[...] = gs[...].T
            fetch(p).wait()
            slot = ebuf.at[p % 2]
            for i in reversed(range(TGT // size)):
                rows = slice(i * size, (i + 1) * size)
                found = []
                for a in (0, 1):
                    own_g = pick(second == bool(a), gs[rows, :])
                    head = slice(HEAD * a, HEAD * a + HEAD)
                    last = (i + 1) * size
                    place = i * (i + 1) // 2
                    e = jnp.concatenate([slot[a, place + j] for j in range(i + 1)], 1)
                    dprob = dot_nt(own_g, r.v_v[0:last, cols])
                    ds = (e.astype(F32) * (dprob - deltas[i][a])).astype(BF)
                    found.append(dot(ds, r.v_k[0:last, cols]))
                    part_k = dot(qt[head, rows], ds)
                    part_v = dot(gt[head, rows], e)
                    if last == TGT:
                        dkt[head, :] = part_k
                        dvt[head, :] = part_v
                    else:
                        dkt[head, 0:last] += part_k
                        dvt[head, 0:last] += part_v
                rights[0, rows, cols] = (
                    jnp.where(second, found[1], found[0]).astype(BF).astype(F32) * SCALE
                ).astype(BF)
            rights[1, :, cols] = dkt[...].T.astype(BF)
            rights[2, :, cols] = dvt[...].T.astype(BF)
            r.vec[10:11, cols] = col_sum(rights[0, :, cols].astype(F32)) * (1.0 / nb)
            r.vec[11:12, cols] = col_sum(rights[2, :, cols].astype(F32)) * (1.0 / nb)

        left_sem = r.load_sem.at[next(free)]
        square_block = pltpu.VMEM((mrows, D), BF)

        def memory_part(wk, wv, key, value, oc, lse_t, delta_t):
            c_kv = [load(r.wk, wk), load(r.wv, wv)]

            @pl.when(inner_slot(me))
            def _():
                pltpu.make_async_copy(r.mem_all, left, left_sem).start()

            for b in range(nb):
                rows = pl.ds(own_rows * b, own_rows)

                @pl.when(me % 7 == 0)
                def _():
                    pltpu.make_async_copy(r.h1_o.at[rows, :], left.at[b], left_sem).start()

            @pl.when(me % 5 == 1)
            def _():
                pltpu.make_async_copy(r.low_all, left, left_sem).start()

            g_co.finish()
            member = jnp.where(
                lax.broadcasted_iota(jnp.int32, (16, D), 1) // HEAD
                == lax.broadcasted_iota(jnp.int32, (16, D), 0),
                1.0,
                0.0,
            ).astype(BF)
            for i in range(4):
                rows = slice(256 * i, 256 * i + 256)
                grad_out = dot_nt(rows_of(r.co_all, i), r.v_wo[...]).astype(BF)
                oc[rows, :] = grad_out
                product = grad_out.astype(F32) * rows_of(r.low_all, i).astype(F32)
                big = product.astype(BF)
                small = (product - big.astype(F32)).astype(BF)
                delta_t[:, rows] = dot_nt(member, big) + dot_nt(member, small)
                lse_t[:, rows] = jnp.concatenate([r.stats_all[2 * i], r.stats_all[2 * i + 1]], 1)
            for c in c_kv:
                c.wait()
            key[...] = dot(r.mem_all[me], wk[...]).astype(BF)
            value[...] = (dot(r.mem_all[me], wv[...]) + par(VBIAS)).astype(BF)
            position = me * mrows + lax.broadcasted_iota(jnp.int32, (mrows, 1), 0)
            live = position < r.length[0]
            second = lanes((mrows, 128)) >= HEAD

            @pl.loop(0, 6)
            def _(p):
                cols = pair_cols(p)
                found_k, found_v = [], []
                for a in (0, 1):
                    sel = second == bool(a)
                    s = dot_nt(pick(sel, key[:, cols]), r.query[:, cols])
                    pr = jnp.where(live, jnp.exp(s - lse_t[pl.ds(2 * p + a, 1), :]), 0.0)
                    dprob = dot_nt(pick(sel, value[:, cols]), oc[:, cols])
                    ds = (pr * (dprob - delta_t[pl.ds(2 * p + a, 1), :])).astype(BF)
                    found_k.append(dot(ds, r.query[:, cols]))
                    found_v.append(dot(pr.astype(BF), oc[:, cols]))
                r.trade_src[0, :, cols] = jnp.where(second, found_k[1], found_k[0]).astype(BF)
                r.trade_src[1, :, cols] = jnp.where(second, found_v[1], found_v[0]).astype(BF)

            trade_start(inner_slot)
            dk, dv = r.trade_src[0], r.trade_src[1]
            r.mem_grad[...] = (dot_nt(dk, wk[...]) + dot_nt(dv, wv[...])).astype(BF)
            r.vec[12:13, :] = col_sum(dv.astype(F32))

        half = pl.ds(pl.multiple_of((me % 2) * 384, 128), 384)

        def form_cross():
            @pl.when(me % 5 != 1)
            def _():
                r.right[me] = r.trade_src[(me // 2 + 2) % 3, :, half]
                for k in range(1, nb):
                    trade(k, (me + k) % nb, (me + nb - k) % nb).wait_recv()

            @pl.when(me % 5 == 1)
            def _():
                r.right[...] = r.co_all[:, :, half]

            pltpu.make_async_copy(r.mem_all, left, left_sem).wait()

            @pl.loop(0, 3)
            def _(c):
                r.slab_cross[span(c), :] = dot_tn(
                    left[:, :, span(c)].reshape(TGT, 256), r.right[...].reshape(TGT, 384)
                ).astype(BF)

            share_start(1)

        self_cols = pl.ds(pl.multiple_of(self_half(me) * 384, 128), 384)

        def self_slab_qkv():
            @pl.loop(0, 3)
            def _(c):
                r.slab_self[span(c), :] = dot_tn(
                    r.v_x[:, span(c)], rights[me // 2, :, self_cols]
                ).astype(BF)

        def self_early():
            @pl.when(jnp.logical_and(is_early(me), me < 6))
            def _():
                self_slab_qkv()

            @pl.when(me >= 6)
            def _():
                @pl.loop(0, 3)
                def _(c):
                    r.slab_self[span(c), :] = dot_tn(
                        r.v_low[:, span(c)], r.so_all[:, :, self_cols].reshape(TGT, 384)
                    ).astype(BF)

            pl.when(is_early(me))(lambda: share_start(0))

        def run_memory():
            pl.run_scoped(
                memory_part,
                square, square, square_block, square_block,
                pltpu.VMEM(wide, BF), pltpu.VMEM((16, TGT), F32), pltpu.VMEM((16, TGT), F32),
            )

        @pl.loop(0, 6)
        def _(p):
            pl.when(p == 1)(lambda: trade_start(lambda slot: slot % 7 == 0))

            @pl.when(p == 2)
            def _():
                settle(3)
                run_memory()
                settle(2)
                g_groups[3].inner_forward(0)

            @pl.when(p == 3)
            def _():
                self_early()
                g_groups[3].inner_forward(1, 2)
                g_groups[3].end_forward(0)

            @pl.when(p == 4)
            def _():
                pl.when(is_early(me))(lambda: settle(0, g_early))
                g_groups[3].end_forward(1, 2)
                g_groups[2].inner_forward(0)

            @pl.when(p == 5)
            def _():
                form_cross()
                g_groups[2].inner_forward(1, 2)
                g_groups[2].end_forward(0)

            one_pair(p)

        @pl.when(is_late(me))
        def _():
            self_slab_qkv()
            share_start(0)

        vectors_start()
        g_early.inner_forward(0)
        settle(1)
        g_groups[2].end_forward(1, 2)
        pl.when(is_late(me))(lambda: settle(0))

        @pl.loop(0, 4)
        def _(i):
            rows = span(i)
            sq, sk, sv = rights[0, rows, :], rights[1, rows, :], rights[2, rows, :]
            go[rows, :] = (
                rows_of(r.so_all, i).astype(F32)
                + dot_nt(sq, r.v_sq[...])
                + dot_nt(sk, r.v_sk[...])
                + dot_nt(sv, r.v_sv[...])
            ).astype(BF)

            @pl.when(i == 0)
            def _():
                g_early.inner_forward(1, 2)
                g_early.end_forward(0)

            pl.when(i == 2)(lambda: g_groups[1].inner_forward(0))

        c_grad = load(go, r.input_grad)
        vectors_spread()
        g_groups[1].inner_forward(1, 2)
        g_early.end_forward(1, 2)
        g_groups[1].end_forward(0)
        g_groups[0].inner_forward()
        g_groups[1].end_forward(1, 2)
        g_groups[0].end_forward()
        c_grad.wait()


    pl.run_scoped(
        self_part,
        pltpu.VMEM(wide, BF), pltpu.VMEM((TGT, 128), BF), pltpu.VMEM((3,) + wide, BF),
        pltpu.VMEM((128, TGT), F32), pltpu.VMEM((128, TGT), F32),
        pltpu.VMEM((128, TGT), BF), pltpu.VMEM((128, TGT), BF), pltpu.VMEM((nb, own_rows, D), BF),
        pltpu.VMEM((2, 2, 10, 256, 256), BF), pltpu.SemaphoreType.DMA((2,)),
    )

    outs = []

    def collect(g):
        g_groups[g].finish()
        outs.append(load(r.ag_out, r.ag_out_o) if g == 3 else load(r.ag.at[g], r.ag_o.at[g]))

    collect(3)
    collect(2)
    g_early.finish()
    collect(1)
    collect(0)
    for k in range(1, nb):
        vspread(k, (me + nb - k) % nb).wait_recv()
    total = r.vall[0]
    for b in range(1, nb):
        total = total + r.vall[b]
    r.vec_out[...] = total
    for k in range(1, nb):
        target = (me + k) % nb
        pl.when(target % 5 != 1)(lambda: trade(k, target, me).wait_send())
        vspread(k, me).wait_send()
    for c in outs:
        c.wait()
    c_n3.wait()


FINISH_IN = ("n3", "grad_in", "mem_in", "ag", "ag_out", "vec", "gain", "shift")
FINISH_OUT = (
    "out", "input_grad", "mem_grad", "s_q", "s_k", "s_v", "s_o", "c_k", "c_v", "c_q", "c_o", "f_in",
    "f_out", "self_bias", "cross_bias", "cv", "d_gain", "d_shift", "in_bias", "out_bias",
)
FINISH_SCRATCH = ("v_ag", "v_ag_out", "v_n3", "v_f", "v_in", "v_out", "v_y", "v_grad", "v_mem", "v_small", "v_wide", "sem")


def finish_part(nb, ndp, *refs):
    r = Refs(FINISH_IN + FINISH_OUT + FINISH_SCRATCH, refs)
    dp = lax.axis_index("dp")
    quarter = D // ndp
    free = iter(range(40))

    def move(src, dst):
        copy = pltpu.make_async_copy(src, dst, r.sem.at[next(free)])
        copy.start()
        return copy

    c_ag = [move(r.ag.at[g], r.v_ag.at[g]) for g in range(3)]
    c_out, c_n3 = move(r.ag_out, r.v_ag_out), move(r.n3, r.v_n3)
    c_grad, c_mem = move(r.grad_in, r.v_grad), move(r.mem_in, r.v_mem)
    done = []
    vec = r.vec
    smalls = (
        (r.self_bias, (10, 11, 6)), (r.cross_bias, (7, 8)), (r.d_gain, (0, 1, 2)),
        (r.d_shift, (3, 4, 5)), (r.cv, (12,)), (r.out_bias, (9,)),
    )
    for m, (ref, rows) in enumerate(smalls):
        for n, row in enumerate(rows):
            r.v_small[m, n : n + 1, :] = vec[row : row + 1, 0:quarter]
        done.append(move(r.v_small.at[m, pl.ds(0, len(rows))], ref))
    for n in range(ndp):
        r.v_wide[:, quarter * n : quarter * n + quarter] = vec[16 + n : 17 + n, 0:quarter]
    done.append(move(r.v_wide, r.in_bias))
    for g, dsts in ((0, (r.s_q, r.s_k, r.s_v, r.s_o)), (1, (r.c_q, r.c_k, r.c_v, r.c_o))):
        c_ag[g].wait()

        @pl.loop(0, quarter // 48)
        def _(i):
            rows = span(i, 48)
            for b in range(nb):
                h = self_half(b) if g == 0 else b % 2
                n = 4 * g + (b // 2 if g == 0 else (0, 3, 1, 1, 2, 2, 3, 0)[b])
                r.v_f[n, rows, 384 * h : 384 * h + 384] = r.v_ag[g, b, rows, :].astype(F32)

        for n, dst in enumerate(dsts):
            done.append(move(r.v_f.at[4 * g + n], dst))
    c_grad.wait()
    c_mem.wait()
    done += [move(r.v_grad, r.input_grad), move(r.v_mem, r.mem_grad)]
    c_ag[2].wait()

    @pl.loop(0, quarter // 48)
    def _(i):
        rows = span(i, 48)
        for b in range(nb):
            for t in range(3):
                col = D * ((b + t) % 4) + 128 * (2 * t + b // 4)
                r.v_in[rows, col : col + 128] = r.v_ag[
                    2, b, rows, 128 * t : 128 * t + 128
                ].astype(F32)

    done.append(move(r.v_in, r.f_in))
    c_out.wait()

    @pl.loop(0, nb)
    def _(b):
        t = (dp - b + nb) % 4

        @pl.when(t < 3)
        def _():
            place = pl.ds(pl.multiple_of(128 * (2 * t + b // 4), 128), 128)
            r.v_out[place, :] = r.v_ag_out[b].astype(F32)

    done.append(move(r.v_out, r.f_out))
    c_n3.wait()
    gain, shift = r.gain[...].astype(F32)[2:3, :], r.shift[...].astype(F32)[2:3, :]

    @pl.loop(0, nb)
    def _(b):
        r.v_y[b] = (r.v_n3[b].astype(F32) * gain + shift).astype(BF)

    done.append(move(r.v_y, r.out))
    for c in done:
        c.wait()


def shared_work(
    nb, ndp,
    inputs, memory, lengths, cotangent, self_query, self_key, self_value, self_out, self_bias,
    cross_query, cross_key, cross_value, cross_out, cross_bias, cross_value_bias,
    norm_gain, norm_bias, ffn_in, ffn_in_bias, ffn_out, ffn_out_bias,
):
    own_rows = TGT // nb
    x, mem, cot = inputs[0], memory[0], cotangent[0]
    mrows = mem.shape[0]
    quarter = D // ndp
    gain, shift = norm_gain.T, norm_bias.T
    vecs = (
        jnp.concatenate([cross_value_bias, ffn_out_bias, ffn_in_bias]).reshape(6, D).astype(F32)
    )
    wide, own, square, block = (TGT, D), (own_rows, D), (D, D), (nb, own_rows, D)
    dma = pltpu.SemaphoreType.DMA
    vm = pltpu.VMEM
    n3, grad_in, mem_grad, ag, ag_out, vec, _, _ = call(
        functools.partial(layer_part, nb, ndp),
        "layer_part",
        (lengths, mem, x, cot, self_query, self_key, self_value, self_out, cross_query, cross_key,
         cross_value, cross_out, ffn_in, ffn_out, gain, shift, self_bias.T, cross_bias.T, vecs),
        [(block, BF), (wide, BF), ((mrows, D), BF), ((3, nb, quarter, 384), BF), ((nb, 128, D), BF),
         ((24, 256), F32), (wide, BF), ((6, 2, 10, 256, 256), BF)],
        [vm((16, D), F32), vm((1, FF), F32), vm(wide, BF)]
        + [vm(square, BF)] * 6
        + [vm(wide, BF)] * 4
        + [vm((TGT, 128), F32), vm(own, BF), vm(own, F32), vm(wide, BF), vm((nb, mrows, D), BF)]
        + [vm(block, BF)] * 4
        + [vm((nb, 16, own_rows), F32), vm((3, own_rows, D), BF), vm((nb, own_rows, 384), BF)]
        + [vm((D, 384), BF)] * 3
        + [vm((4, 128, D), BF), vm((3, ndp, quarter, 384), BF), vm((ndp, 128, D), BF),
           vm((3, nb, quarter, 384), BF), vm((nb, 128, D), BF),
           vm((24, D), F32), vm((ndp, 24, 256), F32), vm((ndp, 24, 256), F32), vm((nb, 24, 256), F32)]
        + [dma((64,)), dma((nb,)), dma((nb,)), dma((4, ndp)), dma((4, ndp)), dma((10, 16)),
           dma((10, 16)), dma((2, nb)), dma((2, nb))],
        collective_id=0,
        in_specs=[SMEM] + [ANY] * 13 + [VMEM] * 5,
        out_specs=[ANY] * 2 + [VMEM] + [ANY] * 2 + [VMEM] + [ANY] * 2,
    )
    weight = ((quarter, D), F32)
    (
        out, input_grad, memory_grad, s_q, s_k, s_v, s_o, c_k, c_v, c_q, c_o, f_in, f_out,
        g_self_bias, g_cross_bias, g_cv, g_gain, g_shift, g_in_bias, g_out_bias,
    ) = call(
        functools.partial(finish_part, nb, ndp),
        "finish_part",
        (n3, grad_in, mem_grad, ag, ag_out, vec, gain, shift),
        [(block, BF), (wide, BF), ((mrows, D), BF)]
        + [weight] * 8
        + [((quarter, FF), F32), ((FF // ndp, D), F32), ((3, quarter), F32), ((2, quarter), F32),
           ((1, quarter), F32), ((3, quarter), F32), ((3, quarter), F32), ((1, FF // ndp), F32),
           ((1, quarter), F32)],
        [vm((3, nb, quarter, 384), BF), vm((nb, 128, D), BF), vm(block, BF),
         vm((8, quarter, D), F32), vm((quarter, FF), F32), vm((FF // ndp, D), F32), vm(block, BF),
         vm(wide, BF), vm((mrows, D), BF), vm((6, 8, quarter), F32), vm((1, FF // ndp), F32),
         dma((40,))],
        in_specs=[ANY] * 5 + [VMEM] * 3,
        out_specs=[ANY] * 20,
    )
    return (
        out.reshape(1, TGT, D), input_grad[None], memory_grad[None],
        s_q, s_k, s_v, s_o, g_self_bias.T, c_q, c_k, c_v, c_o, g_cross_bias.T, g_cv.reshape(quarter),
        g_gain.T, g_shift.T, f_in, g_in_bias.reshape(FF // ndp), f_out, g_out_bias.reshape(quarter),
    )


def merged(array, axis, join):
    gathered = jax.tree.map(
        lambda a, kind: lax.all_gather(a.astype(kind), axis), array, (jnp.bfloat16, jnp.bfloat16)
    )

    def take(source):
        return jax.tree.map(
            lambda a, own: lax.dynamic_index_in_dim(a, source, 0, False).astype(own.dtype),
            gathered,
            array,
        )

    return lax.fori_loop(
        1, lax.axis_size(axis), lambda source, state: join(state, take(source)), take(0)
    )


def layer_norm(residual, gain_col, shift_col):
    average = jnp.mean(residual, axis=-1, keepdims=True)
    centered = residual - average
    variance = jnp.mean(centered * centered, axis=-1, keepdims=True)
    return centered * lax.rsqrt(variance + EPS) * gain_col + shift_col


def exact_gelu(values):
    return jax.nn.gelu(values, approximate=False)


def project(left_side, weight):
    return jnp.dot(left_side, weight, preferred_element_type=jnp.float32)


def project_back(gradient, weight):
    return lax.dot_general(
        gradient, weight, (((1,), (1,)), ((), ())), preferred_element_type=jnp.float32
    )


def weight_grad(left_side, gradient):
    return lax.dot_general(
        left_side, gradient, (((0,), (0,)), ((), ())), preferred_element_type=jnp.float32
    )


def column_sum(gradient):
    return jnp.sum(gradient.astype(jnp.float32), axis=0)


def split_heads(values):
    return values.reshape(values.shape[:-1] + (HEADS, HEAD))


def combine_totals(earlier, latter):
    top_a, sum_a = earlier
    top_b, sum_b = latter
    top_score = jnp.maximum(top_a, top_b)
    return (top_score, sum_a * jnp.exp(top_a - top_score) + sum_b * jnp.exp(top_b - top_score))


def self_scores(query_rows, key_rows, row_start, block_rows):
    scores = jnp.einsum("qhe,khe->hqk", query_rows, key_rows, preferred_element_type=jnp.float32)
    row_pos = row_start + jnp.arange(block_rows)[:, None]
    col_pos = jnp.arange(key_rows.shape[0])[None, :]
    return jnp.where((col_pos <= row_pos)[None], scores, NEG)


def copied_work(
    inputs,
    memory,
    lengths,
    cotangent,
    self_query,
    self_key,
    self_value,
    self_out,
    self_bias,
    cross_query,
    cross_key,
    cross_value,
    cross_out,
    cross_bias,
    cross_value_bias,
    norm_gain,
    norm_bias,
    ffn_in,
    ffn_in_bias,
    ffn_out,
    ffn_out_bias,
):
    all_rows = ITEMS * TGT
    block_rows = min(512, TGT)
    mem_rows = memory.shape[1]
    self_bias_f = self_bias.astype(jnp.float32)
    cross_bias_f = cross_bias.astype(jnp.float32)
    gains = norm_gain.astype(jnp.float32)
    shifts = norm_bias.astype(jnp.float32)
    flat_in = inputs.reshape(all_rows, D)
    query_self = split_heads(
        ((project(flat_in, self_query) + self_bias_f[:, 0]) * SCALE)
        .astype(jnp.bfloat16)
        .reshape(ITEMS, TGT, D)
    )
    key_self = split_heads(project(flat_in, self_key).astype(jnp.bfloat16).reshape(ITEMS, TGT, D))
    value_self = split_heads(
        (project(flat_in, self_value) + self_bias_f[:, 1])
        .astype(jnp.bfloat16)
        .reshape(ITEMS, TGT, D)
    )
    item_index = 0
    attn_blocks = []
    lse_blocks = []
    for row_start in range(0, TGT, block_rows):
        row_end = row_start + block_rows
        scores = self_scores(
            query_self[item_index, row_start:row_end],
            key_self[item_index, :row_end],
            row_start,
            block_rows,
        )
        top_score = jnp.max(scores, axis=-1, keepdims=True)
        log_total = top_score + jnp.log(
            jnp.sum(jnp.exp(scores - top_score), axis=-1, keepdims=True)
        )
        probs_low = jnp.exp(scores - log_total).astype(jnp.bfloat16)
        attn_blocks.append(
            jnp.einsum(
                "hqk,khe->qhe",
                probs_low,
                value_self[item_index, :row_end],
                preferred_element_type=jnp.float32,
            )
        )
        lse_blocks.append(log_total)
    attn_items = [jnp.concatenate(attn_blocks, axis=0)]
    lse_self = [lse_blocks]
    self_attn = jnp.stack(attn_items, axis=0)
    self_low = self_attn.astype(jnp.bfloat16).reshape(all_rows, D)
    resid_one = flat_in.astype(jnp.float32) + project(self_low, self_out) + self_bias_f[:, 2]
    hidden_one, norm1_back = jax.vjp(layer_norm, resid_one, gains[:, 0], shifts[:, 0])
    hidden_low = hidden_one.astype(jnp.bfloat16)
    query_cross = split_heads(
        ((project(hidden_low, cross_query) + cross_bias_f[:, 0]) * SCALE)
        .astype(jnp.bfloat16)
        .reshape(ITEMS, TGT, D)
    )
    flat_mem = memory.reshape(ITEMS * mem_rows, D)
    key_cross = split_heads(
        project(flat_mem, cross_key).astype(jnp.bfloat16).reshape(ITEMS, mem_rows, D)
    )
    value_cross = split_heads(
        (project(flat_mem, cross_value) + cross_value_bias.astype(jnp.float32))
        .astype(jnp.bfloat16)
        .reshape(ITEMS, mem_rows, D)
    )
    position = lax.axis_index("blk") * mem_rows + jnp.arange(mem_rows)
    live_mask = position[None, :] < lengths[:, None]

    def cross_scores():
        raw_scores = jnp.einsum(
            "bqhe,bkhe->bhqk", query_cross, key_cross, preferred_element_type=jnp.float32
        )
        return jnp.where(live_mask[:, None, None, :], raw_scores, NEG)

    scores = cross_scores()
    top_local = jnp.max(scores, axis=-1)
    sum_local = jnp.sum(jnp.exp(scores - top_local[..., None]), axis=-1)
    top_all, sum_all = merged((top_local, sum_local), "blk", combine_totals)
    cross_lse = top_all + jnp.log(sum_all)
    probs_low = jnp.exp(scores - cross_lse[..., None]).astype(jnp.bfloat16)
    share_out = jnp.einsum(
        "bhqk,bkhe->bqhe", probs_low, value_cross, preferred_element_type=jnp.float32
    ).reshape(all_rows, D)
    cot_flat = cotangent.reshape(all_rows, D)
    attn_rows = lax.psum(share_out, "blk")
    cross_low = attn_rows.astype(jnp.bfloat16)
    resid_two = hidden_one + project(cross_low, cross_out) + cross_bias_f[:, 1]
    hidden_two, norm2_back = jax.vjp(layer_norm, resid_two, gains[:, 1], shifts[:, 1])
    second_low = hidden_two.astype(jnp.bfloat16)
    pre_act = project(second_low, ffn_in) + ffn_in_bias.astype(jnp.float32)
    activated, gelu_back = jax.vjp(exact_gelu, pre_act)
    act_low = activated.astype(jnp.bfloat16)
    resid_three = hidden_two + project(act_low, ffn_out) + ffn_out_bias.astype(jnp.float32)
    result, norm3_back = jax.vjp(layer_norm, resid_three, gains[:, 2], shifts[:, 2])
    result_low = result.astype(jnp.bfloat16)
    grad_r3, grad_gain3, grad_shift3 = norm3_back(cot_flat.astype(jnp.float32))
    z_low = grad_r3.astype(jnp.bfloat16)
    g_ffn_out = weight_grad(act_low, z_low)
    g_ffn_out_bias = column_sum(z_low)
    (grad_pre,) = gelu_back(project_back(z_low, ffn_out))
    pre_low = grad_pre.astype(jnp.bfloat16)
    g_ffn_in = weight_grad(second_low, pre_low)
    g_ffn_in_bias = column_sum(pre_low)
    grad_h2 = grad_r3 + project_back(pre_low, ffn_in)
    grad_r2, grad_gain2, grad_shift2 = norm2_back(grad_h2)
    co_low = grad_r2.astype(jnp.bfloat16)
    g_cross_out = weight_grad(cross_low, co_low)
    g_co_bias = column_sum(co_low)
    oc_low = project_back(co_low, cross_out).astype(jnp.bfloat16)
    out_rows = result_low.reshape(ITEMS, TGT, D)
    grad_oc = split_heads(oc_low.reshape(ITEMS, TGT, D))
    cross_delta = jnp.transpose(
        jnp.sum(
            grad_oc.astype(jnp.float32) * split_heads(attn_rows.reshape(ITEMS, TGT, D)), axis=-1
        ),
        (0, 2, 1),
    )
    scores = cross_scores()
    prob_full = jnp.exp(scores - cross_lse[..., None])
    grad_probs = jnp.einsum(
        "bqhe,bkhe->bhqk", grad_oc, value_cross, preferred_element_type=jnp.float32
    )
    grad_scores = (prob_full * (grad_probs - cross_delta[..., None])).astype(jnp.bfloat16)
    query_share = jnp.einsum(
        "bhqk,bkhe->bqhe", grad_scores, key_cross, preferred_element_type=jnp.float32
    ).reshape(all_rows, D)
    key_low = (
        jnp.einsum("bhqk,bqhe->bkhe", grad_scores, query_cross, preferred_element_type=jnp.float32)
        .astype(jnp.bfloat16)
        .reshape(ITEMS * mem_rows, D)
    )
    value_low = (
        jnp.einsum(
            "bhqk,bqhe->bkhe",
            prob_full.astype(jnp.bfloat16),
            grad_oc,
            preferred_element_type=jnp.float32,
        )
        .astype(jnp.bfloat16)
        .reshape(ITEMS * mem_rows, D)
    )
    grad_cq = lax.psum(query_share, "blk")
    cq_low = (grad_cq * SCALE).astype(jnp.bfloat16)
    g_cross_query = weight_grad(hidden_one.astype(jnp.bfloat16), cq_low)
    g_cq_bias = column_sum(cq_low)
    grad_h1_rows = grad_r2 + project_back(cq_low, cross_query)
    g_cross_key_dev = weight_grad(flat_mem, key_low)
    g_cross_value_dev = weight_grad(flat_mem, value_low)
    g_cv_bias_dev = column_sum(value_low)
    memory_grad = (
        (project_back(key_low, cross_key) + project_back(value_low, cross_value))
        .astype(jnp.bfloat16)
        .reshape(ITEMS, mem_rows, D)
    )
    g_cross_key, g_cross_value, g_cv_bias = lax.psum(
        (g_cross_key_dev, g_cross_value_dev, g_cv_bias_dev), "blk"
    )
    grad_r1, grad_gain1, grad_shift1 = norm1_back(grad_h1_rows)
    so_low = grad_r1.astype(jnp.bfloat16)
    g_self_out = weight_grad(self_low, so_low)
    g_so_bias = column_sum(so_low)
    grad_os = split_heads(
        project_back(so_low, self_out).astype(jnp.bfloat16).reshape(ITEMS, TGT, D)
    )
    item_index = 0
    key_grad = jnp.zeros((TGT, HEADS, HEAD), jnp.float32)
    value_grad = jnp.zeros((TGT, HEADS, HEAD), jnp.float32)
    query_blocks = []
    for row_start in range(0, TGT, block_rows):
        row_end = row_start + block_rows
        query_rows = query_self[item_index, row_start:row_end]
        key_rows = key_self[item_index, :row_end]
        scores = self_scores(query_rows, key_rows, row_start, block_rows)
        prob_full = jnp.exp(scores - lse_self[item_index][row_start // block_rows])
        grad_out = grad_os[item_index, row_start:row_end]
        row_delta = jnp.transpose(
            jnp.sum(
                grad_out.astype(jnp.float32) * self_attn[item_index, row_start:row_end], axis=-1
            )
        )
        grad_probs = jnp.einsum(
            "qhe,khe->hqk",
            grad_out,
            value_self[item_index, :row_end],
            preferred_element_type=jnp.float32,
        )
        grad_scores = (prob_full * (grad_probs - row_delta[:, :, None])).astype(jnp.bfloat16)
        query_blocks.append(
            jnp.einsum("hqk,khe->qhe", grad_scores, key_rows, preferred_element_type=jnp.float32)
        )
        key_grad = key_grad.at[:row_end].add(
            jnp.einsum("hqk,qhe->khe", grad_scores, query_rows, preferred_element_type=jnp.float32)
        )
        value_grad = value_grad.at[:row_end].add(
            jnp.einsum(
                "hqk,qhe->khe",
                prob_full.astype(jnp.bfloat16),
                grad_out,
                preferred_element_type=jnp.float32,
            )
        )
    query_items = [jnp.concatenate(query_blocks, axis=0)]
    key_items = [key_grad]
    value_items = [value_grad]
    sq_low = (jnp.stack(query_items, 0).astype(jnp.bfloat16) * jnp.bfloat16(SCALE)).reshape(
        all_rows, D
    )
    sk_low = jnp.stack(key_items, 0).astype(jnp.bfloat16).reshape(all_rows, D)
    sv_low = jnp.stack(value_items, 0).astype(jnp.bfloat16).reshape(all_rows, D)
    g_self_query = weight_grad(flat_in, sq_low)
    g_self_key = weight_grad(flat_in, sk_low)
    g_self_value = weight_grad(flat_in, sv_low)
    g_sq_bias = column_sum(sq_low)
    g_sv_bias = column_sum(sv_low)
    input_grad = (
        (
            grad_r1
            + project_back(sq_low, self_query)
            + project_back(sk_low, self_key)
            + project_back(sv_low, self_value)
        )
        .astype(jnp.bfloat16)
        .reshape(ITEMS, TGT, D)
    )
    g_self_bias = jnp.stack([g_sq_bias, g_sv_bias, g_so_bias], axis=1)
    g_cross_bias = jnp.stack([g_cq_bias, g_co_bias], axis=1)
    g_norm_gain = jnp.stack([grad_gain1, grad_gain2, grad_gain3], axis=1)
    g_norm_bias = jnp.stack([grad_shift1, grad_shift2, grad_shift3], axis=1)
    summed = (
        lax.psum_scatter(
            g_self_query.astype(jnp.bfloat16), "dp", scatter_dimension=0, tiled=True
        ).astype(jnp.float32),
        lax.psum_scatter(
            g_self_key.astype(jnp.bfloat16), "dp", scatter_dimension=0, tiled=True
        ).astype(jnp.float32),
        lax.psum_scatter(
            g_self_value.astype(jnp.bfloat16), "dp", scatter_dimension=0, tiled=True
        ).astype(jnp.float32),
        lax.psum_scatter(
            g_self_out.astype(jnp.bfloat16), "dp", scatter_dimension=0, tiled=True
        ).astype(jnp.float32),
        lax.psum_scatter(
            g_cross_query.astype(jnp.bfloat16), "dp", scatter_dimension=0, tiled=True
        ).astype(jnp.float32),
        lax.psum_scatter(
            g_cross_key.astype(jnp.bfloat16), "dp", scatter_dimension=0, tiled=True
        ).astype(jnp.float32),
        lax.psum_scatter(
            g_cross_value.astype(jnp.bfloat16), "dp", scatter_dimension=0, tiled=True
        ).astype(jnp.float32),
        lax.psum_scatter(
            g_cross_out.astype(jnp.bfloat16), "dp", scatter_dimension=0, tiled=True
        ).astype(jnp.float32),
        lax.psum_scatter(
            g_ffn_in.astype(jnp.bfloat16), "dp", scatter_dimension=0, tiled=True
        ).astype(jnp.float32),
        lax.psum_scatter(
            g_ffn_out.astype(jnp.bfloat16), "dp", scatter_dimension=0, tiled=True
        ).astype(jnp.float32),
        lax.psum_scatter(
            g_self_bias.astype(jnp.bfloat16), "dp", scatter_dimension=0, tiled=True
        ).astype(jnp.float32),
        lax.psum_scatter(
            g_cross_bias.astype(jnp.bfloat16), "dp", scatter_dimension=0, tiled=True
        ).astype(jnp.float32),
        lax.psum_scatter(
            g_cv_bias.astype(jnp.bfloat16), "dp", scatter_dimension=0, tiled=True
        ).astype(jnp.float32),
        lax.psum_scatter(
            g_norm_gain.astype(jnp.bfloat16), "dp", scatter_dimension=0, tiled=True
        ).astype(jnp.float32),
        lax.psum_scatter(
            g_norm_bias.astype(jnp.bfloat16), "dp", scatter_dimension=0, tiled=True
        ).astype(jnp.float32),
        lax.psum_scatter(
            g_ffn_in_bias.astype(jnp.bfloat16), "dp", scatter_dimension=0, tiled=True
        ).astype(jnp.float32),
        lax.psum_scatter(
            g_ffn_out_bias.astype(jnp.bfloat16), "dp", scatter_dimension=0, tiled=True
        ).astype(jnp.float32),
    )
    (
        s_query,
        s_key,
        s_value,
        s_out,
        c_query,
        c_key,
        c_value,
        c_out,
        f_in,
        f_out,
        r_self_bias,
        r_cross_bias,
        r_cv_bias,
        r_gain,
        r_shift,
        r_in_bias,
        r_out_bias,
    ) = summed
    return (
        out_rows,
        input_grad,
        memory_grad,
        s_query,
        s_key,
        s_value,
        s_out,
        r_self_bias,
        c_query,
        c_key,
        c_value,
        c_out,
        r_cross_bias,
        r_cv_bias,
        r_gain,
        r_shift,
        f_in,
        r_in_bias,
        f_out,
        r_out_bias,
    )


def solution(mesh):
    nb, ndp = mesh.shape["blk"], mesh.shape["dp"]
    body = copied_work
    if (nb, ndp) == (8, 4):
        body = functools.partial(shared_work, nb, ndp)
    return jax.shard_map(
        body,
        mesh=mesh,
        in_specs=(
            P("dp", None, None),
            P("dp", "blk", None),
            P("dp"),
            P("dp", None, None),
            P(),
            P(),
            P(),
            P(),
            P(),
            P(),
            P(),
            P(),
            P(),
            P(),
            P(),
            P(),
            P(),
            P(),
            P(),
            P(),
            P(),
        ),
        out_specs=(
            P("dp", None, None),
            P("dp", None, None),
            P("dp", "blk", None),
            P("dp", None),
            P("dp", None),
            P("dp", None),
            P("dp", None),
            P("dp", None),
            P("dp", None),
            P("dp", None),
            P("dp", None),
            P("dp", None),
            P("dp", None),
            P("dp"),
            P("dp", None),
            P("dp", None),
            P("dp", None),
            P("dp"),
            P("dp", None),
            P("dp"),
        ),
        check_vma=False,
    )
```

```python
import functools

import jax
import jax.numpy as jnp
from jax import lax
from jax.experimental import pallas as pl
from jax.experimental.pallas import tpu as pltpu
from jax.sharding import PartitionSpec as P

D = 768
HEADS = 12
HEAD = 64
FF = 3072
TGT = 1024
ITEMS = 1


NEG = -1e30
EPS = 1e-05
SCALE = 0.125
BF = jnp.bfloat16
F32 = jnp.float32
MESH = pl.DeviceIdType.MESH
VMEM = pl.BlockSpec(memory_space=pltpu.VMEM)
SMEM = pl.BlockSpec(memory_space=pltpu.SMEM)
ANY = pl.BlockSpec(memory_space=pl.ANY)
LIMIT = 62 * 2**20


def dot(a, b):
    return jnp.dot(a, b, preferred_element_type=F32)


def dot_nt(a, b):
    return lax.dot_general(a, b, (((1,), (1,)), ((), ())), preferred_element_type=F32)


def dot_tn(a, b):
    return lax.dot_general(a, b, (((0,), (0,)), ((), ())), preferred_element_type=F32)


def lanes(shape):
    return lax.broadcasted_iota(jnp.int32, shape, 1)


def norm_parts(residual):
    centered = residual - jnp.mean(residual, axis=-1, keepdims=True)
    inv = lax.rsqrt(jnp.mean(centered * centered, axis=-1, keepdims=True) + EPS)
    return centered * inv, inv


def norm_grad(gradient, normed, inv, gain):
    scaled = gradient * gain
    return (
        scaled
        - jnp.mean(scaled, axis=-1, keepdims=True)
        - normed * jnp.mean(scaled * normed, axis=-1, keepdims=True)
    ) * inv


def gelu_parts(values):
    cdf = 0.5 * (1.0 + lax.erf(values * 0.7071067811865476))
    slope = cdf + values * (jnp.exp(-0.5 * values * values) * 0.3989422804014327)
    return values * cdf, slope


def col_sum(values):
    return jnp.sum(values, axis=0, keepdims=True)


class Gather:
    def __init__(self, buf, send, recv, live=None):
        self.buf, self.send, self.recv = buf, send, recv
        self.me = lax.axis_index("blk")
        self.y, self.z = self.me % 2, self.me // 2
        self.others = (1 + self.z % 2, (2 + 3 * self.z) % 5, 3 * (1 - self.z // 2))
        self.paired = self.z + 1 - 2 * (self.z % 2)
        self.live = live
        self.inner = self.z % 3 != 0
        self.end = self.z % 3 == 0
        self.half = buf.shape[1] // 2

    def _do(self, slot, act, also=None):
        wanted = [c for c in (also, self.live and self.live(slot)) if c is not None]
        if not wanted:
            act()
        else:
            pl.when(wanted[0] if len(wanted) == 1 else jnp.logical_and(*wanted))(act)

    def _copy(self, slot, z, y, sem, recv=None, part=None):
        ref = self.buf.at[slot]
        if part is not None:
            ref = ref.at[pl.ds(part * self.half, self.half), :]
        return pltpu.make_async_remote_copy(
            src_ref=ref,
            dst_ref=ref,
            send_sem=self.send.at[sem],
            recv_sem=self.recv.at[slot if recv is None else recv],
            device_id=(lax.axis_index("dp"), z * 2 + y),
            device_id_type=MESH,
        )

    def _along(self, z):
        return self._copy(self.me, z, self.y, z)

    def _across(self, z, part=None):
        return self._copy(2 * z + self.y, self.z, 1 - self.y, 4 + z, part=part)

    def _pass_on(self, z):
        return self._copy(2 * z + self.y, self.others[1], self.y, 8 + z)

    def _mirror(self, z):
        return 2 * z + 1 - self.y

    def _pass_mirror(self):
        return self._copy(self._mirror(self.z), self.paired, self.y, 12, 8, 1)

    def _arrived(self, slot, part=None, recv=None, also=None):
        copy = self._copy(slot, self.z, 1 - self.y, 0, recv, part)
        self._do(slot, lambda: copy.wait_recv(), also)

    def _by_pair(self, n, half, whole):
        if n == 2:
            whole()
        else:
            pl.when(self.end if n == 0 else self.inner)(half)
            pl.when(self.inner if n == 0 else self.end)(whole)

    def start(self):
        def act():
            self._across(self.z).start()
            for z in self.others[:2]:
                self._along(z).start()

        self._do(self.me, act)

    def _forward(self, inner, which):
        for n in which or (0, 1, 2):
            z = self.others[n]
            slot = 2 * z + self.y
            if n == 0:
                mirror = self._mirror(self.z)
                self._arrived(mirror)
                self._do(mirror, lambda: self._pass_mirror().start())
            self._arrived(slot)
            part = 0 if n == int(inner) else None
            self._do(slot, lambda: self._across(z, part).start())
            if inner and n != 1:
                self._do(slot, lambda: self._pass_on(z).start())

    def inner_forward(self, *which):
        pl.when(self.inner)(lambda: self._forward(True, which))

    def end_forward(self, *which):
        pl.when(self.end)(lambda: self._forward(False, which))

    def finish(self):
        for n, z in enumerate(self.others):
            slot = self._mirror(z)

            def half():
                self._arrived(slot, 0)
                self._arrived(slot, 1, 8)

            self._by_pair(n, half, lambda: self._arrived(slot))

        def act():
            self._across(self.z).wait_send()
            for z in self.others[:2]:
                self._along(z).wait_send()

        self._do(self.me, act)
        self._do(self._mirror(self.z), lambda: self._pass_mirror().wait_send())
        for n, z in enumerate(self.others):
            slot = 2 * z + self.y
            self._do(
                slot,
                lambda: self._by_pair(
                    n, lambda: self._across(z, 0).wait_send(), lambda: self._across(z).wait_send()
                ),
            )
            if n != 1:
                self._do(slot, lambda: self._pass_on(z).wait_send(), self.inner)


def greet(blk_peers, dp_peers):
    dp, blk = lax.axis_index("dp"), lax.axis_index("blk")
    barrier = pltpu.get_barrier_semaphore()
    for k in range(1, blk_peers):
        pl.semaphore_signal(
            barrier, inc=1, device_id=(dp, (blk + k) % blk_peers), device_id_type=MESH
        )
    for k in range(1, dp_peers):
        pl.semaphore_signal(
            barrier, inc=1, device_id=((dp + k) % dp_peers, blk), device_id_type=MESH
        )
    pl.semaphore_wait(barrier, max(blk_peers - 1, 0) + max(dp_peers - 1, 0))


def call(body, name, ins, outs, scratch=(), collective_id=None, in_specs=None, out_specs=None):
    extra = {} if collective_id is None else {"collective_id": collective_id, "has_side_effects": True}
    return pl.pallas_call(
        body,
        out_shape=[jax.ShapeDtypeStruct(s, k) for s, k in outs],
        in_specs=in_specs or [VMEM] * len(ins),
        out_specs=out_specs or [VMEM] * len(outs),
        scratch_shapes=list(scratch),
        compiler_params=pltpu.CompilerParams(vmem_limit_bytes=LIMIT, **extra),
        name=name,
    )(*ins)


def pair_cols(p):
    return pl.ds(pl.multiple_of(p * 128, 128), 128)


def pick(own, block):
    return jnp.where(own, block, jnp.zeros_like(block))


class Refs:
    def __init__(self, names, refs):
        for name, ref in zip(names, refs, strict=True):
            setattr(self, name, ref)


def two(i):
    return pl.ds(2 * i, 2)


def rows_of(ref, i):
    return ref[two(i)].reshape(256, ref.shape[-1])


def span(i, size=256):
    return pl.ds(pl.multiple_of(i * size, size), size)


def head_col(block, h):
    return jnp.sum(jnp.where(lanes(block.shape) == h, block, 0.0), -1, keepdims=True)


def triangle(size):
    return lanes((size, size)) <= lax.broadcasted_iota(jnp.int32, (size, size), 0)


LAYER_IN = (
    "length", "mem", "x", "cot", "sq", "sk", "sv", "so_w", "wq", "wk", "wv", "wo", "wi", "wf",
    "gain", "shift", "sbias", "cbias", "vecs",
)
LAYER_OUT = ("n3_out", "input_grad", "mem_grad", "ag_o", "ag_c_o", "ag_out_o", "self_e_o", "self_l_o", "vec_out", "h1_o", "e_o")
LAYER_SCRATCH = (
    "par", "bi", "v_x", "v_sq", "v_sk", "v_sv", "v_so", "v_wq", "v_wo", "v_q", "v_k", "v_v", "v_low",
    "inv", "attn_own", "r1_own", "query", "mem_all", "low_all", "n3_all", "so_all", "co_all",
    "stats_all", "trade_src", "right", "core_e", "core_l", "chip_e", "chip_l",
    "slab_cross", "slab_in", "slab_out", "got", "got_c", "got_out", "ag_c", "ag", "ag_out", "vec", "vq", "vgot", "vall", "load_sem", "x_send", "x_recv",
    "d_send", "d_recv", "g_send", "g_recv", "v_send", "v_recv", "s_send", "s_recv",
)
GAIN, SHIFT, SBIAS, CBIAS, VBIAS, FBIAS = 0, 3, 6, 9, 11, 12


def hidden_offsets(me):
    return [pl.multiple_of(D * ((me + t) % 4) + 128 * (2 * t + me // 4), 128) for t in range(3)]


def layer_part(nb, ndp, *refs):
    r = Refs(LAYER_IN + LAYER_OUT + LAYER_SCRATCH, refs)
    dp, me = lax.axis_index("dp"), lax.axis_index("blk")
    own_rows = TGT // nb
    quarter = D // ndp
    mrows = r.mem.shape[0]
    total_rows = nb * mrows
    wide = (TGT, D)
    free = iter(range(64))

    def load(src, dst):
        copy = pltpu.make_async_copy(src, dst, r.load_sem.at[next(free)])
        copy.start()
        return copy

    def par(row):
        return r.par[row : row + 1, :]

    gathers = [
        Gather(buf, r.g_send.at[n], r.g_recv.at[n])
        for n, buf in enumerate((r.mem_all, r.low_all, r.n3_all, r.so_all, r.co_all, r.stats_all))
    ]
    g_mem, g_low, g_n3, g_so, g_co, g_stats = gathers
    g_groups = [
        Gather(buf, r.g_send.at[6 + g], r.g_recv.at[6 + g])
        for g, buf in enumerate((r.ag_c.at[0], r.ag_c.at[1], r.ag))
    ]
    g_groups.append(
        Gather(
            r.ag_out, r.g_send.at[9], r.g_recv.at[9], lambda slot: (dp - slot + nb) % 4 < 3
        )
    )

    def slab_rows(g, owner):
        if g == 2:
            return r.slab_in.at[pl.ds(pl.multiple_of(owner * quarter, 16), quarter), :]
        start = pl.multiple_of(owner * quarter + g * (quarter // 2), 16)
        return r.slab_cross.at[pl.ds(start, quarter // 2), :]

    def share(g, k):
        peer = (dp + k) % ndp
        if g == 3:
            src, dst = r.slab_out.at[(peer - me + nb) % 4], r.got_out.at[k]
        else:
            src, dst = slab_rows(g, peer), (r.got if g == 2 else r.got_c.at[g]).at[k]
        return pltpu.make_async_remote_copy(
            src_ref=src, dst_ref=dst, send_sem=r.d_send.at[g, k], recv_sem=r.d_recv.at[g, k],
            device_id=(peer, me), device_id_type=MESH,
        )

    def share_start(g):
        for k in range(1, ndp):
            share(g, k).start()

    def settle(g):
        for k in range(1, ndp):
            share(g, k).wait()
        if g == 3:
            total = r.slab_out[(dp - me + nb) % 4].astype(F32)
            for k in range(1, ndp):
                total = total + r.got_out[k].astype(F32)
            r.ag_out[me] = total.astype(BF)
        else:
            got, out = (r.got, r.ag) if g == 2 else (r.got_c.at[g], r.ag_c.at[g])
            total = slab_rows(g, dp)[...].astype(F32)
            for k in range(1, ndp):
                total = total + got[k].astype(F32)
            out[me] = total.astype(BF)
        g_groups[g].start()

    core, chip = dp % 2, dp // 2
    parts = [[None, r.core_e, r.chip_e], [None, r.core_l, r.chip_l]]

    def to_core(n, other):
        slab, core_got, _ = parts[n]
        start = pl.multiple_of((2 * other + 1 - core) * quarter, 16)
        return pltpu.make_async_remote_copy(
            src_ref=slab.at[pl.ds(start, quarter), :], dst_ref=core_got.at[other],
            send_sem=r.s_send.at[n, other], recv_sem=r.s_recv.at[n, other],
            device_id=(2 * chip + 1 - core, me), device_id_type=MESH,
        )

    def to_chip(n):
        _, core_got, chip_got = parts[n]
        return pltpu.make_async_remote_copy(
            src_ref=core_got.at[1 - chip], dst_ref=chip_got,
            send_sem=r.s_send.at[n, 2], recv_sem=r.s_recv.at[n, 2],
            device_id=(2 - 2 * chip + core, me), device_id_type=MESH,
        )

    def self_start(n):
        for other in (0, 1):
            to_core(n, other).start()

    def self_middle(n):
        slab, core_got, _ = parts[n]
        for other in (0, 1):
            to_core(n, other).wait()
        for other in (0, 1):
            @pl.loop(0, quarter // 48)
            def _(i):
                start = pl.multiple_of((2 * other + core) * quarter, 16)
                mine = slab[pl.ds(start + span(i, 48).start, 48), :].astype(F32)
                rows = span(i, 48)
                core_got[other, rows, :] = (mine + core_got[other, rows, :].astype(F32)).astype(BF)

        to_chip(n).start()

    def self_end(n):
        _, core_got, chip_got = parts[n]
        to_chip(n).wait()

        @pl.loop(0, quarter // 48)
        def _(i):
            rows = span(i, 48)
            chip_got[rows, :] = (
                chip_got[rows, :].astype(F32) + core_got[chip, rows, :].astype(F32)
            ).astype(BF)

    c_mem = load(r.mem, r.mem_all.at[me])
    c_x = load(r.x, r.v_x)
    c_qkv = [load(s, d) for s, d in ((r.sq, r.v_sq), (r.sk, r.v_sk), (r.sv, r.v_sv))]
    c_more = [load(s, d) for s, d in ((r.so_w, r.v_so), (r.wq, r.v_wq), (r.wo, r.v_wo))]
    r.par[0:3, :] = r.gain[...].astype(F32)
    r.par[3:6, :] = r.shift[...].astype(F32)
    r.par[6:9, :] = r.sbias[...].astype(F32)
    r.par[9:11, :] = r.cbias[...].astype(F32)
    r.par[11:13, :] = r.vecs[0:2, :]
    for c in range(4):
        r.bi[:, D * c : D * c + D] = r.vecs[2 + c : 3 + c, :]
    greet(nb, ndp)
    c_mem.wait()
    g_mem.start()
    c_x.wait()
    for c in c_qkv:
        c.wait()

    @pl.loop(0, 4)
    def _(i):
        rows = span(i)
        block = r.v_x[rows, :]
        r.v_q[rows, :] = ((dot(block, r.v_sq[...]) + par(SBIAS)) * SCALE).astype(BF)
        r.v_k[rows, :] = dot(block, r.v_sk[...]).astype(BF)
        r.v_v[rows, :] = (dot(block, r.v_sv[...]) + par(SBIAS + 1)).astype(BF)

    own = span(me, own_rows)
    second_own = lanes((own_rows, 128)) >= HEAD
    reach = lanes((own_rows, TGT)) - lax.broadcasted_iota(jnp.int32, (own_rows, TGT), 0)
    seen = reach <= me * own_rows

    @pl.loop(0, 6)
    def _(p):
        cols = pair_cols(p)
        found = []
        for a in (0, 1):
            head = pick(second_own == bool(a), r.v_q[own, cols])
            s = jnp.where(seen, dot_nt(head, r.v_k[:, cols]), NEG)
            e = jnp.exp(s - jnp.max(s, -1, keepdims=True))
            found.append(dot(e.astype(BF), r.v_v[:, cols]) / jnp.sum(e, -1, keepdims=True))
        r.attn_own[:, cols] = jnp.where(second_own, found[1], found[0]).astype(BF)

    g_mem.inner_forward(0)
    g_mem.end_forward(0)
    for c in c_more:
        c.wait()
    r.r1_own[...] = r.v_x[own, :].astype(F32) + dot(r.attn_own[...], r.v_so[...]) + par(SBIAS + 2)

    r.inv[...] = jnp.zeros_like(r.inv)

    def pairs(first, last, between):
        def body(ebuf, esem):
            def keep(p):
                return pltpu.make_async_copy(ebuf.at[p % 2], r.e_o.at[p], esem.at[p % 2])

            size = 256

            def one_pair(p):
                slot = ebuf.at[p % 2]
                cols = pair_cols(p)
                for i in range(TGT // size):
                    rows = slice(i * size, (i + 1) * size)
                    place = i * (i + 1) // 2
                    second = lanes((size, 128)) >= HEAD
                    found, kept = [], r.inv[rows, :]
                    for a in (0, 1):
                        head = pick(second == bool(a), r.v_q[rows, cols])
                        last = (i + 1) * size
                        s = dot_nt(head, r.v_k[0:last, cols])
                        s_diag = jnp.where(triangle(size), s[:, i * size :], NEG)
                        s = jnp.concatenate([s[:, : i * size], s_diag], 1) if i else s_diag
                        e = jnp.exp(s - jnp.max(s, -1, keepdims=True))
                        total = jnp.sum(e, -1, keepdims=True)
                        e_low = e.astype(BF)
                        for j in range(i + 1):
                            slot[a, place + j] = e_low[:, j * size : (j + 1) * size]
                        part = dot(e_low, r.v_v[0:last, cols])
                        inverse = 1.0 / total
                        found.append(part * inverse)
                        kept = jnp.where(lanes((size, 128)) == 2 * p + a, inverse, kept)
                    r.v_low[rows, cols] = jnp.where(second, found[1], found[0]).astype(BF)
                    r.inv[rows, :] = kept
                keep(p).start()

            @pl.loop(first, last)
            def _(p):
                @pl.when(p >= first + 2)
                def _():
                    keep(p - 2).wait()

                one_pair(p)
                between(p)

            for p in range(max(first, last - 2), last):
                keep(p).wait()

        pl.run_scoped(
            body, pltpu.VMEM((2, 2, 10, 256, 256), BF), pltpu.SemaphoreType.DMA((2,))
        )

    def pass_memory(p):
        pl.when(p == 0)(lambda: g_mem.inner_forward(1, 2))
        pl.when(p == 1)(lambda: g_mem.end_forward(1))

    pairs(0, 2, pass_memory)

    def row_part(wi, wf, wk, wv, key, value, probs, slope, act, attn, cotv):
        c_kv = [load(r.wk, wk), load(r.wv, wv)]
        c_wi, c_cot, c_wf = load(r.wi, wi), load(r.cot.at[own, :], cotv), load(r.wf, wf)
        n1, inv1 = norm_parts(r.r1_own[...])
        h1 = n1 * par(GAIN) + par(SHIFT)
        query = ((dot(h1.astype(BF), r.v_wq[...]) + par(CBIAS)) * SCALE).astype(BF)
        for c in c_kv:
            c.wait()
        g_mem.end_forward(2)
        g_mem.finish()

        @pl.loop(0, total_rows // 256)
        def _(i):
            block = rows_of(r.mem_all, i)
            key[span(i), :] = dot(block, wk[...]).astype(BF)
            value[span(i), :] = (dot(block, wv[...]) + par(VBIAS)).astype(BF)

        live = lanes((own_rows, total_rows)) < r.length[0]
        stat = jnp.zeros((own_rows, 128), F32)
        for p in range(6):
            cols = slice(128 * p, 128 * p + 128)
            found = []
            for a in (0, 1):
                head = pick(second_own == bool(a), query[:, cols])
                s = jnp.where(live, dot_nt(head, key[:, cols]), NEG)
                top = jnp.max(s, -1, keepdims=True)
                e = jnp.exp(s - top)
                total = jnp.sum(e, -1, keepdims=True)
                pr = (e * (1.0 / total)).astype(BF)
                probs[2 * p + a] = pr
                found.append(dot(pr, value[:, cols]))
                stat = jnp.where(lanes((own_rows, 128)) == 2 * p + a, top + jnp.log(total), stat)
            attn[:, cols] = jnp.where(second_own, found[1], found[0])
        low = attn[...].astype(BF)
        r.low_all[me] = low
        g_low.start()
        r2 = h1 + dot(low, r.v_wo[...]) + par(CBIAS + 1)
        n2, inv2 = norm_parts(r2)
        h2 = n2 * par(GAIN + 1) + par(SHIFT + 1)
        h2_low = h2.astype(BF)
        c_wi.wait()

        @pl.loop(0, FF // 512)
        def _(c):
            cols = span(c, 512)
            up, down = gelu_parts(dot(h2_low, wi[:, cols]) + r.bi[:, cols])
            act[:, cols] = up.astype(BF)
            slope[:, cols] = down

        c_wf.wait()
        r3 = h2 + dot(act[...], wf[...]) + par(FBIAS)
        n3, inv3 = norm_parts(r3)
        r.n3_all[me] = n3.astype(BF)
        r.stats_all[me] = jnp.where(lanes((own_rows, 128)) == HEADS, inv3, stat).T[0:16, :]
        g_stats.start()
        g_n3.start()
        g_low.inner_forward(0)
        c_cot.wait()
        g3 = cotv[...].astype(F32)
        vec = r.vec
        vec[...] = jnp.zeros_like(vec)
        vec[2:3, :] = col_sum(g3 * n3)
        vec[5:6, :] = col_sum(g3)
        grad_r3 = norm_grad(g3, n3, inv3, par(GAIN + 2))
        z_low = grad_r3.astype(BF)
        vec[9:10, :] = col_sum(z_low.astype(F32))

        @pl.loop(0, FF // 512)
        def _(c):
            cols = span(c, 512)
            act[:, cols] = (dot_nt(z_low, wf[cols, :]) * slope[:, cols]).astype(BF)

        grad_h2 = grad_r3 + dot_nt(act[...], wi[...])
        vec[1:2, :] = col_sum(grad_h2 * n2)
        vec[4:5, :] = col_sum(grad_h2)
        grad_r2 = norm_grad(grad_h2, n2, inv2, par(GAIN + 1))
        co_low = grad_r2.astype(BF)
        g_low.inner_forward(1, 2)
        g_low.end_forward(0)
        r.co_all[me] = co_low
        vec[8:9, :] = col_sum(co_low.astype(F32))
        oc = dot_nt(co_low, r.v_wo[...]).astype(BF)
        product = oc.astype(F32) * attn[...]
        for p in range(6):
            cols = slice(128 * p, 128 * p + 128)
            found = []
            for a in (0, 1):
                sel = second_own == bool(a)
                delta = jnp.sum(jnp.where(sel, product[:, cols], 0.0), -1, keepdims=True)
                dprob = dot_nt(pick(sel, oc[:, cols]), value[:, cols])
                ds = (probs[2 * p + a].astype(F32) * (dprob - delta)).astype(BF)
                found.append(dot(ds, key[:, cols]))
            r.trade_src[2, :, cols] = (
                jnp.where(second_own, found[1], found[0]).astype(BF).astype(F32) * SCALE
            ).astype(BF)
        cq_low = r.trade_src[2]
        vec[7:8, :] = col_sum(cq_low.astype(F32))
        grad_h1 = grad_r2 + dot_nt(cq_low, r.v_wq[...])
        vec[0:1, :] = col_sum(grad_h1 * n1)
        vec[3:4, :] = col_sum(grad_h1)
        so_low = norm_grad(grad_h1, n1, inv1, par(GAIN)).astype(BF)
        r.so_all[me] = so_low
        vec[6:7, :] = col_sum(so_low.astype(F32))
        g_so.start()

    memory_block = pltpu.VMEM((total_rows, D), BF)
    square = pltpu.VMEM((D, D), BF)
    pl.run_scoped(
        row_part,
        pltpu.VMEM((D, FF), BF), pltpu.VMEM((FF, D), BF), square, square, memory_block, memory_block,
        pltpu.VMEM((HEADS, own_rows, total_rows), BF),
        pltpu.VMEM((own_rows, FF), F32), pltpu.VMEM((own_rows, FF), BF),
        pltpu.VMEM((own_rows, D), F32), pltpu.VMEM((own_rows, D), BF),
    )

    def pass_rows(p):
        @pl.when(p == 2)
        def _():
            g_low.end_forward(1, 2)
            g_n3.inner_forward(0)

        @pl.when(p == 3)
        def _():
            g_n3.inner_forward(1, 2)
            g_n3.end_forward(0)

        @pl.when(p == 4)
        def _():
            g_co.start()
            g_so.inner_forward(0)
            g_n3.end_forward(1)

        @pl.when(p == 5)
        def _():
            g_so.inner_forward(1, 2)
            g_n3.end_forward(2)
            g_so.end_forward(0)

    pairs(2, 6, pass_rows)

    def hidden_scope(h2_low, z_low, act, slope, wi_own, wf_own):
        offsets = hidden_offsets(me)
        c_cot = load(r.cot, z_low)
        own_w = [
            load(r.wi.at[:, pl.ds(off, 128)], wi_own.at[:, pl.ds(128 * t, 128)])
            for t, off in enumerate(offsets)
        ] + [
            load(r.wf.at[pl.ds(off, 128), :], wf_own.at[pl.ds(128 * t, 128), :])
            for t, off in enumerate(offsets)
        ]

        def hidden_forward(r1v, h1v):
            @pl.loop(0, 4)
            def _(i):
                rows = span(i)
                resid = (
                    r.v_x[rows, :].astype(F32) + dot(r.v_low[rows, :], r.v_so[...]) + par(SBIAS + 2)
                )
                n1, _ = norm_parts(resid)
                h1 = n1 * par(GAIN) + par(SHIFT)
                r1v[rows, :] = h1
                h1v[rows, :] = h1.astype(BF)
                r.query[rows, :] = (
                    (dot(h1.astype(BF), r.v_wq[...]) + par(CBIAS)) * SCALE
                ).astype(BF)

            c_h1 = load(h1v, r.h1_o)
            g_stats.inner_forward()
            g_co.inner_forward(0)
            g_so.end_forward(1)
            g_low.finish()

            @pl.loop(0, 4)
            def _(i):
                r2 = r1v[span(i), :] + dot(rows_of(r.low_all, i), r.v_wo[...]) + par(CBIAS + 1)
                n2, _ = norm_parts(r2)
                h2_low[two(i)] = (
                    (n2 * par(GAIN + 1) + par(SHIFT + 1)).astype(BF).reshape(2, 128, D)
                )

            g_co.inner_forward(1, 2)
            g_so.end_forward(2)
            c_h1.wait()

        pl.run_scoped(hidden_forward, pltpu.VMEM(wide, F32), pltpu.VMEM(wide, BF))
        for c in own_w:
            c.wait()
        bias = jnp.concatenate([r.bi[:, pl.ds(off, 128)] for off in offsets], axis=1)

        @pl.loop(0, 4)
        def _(i):
            up, down = gelu_parts(dot(rows_of(h2_low, i), wi_own[...]) + bias)
            act[span(i), :] = up.astype(BF)
            slope[span(i), :] = down

        def hidden_backward():
            g_stats.end_forward()
            g_co.end_forward(0)
            g_stats.finish()
            g_n3.finish()
            c_cot.wait()

            @pl.loop(0, 4)
            def _(i):
                normed = rows_of(r.n3_all, i).astype(F32)
                tile = r.stats_all[two(i)]
                inv3 = jnp.concatenate(
                    [
                        jnp.concatenate([tile[b], jnp.zeros((112, 128), F32)], 0).T[:, HEADS : HEADS + 1]
                        for b in (0, 1)
                    ],
                    0,
                )
                z_low[span(i), :] = norm_grad(
                    z_low[span(i), :].astype(F32), normed, inv3, par(GAIN + 2)
                ).astype(BF)

            g_co.end_forward(1)
            for t in range(3):
                r.slab_out[t] = dot_tn(act[:, 128 * t : 128 * t + 128], z_low[...]).astype(BF)
            r.slab_out[3] = jnp.zeros_like(r.slab_out[3])
            share_start(3)

            @pl.loop(0, 4)
            def _(i):
                rows = span(i)
                act[rows, :] = (dot_nt(z_low[rows, :], wf_own[...]) * slope[rows, :]).astype(BF)

            g_co.end_forward(2)
            total = col_sum(act[...].astype(F32))
            for t in range(3):
                lane = pl.ds(pl.multiple_of(128 * (2 * t + me // 4), 128), 128)
                which = lax.broadcasted_iota(jnp.int32, (4, 128), 0) == (me + t) % 4
                r.vec[13:17, lane] = jnp.where(which, total[:, 128 * t : 128 * t + 128], 0.0)

            @pl.loop(0, 3)
            def _(c):
                cols = span(c)
                r.slab_in[cols, :] = dot_tn(
                    h2_low[:, :, cols].reshape(TGT, 256), act[...]
                ).astype(BF)

            share_start(2)

        hidden_backward()

    pl.run_scoped(
        hidden_scope,
        pltpu.VMEM((nb, own_rows, D), BF), pltpu.VMEM(wide, BF),
        pltpu.VMEM((TGT, 384), BF), pltpu.VMEM((TGT, 384), F32),
        pltpu.VMEM((D, 384), BF), pltpu.VMEM((384, D), BF),
    )
    c_n3 = load(r.n3_all, r.n3_out)

    def trade(k, target, origin):
        source = (target // 2 + 2) % 3
        return pltpu.make_async_remote_copy(
            src_ref=r.trade_src.at[source, :, pl.ds(pl.multiple_of((target % 2) * 384, 128), 384)],
            dst_ref=r.right.at[origin],
            send_sem=r.x_send.at[k], recv_sem=r.x_recv.at[k],
            device_id=(dp, target), device_id_type=MESH,
        )

    def inner_slot(slot):
        return jnp.logical_and(slot >= 2, slot < 6)

    def trade_start(wanted):
        for k in range(1, nb):
            target = (me + k) % nb
            pl.when(wanted(target))(lambda: trade(k, target, me).start())

    def vshare(k):
        peer = (dp + k) % ndp
        return pltpu.make_async_remote_copy(
            src_ref=r.vq.at[peer], dst_ref=r.vgot.at[k],
            send_sem=r.v_send.at[0, k], recv_sem=r.v_recv.at[0, k],
            device_id=(peer, me), device_id_type=MESH,
        )

    def vspread(k, origin):
        return pltpu.make_async_remote_copy(
            src_ref=r.vall.at[origin], dst_ref=r.vall.at[origin],
            send_sem=r.v_send.at[1, k], recv_sem=r.v_recv.at[1, k],
            device_id=(dp, (me + k) % nb), device_id_type=MESH,
        )

    def vectors_start():
        vec = r.vec[...]
        r.vq[...] = jnp.zeros_like(r.vq)
        for q in range(ndp):
            r.vq[q, 0:16, 0:quarter] = vec[0:16, quarter * q : quarter * q + quarter]
            for s in range(ndp):
                r.vq[q, 16 + s : 17 + s, 0:quarter] = vec[
                    13 + q : 14 + q, quarter * s : quarter * s + quarter
                ]
        for k in range(1, ndp):
            vshare(k).start()

    def vectors_spread():
        for k in range(1, ndp):
            vshare(k).wait()
        total = r.vq[dp]
        for k in range(1, ndp):
            total = total + r.vgot[k]
        r.vall[me] = total
        for k in range(1, nb):
            vspread(k, me).start()

    def self_part(go, gs, rights, dkt, dvt, qt, gt, slab_e, slab_l, ebuf, esem):
        parts[0][0], parts[1][0] = slab_e, slab_l
        size = 256

        def fetch(p):
            return pltpu.make_async_copy(r.e_o.at[p], ebuf.at[p % 2], esem.at[p % 2])

        fetch(0).start()
        g_so.finish()

        @pl.loop(0, 4)
        def _(i):
            go[span(i), :] = dot_nt(rows_of(r.so_all, i), r.v_so[...]).astype(BF)

        def one_pair(p):
            @pl.when(p + 1 < 6)
            def _():
                fetch(p + 1).start()

            cols = pair_cols(p)
            second = lanes((size, 128)) >= HEAD
            deltas = []
            for i in range(TGT // size):
                rows = slice(i * size, (i + 1) * size)
                invs = [head_col(r.inv[rows, :], 2 * p + a) for a in (0, 1)]
                scaled = go[rows, cols].astype(F32) * jnp.where(second, invs[1], invs[0])
                gs[rows, :] = scaled.astype(BF)
                product = scaled * r.v_low[rows, cols].astype(F32)
                deltas.append(
                    [
                        jnp.sum(jnp.where(second == bool(a), product, 0.0), -1, keepdims=True)
                        for a in (0, 1)
                    ]
                )
            qt[...] = r.v_q[:, cols].T
            gt[...] = gs[...].T
            fetch(p).wait()
            slot = ebuf.at[p % 2]
            for i in reversed(range(TGT // size)):
                rows = slice(i * size, (i + 1) * size)
                found = []
                for a in (0, 1):
                    own_g = pick(second == bool(a), gs[rows, :])
                    head = slice(HEAD * a, HEAD * a + HEAD)
                    last = (i + 1) * size
                    place = i * (i + 1) // 2
                    e = jnp.concatenate([slot[a, place + j] for j in range(i + 1)], 1)
                    dprob = dot_nt(own_g, r.v_v[0:last, cols])
                    ds = (e.astype(F32) * (dprob - deltas[i][a])).astype(BF)
                    found.append(dot(ds, r.v_k[0:last, cols]))
                    part_k = dot(qt[head, rows], ds)
                    part_v = dot(gt[head, rows], e)
                    if last == TGT:
                        dkt[head, :] = part_k
                        dvt[head, :] = part_v
                    else:
                        dkt[head, 0:last] += part_k
                        dvt[head, 0:last] += part_v
                rights[0, rows, cols] = (
                    jnp.where(second, found[1], found[0]).astype(BF).astype(F32) * SCALE
                ).astype(BF)
            rights[1, :, cols] = dkt[...].T.astype(BF)
            rights[2, :, cols] = dvt[...].T.astype(BF)
            r.vec[10:11, cols] = col_sum(rights[0, :, cols].astype(F32)) * (1.0 / nb)
            r.vec[11:12, cols] = col_sum(rights[2, :, cols].astype(F32)) * (1.0 / nb)

        square_block = pltpu.VMEM((mrows, D), BF)

        def memory_part(wk, wv, key, value, lse_t, delta_t):
            c_kv = [load(r.wk, wk), load(r.wv, wv)]

            g_co.finish()
            c_n3.wait()
            oc = r.n3_all
            member = jnp.where(
                lax.broadcasted_iota(jnp.int32, (16, D), 1) // HEAD
                == lax.broadcasted_iota(jnp.int32, (16, D), 0),
                1.0,
                0.0,
            ).astype(BF)
            for i in range(4):
                rows = slice(256 * i, 256 * i + 256)
                grad_out = dot_nt(rows_of(r.co_all, i), r.v_wo[...]).astype(BF)
                oc[two(i)] = grad_out.reshape(2, 128, D)
                product = grad_out.astype(F32) * rows_of(r.low_all, i).astype(F32)
                big = product.astype(BF)
                small = (product - big.astype(F32)).astype(BF)
                delta_t[:, rows] = dot_nt(member, big) + dot_nt(member, small)
                lse_t[:, rows] = jnp.concatenate([r.stats_all[2 * i], r.stats_all[2 * i + 1]], 1)
            for c in c_kv:
                c.wait()
            key[...] = dot(r.mem_all[me], wk[...]).astype(BF)
            value[...] = (dot(r.mem_all[me], wv[...]) + par(VBIAS)).astype(BF)
            self_middle(0)
            position = me * mrows + lax.broadcasted_iota(jnp.int32, (mrows, 1), 0)
            live = position < r.length[0]
            second = lanes((mrows, 128)) >= HEAD

            @pl.loop(0, 6)
            def _(p):
                cols = pair_cols(p)
                found_k, found_v = [], []
                for a in (0, 1):
                    sel = second == bool(a)
                    s = dot_nt(pick(sel, key[:, cols]), r.query[:, cols])
                    pr = jnp.where(live, jnp.exp(s - lse_t[pl.ds(2 * p + a, 1), :]), 0.0)
                    dprob = dot_nt(pick(sel, value[:, cols]), oc[:, :, cols].reshape(TGT, 128))
                    ds = (pr * (dprob - delta_t[pl.ds(2 * p + a, 1), :])).astype(BF)
                    found_k.append(dot(ds, r.query[:, cols]))
                    found_v.append(dot(pr.astype(BF), oc[:, :, cols].reshape(TGT, 128)))
                r.trade_src[0, :, cols] = jnp.where(second, found_k[1], found_k[0]).astype(BF)
                r.trade_src[1, :, cols] = jnp.where(second, found_v[1], found_v[0]).astype(BF)

            c_h1.start()
            trade_start(inner_slot)
            dk, dv = r.trade_src[0], r.trade_src[1]
            r.mem_grad[...] = (dot_nt(dk, wk[...]) + dot_nt(dv, wv[...])).astype(BF)
            r.vec[12:13, :] = col_sum(dv.astype(F32))

        half = pl.ds(pl.multiple_of((me % 2) * 384, 128), 384)

        c_h1 = pltpu.make_async_copy(r.h1_o, r.query, r.load_sem.at[next(free)])

        def form_cross():
            @pl.when(me % 5 != 1)
            def _():
                r.right[me] = r.trade_src[(me // 2 + 2) % 3, :, half]
                for k in range(1, nb):
                    trade(k, (me + k) % nb, (me + nb - k) % nb).wait_recv()

            @pl.when(me % 5 == 1)
            def _():
                r.right[...] = r.co_all[:, :, half]

            def product(left):
                @pl.loop(0, 3)
                def _(c):
                    r.slab_cross[span(c), :] = dot_tn(
                        left(span(c)), r.right[...].reshape(TGT, 384)
                    ).astype(BF)

            c_h1.wait()
            pl.when(inner_slot(me))(
                lambda: product(lambda cols: r.mem_all[:, :, cols].reshape(TGT, 256))
            )
            pl.when(me % 7 == 0)(lambda: product(lambda cols: r.query[:, cols]))
            pl.when(me % 5 == 1)(
                lambda: product(lambda cols: r.low_all[:, :, cols].reshape(TGT, 256))
            )
            share_start(0)
            share_start(1)

        def self_slab(n):
            slab = parts[n][0]

            @pl.loop(0, 3)
            def _(c):
                rows = span(c)
                for weight in range(3):
                    slab[rows, 384 * weight : 384 * weight + 384] = dot_tn(
                        r.v_x[:, rows], rights[weight, :, 384 * n : 384 * n + 384]
                    ).astype(BF)
                if n == 0:
                    slab[rows, 1152:] = dot_tn(
                        r.v_low[:, rows], r.so_all[...].reshape(TGT, D)
                    ).astype(BF)

            self_start(n)

        def run_memory():
            pl.run_scoped(
                memory_part,
                square, square, square_block, square_block,
                pltpu.VMEM((16, TGT), F32), pltpu.VMEM((16, TGT), F32),
            )

        @pl.loop(0, 6)
        def _(p):
            pl.when(p == 1)(lambda: trade_start(lambda slot: slot % 7 == 0))

            pl.when(p == 2)(lambda: settle(3))

            @pl.when(p == 3)
            def _():
                self_slab(0)
                settle(2)
                run_memory()
                g_groups[3].inner_forward()
                g_groups[3].end_forward(0)

            @pl.when(p == 4)
            def _():
                g_groups[3].end_forward(1, 2)
                g_groups[2].inner_forward(0)

            @pl.when(p == 5)
            def _():
                form_cross()
                g_groups[2].inner_forward(1, 2)
                g_groups[2].end_forward(0)

            one_pair(p)

        self_slab(1)
        vectors_start()
        settle(0)
        settle(1)
        g_groups[2].end_forward(1, 2)
        self_middle(1)

        @pl.loop(0, 4)
        def _(i):
            rows = span(i)
            sq, sk, sv = rights[0, rows, :], rights[1, rows, :], rights[2, rows, :]
            go[rows, :] = (
                rows_of(r.so_all, i).astype(F32)
                + dot_nt(sq, r.v_sq[...])
                + dot_nt(sk, r.v_sk[...])
                + dot_nt(sv, r.v_sv[...])
            ).astype(BF)

            pl.when(i == 1)(lambda: g_groups[0].inner_forward(0))

            @pl.when(i == 3)
            def _():
                g_groups[0].inner_forward(1, 2)
                g_groups[1].inner_forward(0)

        c_grad = load(go, r.input_grad)
        g_groups[0].end_forward(0)
        g_groups[1].inner_forward(1, 2)
        vectors_spread()
        g_groups[0].end_forward(1, 2)
        g_groups[1].end_forward()
        c_grad.wait()


    pl.run_scoped(
        self_part,
        pltpu.VMEM(wide, BF), pltpu.VMEM((TGT, 128), BF), pltpu.VMEM((3,) + wide, BF),
        pltpu.VMEM((128, TGT), F32), pltpu.VMEM((128, TGT), F32),
        pltpu.VMEM((128, TGT), BF), pltpu.VMEM((128, TGT), BF),
        pltpu.VMEM((D, 1920), BF), pltpu.VMEM((D, 1152), BF),
        pltpu.VMEM((2, 2, 10, 256, 256), BF), pltpu.SemaphoreType.DMA((2,)),
    )

    outs = []

    def collect(g, src, dst):
        g_groups[g].finish()
        outs.append(load(src, dst))

    collect(3, r.ag_out, r.ag_out_o)
    collect(2, r.ag, r.ag_o)
    self_end(0)
    outs.append(load(r.chip_e, r.self_e_o))
    self_end(1)
    outs.append(load(r.chip_l, r.self_l_o))
    for g in (0, 1):
        collect(g, r.ag_c.at[g], r.ag_c_o.at[g])
    for k in range(1, nb):
        vspread(k, (me + nb - k) % nb).wait_recv()
    total = r.vall[0]
    for b in range(1, nb):
        total = total + r.vall[b]
    r.vec_out[...] = total
    for k in range(1, nb):
        target = (me + k) % nb
        pl.when(target % 5 != 1)(lambda: trade(k, target, me).wait_send())
        vspread(k, me).wait_send()
    for c in outs:
        c.wait()


FINISH_IN = (
    "n3", "grad_in", "mem_in", "ag", "ag_c", "ag_out", "self_e", "self_l", "vec", "gain", "shift",
)
FINISH_OUT = (
    "out", "input_grad", "mem_grad", "s_q", "s_k", "s_v", "s_o", "c_k", "c_v", "c_q", "c_o", "f_in",
    "f_out", "self_bias", "cross_bias", "cv", "d_gain", "d_shift", "in_bias", "out_bias",
)
FINISH_SCRATCH = ("v_e", "v_l", "v_ag", "v_c", "v_ag_out", "v_n3", "v_f", "v_in", "v_out", "v_y", "v_grad", "v_mem", "v_small", "v_wide", "sem")


def finish_part(nb, ndp, *refs):
    r = Refs(FINISH_IN + FINISH_OUT + FINISH_SCRATCH, refs)
    dp = lax.axis_index("dp")
    quarter = D // ndp
    free = iter(range(40))

    def move(src, dst):
        copy = pltpu.make_async_copy(src, dst, r.sem.at[next(free)])
        copy.start()
        return copy

    c_self = [move(r.self_e, r.v_e), move(r.self_l, r.v_l)]
    c_ag = [move(r.ag_c, r.v_c), move(r.ag, r.v_ag)]
    c_out, c_n3 = move(r.ag_out, r.v_ag_out), move(r.n3, r.v_n3)
    c_grad, c_mem = move(r.grad_in, r.v_grad), move(r.mem_in, r.v_mem)
    done = []
    vec = r.vec
    smalls = (
        (r.self_bias, (10, 11, 6)), (r.cross_bias, (7, 8)), (r.d_gain, (0, 1, 2)),
        (r.d_shift, (3, 4, 5)), (r.cv, (12,)), (r.out_bias, (9,)),
    )
    for m, (ref, rows) in enumerate(smalls):
        for n, row in enumerate(rows):
            r.v_small[m, n : n + 1, :] = vec[row : row + 1, 0:quarter]
        done.append(move(r.v_small.at[m, pl.ds(0, len(rows))], ref))
    for n in range(ndp):
        r.v_wide[:, quarter * n : quarter * n + quarter] = vec[16 + n : 17 + n, 0:quarter]
    done.append(move(r.v_wide, r.in_bias))
    for c in c_self:
        c.wait()

    @pl.loop(0, quarter // 48)
    def _(i):
        rows = span(i, 48)
        for n in range(3):
            cols = slice(384 * n, 384 * n + 384)
            r.v_f[n, rows, 0:384] = r.v_e[rows, cols].astype(F32)
            r.v_f[n, rows, 384:] = r.v_l[rows, cols].astype(F32)
        r.v_f[3, rows, :] = r.v_e[rows, 1152:].astype(F32)

    for n, dst in enumerate((r.s_q, r.s_k, r.s_v, r.s_o)):
        done.append(move(r.v_f.at[n], dst))
    c_ag[0].wait()

    @pl.loop(0, quarter // 48)
    def _(i):
        rows = span(i, 48)
        for b, n in enumerate((4, 7, 5, 5, 6, 6, 7, 4)):
            half = slice(384 * (b % 2), 384 * (b % 2) + 384)
            r.v_f[n, rows, half] = r.v_c[i // 2, b, span(i % 2, 48), :].astype(F32)

    for n, dst in enumerate((r.c_q, r.c_k, r.c_v, r.c_o)):
        done.append(move(r.v_f.at[4 + n], dst))
    c_grad.wait()
    c_mem.wait()
    done += [move(r.v_grad, r.input_grad), move(r.v_mem, r.mem_grad)]
    c_ag[1].wait()

    @pl.loop(0, quarter // 48)
    def _(i):
        rows = span(i, 48)
        for b in range(nb):
            for t in range(3):
                col = D * ((b + t) % 4) + 128 * (2 * t + b // 4)
                r.v_in[rows, col : col + 128] = r.v_ag[
                    b, rows, 128 * t : 128 * t + 128
                ].astype(F32)

    done.append(move(r.v_in, r.f_in))
    c_out.wait()

    @pl.loop(0, nb)
    def _(b):
        t = (dp - b + nb) % 4

        @pl.when(t < 3)
        def _():
            place = pl.ds(pl.multiple_of(128 * (2 * t + b // 4), 128), 128)
            r.v_out[place, :] = r.v_ag_out[b].astype(F32)

    done.append(move(r.v_out, r.f_out))
    c_n3.wait()
    gain, shift = r.gain[...].astype(F32)[2:3, :], r.shift[...].astype(F32)[2:3, :]

    @pl.loop(0, nb)
    def _(b):
        r.v_y[b] = (r.v_n3[b].astype(F32) * gain + shift).astype(BF)

    done.append(move(r.v_y, r.out))
    for c in done:
        c.wait()


def shared_work(
    nb, ndp,
    inputs, memory, lengths, cotangent, self_query, self_key, self_value, self_out, self_bias,
    cross_query, cross_key, cross_value, cross_out, cross_bias, cross_value_bias,
    norm_gain, norm_bias, ffn_in, ffn_in_bias, ffn_out, ffn_out_bias,
):
    own_rows = TGT // nb
    x, mem, cot = inputs[0], memory[0], cotangent[0]
    mrows = mem.shape[0]
    quarter = D // ndp
    gain, shift = norm_gain.T, norm_bias.T
    vecs = (
        jnp.concatenate([cross_value_bias, ffn_out_bias, ffn_in_bias]).reshape(6, D).astype(F32)
    )
    wide, own, square, block = (TGT, D), (own_rows, D), (D, D), (nb, own_rows, D)
    dma = pltpu.SemaphoreType.DMA
    vm = pltpu.VMEM
    n3, grad_in, mem_grad, ag, ag_c, ag_out, self_e, self_l, vec, _, _ = call(
        functools.partial(layer_part, nb, ndp),
        "layer_part",
        (lengths, mem, x, cot, self_query, self_key, self_value, self_out, cross_query, cross_key,
         cross_value, cross_out, ffn_in, ffn_out, gain, shift, self_bias.T, cross_bias.T, vecs),
        [(block, BF), (wide, BF), ((mrows, D), BF), ((nb, quarter, 384), BF),
         ((2, nb, quarter // 2, 384), BF), ((nb, 128, D), BF), ((quarter, 1920), BF), ((quarter, 1152), BF), ((24, 256), F32), (wide, BF), ((6, 2, 10, 256, 256), BF)],
        [vm((16, D), F32), vm((1, FF), F32), vm(wide, BF)]
        + [vm(square, BF)] * 6
        + [vm(wide, BF)] * 4
        + [vm((TGT, 128), F32), vm(own, BF), vm(own, F32), vm(wide, BF), vm((nb, mrows, D), BF)]
        + [vm(block, BF)] * 4
        + [vm((nb, 16, own_rows), F32), vm((3, own_rows, D), BF), vm((nb, own_rows, 384), BF)]
        + [vm((2, quarter, 1920), BF), vm((2, quarter, 1152), BF),
           vm((quarter, 1920), BF), vm((quarter, 1152), BF)]
        + [vm((D, 384), BF)] * 2
        + [vm((4, 128, D), BF), vm((ndp, quarter, 384), BF), vm((2, ndp, quarter // 2, 384), BF),
           vm((ndp, 128, D), BF), vm((2, nb, quarter // 2, 384), BF), vm((nb, quarter, 384), BF),
           vm((nb, 128, D), BF),
           vm((24, D), F32), vm((ndp, 24, 256), F32), vm((ndp, 24, 256), F32), vm((nb, 24, 256), F32)]
        + [dma((64,)), dma((nb,)), dma((nb,)), dma((4, ndp)), dma((4, ndp)), dma((10, 16)),
           dma((10, 16)), dma((2, nb)), dma((2, nb)), dma((2, 3)), dma((2, 3))],
        collective_id=0,
        in_specs=[SMEM] + [ANY] * 13 + [VMEM] * 5,
        out_specs=[ANY] * 2 + [VMEM] + [ANY] * 5 + [VMEM] + [ANY] * 2,
    )
    weight = ((quarter, D), F32)
    (
        out, input_grad, memory_grad, s_q, s_k, s_v, s_o, c_k, c_v, c_q, c_o, f_in, f_out,
        g_self_bias, g_cross_bias, g_cv, g_gain, g_shift, g_in_bias, g_out_bias,
    ) = call(
        functools.partial(finish_part, nb, ndp),
        "finish_part",
        (n3, grad_in, mem_grad, ag, ag_c, ag_out, self_e, self_l, vec, gain, shift),
        [(block, BF), (wide, BF), ((mrows, D), BF)]
        + [weight] * 8
        + [((quarter, FF), F32), ((FF // ndp, D), F32), ((3, quarter), F32), ((2, quarter), F32),
           ((1, quarter), F32), ((3, quarter), F32), ((3, quarter), F32), ((1, FF // ndp), F32),
           ((1, quarter), F32)],
        [vm((quarter, 1920), BF), vm((quarter, 1152), BF), vm((nb, quarter, 384), BF),
         vm((2, nb, quarter // 2, 384), BF),
         vm((nb, 128, D), BF), vm(block, BF),
         vm((8, quarter, D), F32), vm((quarter, FF), F32), vm((FF // ndp, D), F32), vm(block, BF),
         vm(wide, BF), vm((mrows, D), BF), vm((6, 8, quarter), F32), vm((1, FF // ndp), F32),
         dma((40,))],
        in_specs=[ANY] * 8 + [VMEM] * 3,
        out_specs=[ANY] * 20,
    )
    return (
        out.reshape(1, TGT, D), input_grad[None], memory_grad[None],
        s_q, s_k, s_v, s_o, g_self_bias.T, c_q, c_k, c_v, c_o, g_cross_bias.T, g_cv.reshape(quarter),
        g_gain.T, g_shift.T, f_in, g_in_bias.reshape(FF // ndp), f_out, g_out_bias.reshape(quarter),
    )


def merged(array, axis, join):
    gathered = jax.tree.map(
        lambda a, kind: lax.all_gather(a.astype(kind), axis), array, (jnp.bfloat16, jnp.bfloat16)
    )

    def take(source):
        return jax.tree.map(
            lambda a, own: lax.dynamic_index_in_dim(a, source, 0, False).astype(own.dtype),
            gathered,
            array,
        )

    return lax.fori_loop(
        1, lax.axis_size(axis), lambda source, state: join(state, take(source)), take(0)
    )


def layer_norm(residual, gain_col, shift_col):
    average = jnp.mean(residual, axis=-1, keepdims=True)
    centered = residual - average
    variance = jnp.mean(centered * centered, axis=-1, keepdims=True)
    return centered * lax.rsqrt(variance + EPS) * gain_col + shift_col


def exact_gelu(values):
    return jax.nn.gelu(values, approximate=False)


def project(left_side, weight):
    return jnp.dot(left_side, weight, preferred_element_type=jnp.float32)


def project_back(gradient, weight):
    return lax.dot_general(
        gradient, weight, (((1,), (1,)), ((), ())), preferred_element_type=jnp.float32
    )


def weight_grad(left_side, gradient):
    return lax.dot_general(
        left_side, gradient, (((0,), (0,)), ((), ())), preferred_element_type=jnp.float32
    )


def column_sum(gradient):
    return jnp.sum(gradient.astype(jnp.float32), axis=0)


def split_heads(values):
    return values.reshape(values.shape[:-1] + (HEADS, HEAD))


def combine_totals(earlier, latter):
    top_a, sum_a = earlier
    top_b, sum_b = latter
    top_score = jnp.maximum(top_a, top_b)
    return (top_score, sum_a * jnp.exp(top_a - top_score) + sum_b * jnp.exp(top_b - top_score))


def self_scores(query_rows, key_rows, row_start, block_rows):
    scores = jnp.einsum("qhe,khe->hqk", query_rows, key_rows, preferred_element_type=jnp.float32)
    row_pos = row_start + jnp.arange(block_rows)[:, None]
    col_pos = jnp.arange(key_rows.shape[0])[None, :]
    return jnp.where((col_pos <= row_pos)[None], scores, NEG)


def copied_work(
    inputs,
    memory,
    lengths,
    cotangent,
    self_query,
    self_key,
    self_value,
    self_out,
    self_bias,
    cross_query,
    cross_key,
    cross_value,
    cross_out,
    cross_bias,
    cross_value_bias,
    norm_gain,
    norm_bias,
    ffn_in,
    ffn_in_bias,
    ffn_out,
    ffn_out_bias,
):
    all_rows = ITEMS * TGT
    block_rows = min(512, TGT)
    mem_rows = memory.shape[1]
    self_bias_f = self_bias.astype(jnp.float32)
    cross_bias_f = cross_bias.astype(jnp.float32)
    gains = norm_gain.astype(jnp.float32)
    shifts = norm_bias.astype(jnp.float32)
    flat_in = inputs.reshape(all_rows, D)
    query_self = split_heads(
        ((project(flat_in, self_query) + self_bias_f[:, 0]) * SCALE)
        .astype(jnp.bfloat16)
        .reshape(ITEMS, TGT, D)
    )
    key_self = split_heads(project(flat_in, self_key).astype(jnp.bfloat16).reshape(ITEMS, TGT, D))
    value_self = split_heads(
        (project(flat_in, self_value) + self_bias_f[:, 1])
        .astype(jnp.bfloat16)
        .reshape(ITEMS, TGT, D)
    )
    item_index = 0
    attn_blocks = []
    lse_blocks = []
    for row_start in range(0, TGT, block_rows):
        row_end = row_start + block_rows
        scores = self_scores(
            query_self[item_index, row_start:row_end],
            key_self[item_index, :row_end],
            row_start,
            block_rows,
        )
        top_score = jnp.max(scores, axis=-1, keepdims=True)
        log_total = top_score + jnp.log(
            jnp.sum(jnp.exp(scores - top_score), axis=-1, keepdims=True)
        )
        probs_low = jnp.exp(scores - log_total).astype(jnp.bfloat16)
        attn_blocks.append(
            jnp.einsum(
                "hqk,khe->qhe",
                probs_low,
                value_self[item_index, :row_end],
                preferred_element_type=jnp.float32,
            )
        )
        lse_blocks.append(log_total)
    attn_items = [jnp.concatenate(attn_blocks, axis=0)]
    lse_self = [lse_blocks]
    self_attn = jnp.stack(attn_items, axis=0)
    self_low = self_attn.astype(jnp.bfloat16).reshape(all_rows, D)
    resid_one = flat_in.astype(jnp.float32) + project(self_low, self_out) + self_bias_f[:, 2]
    hidden_one, norm1_back = jax.vjp(layer_norm, resid_one, gains[:, 0], shifts[:, 0])
    hidden_low = hidden_one.astype(jnp.bfloat16)
    query_cross = split_heads(
        ((project(hidden_low, cross_query) + cross_bias_f[:, 0]) * SCALE)
        .astype(jnp.bfloat16)
        .reshape(ITEMS, TGT, D)
    )
    flat_mem = memory.reshape(ITEMS * mem_rows, D)
    key_cross = split_heads(
        project(flat_mem, cross_key).astype(jnp.bfloat16).reshape(ITEMS, mem_rows, D)
    )
    value_cross = split_heads(
        (project(flat_mem, cross_value) + cross_value_bias.astype(jnp.float32))
        .astype(jnp.bfloat16)
        .reshape(ITEMS, mem_rows, D)
    )
    position = lax.axis_index("blk") * mem_rows + jnp.arange(mem_rows)
    live_mask = position[None, :] < lengths[:, None]

    def cross_scores():
        raw_scores = jnp.einsum(
            "bqhe,bkhe->bhqk", query_cross, key_cross, preferred_element_type=jnp.float32
        )
        return jnp.where(live_mask[:, None, None, :], raw_scores, NEG)

    scores = cross_scores()
    top_local = jnp.max(scores, axis=-1)
    sum_local = jnp.sum(jnp.exp(scores - top_local[..., None]), axis=-1)
    top_all, sum_all = merged((top_local, sum_local), "blk", combine_totals)
    cross_lse = top_all + jnp.log(sum_all)
    probs_low = jnp.exp(scores - cross_lse[..., None]).astype(jnp.bfloat16)
    share_out = jnp.einsum(
        "bhqk,bkhe->bqhe", probs_low, value_cross, preferred_element_type=jnp.float32
    ).reshape(all_rows, D)
    cot_flat = cotangent.reshape(all_rows, D)
    attn_rows = lax.psum(share_out, "blk")
    cross_low = attn_rows.astype(jnp.bfloat16)
    resid_two = hidden_one + project(cross_low, cross_out) + cross_bias_f[:, 1]
    hidden_two, norm2_back = jax.vjp(layer_norm, resid_two, gains[:, 1], shifts[:, 1])
    second_low = hidden_two.astype(jnp.bfloat16)
    pre_act = project(second_low, ffn_in) + ffn_in_bias.astype(jnp.float32)
    activated, gelu_back = jax.vjp(exact_gelu, pre_act)
    act_low = activated.astype(jnp.bfloat16)
    resid_three = hidden_two + project(act_low, ffn_out) + ffn_out_bias.astype(jnp.float32)
    result, norm3_back = jax.vjp(layer_norm, resid_three, gains[:, 2], shifts[:, 2])
    result_low = result.astype(jnp.bfloat16)
    grad_r3, grad_gain3, grad_shift3 = norm3_back(cot_flat.astype(jnp.float32))
    z_low = grad_r3.astype(jnp.bfloat16)
    g_ffn_out = weight_grad(act_low, z_low)
    g_ffn_out_bias = column_sum(z_low)
    (grad_pre,) = gelu_back(project_back(z_low, ffn_out))
    pre_low = grad_pre.astype(jnp.bfloat16)
    g_ffn_in = weight_grad(second_low, pre_low)
    g_ffn_in_bias = column_sum(pre_low)
    grad_h2 = grad_r3 + project_back(pre_low, ffn_in)
    grad_r2, grad_gain2, grad_shift2 = norm2_back(grad_h2)
    co_low = grad_r2.astype(jnp.bfloat16)
    g_cross_out = weight_grad(cross_low, co_low)
    g_co_bias = column_sum(co_low)
    oc_low = project_back(co_low, cross_out).astype(jnp.bfloat16)
    out_rows = result_low.reshape(ITEMS, TGT, D)
    grad_oc = split_heads(oc_low.reshape(ITEMS, TGT, D))
    cross_delta = jnp.transpose(
        jnp.sum(
            grad_oc.astype(jnp.float32) * split_heads(attn_rows.reshape(ITEMS, TGT, D)), axis=-1
        ),
        (0, 2, 1),
    )
    scores = cross_scores()
    prob_full = jnp.exp(scores - cross_lse[..., None])
    grad_probs = jnp.einsum(
        "bqhe,bkhe->bhqk", grad_oc, value_cross, preferred_element_type=jnp.float32
    )
    grad_scores = (prob_full * (grad_probs - cross_delta[..., None])).astype(jnp.bfloat16)
    query_share = jnp.einsum(
        "bhqk,bkhe->bqhe", grad_scores, key_cross, preferred_element_type=jnp.float32
    ).reshape(all_rows, D)
    key_low = (
        jnp.einsum("bhqk,bqhe->bkhe", grad_scores, query_cross, preferred_element_type=jnp.float32)
        .astype(jnp.bfloat16)
        .reshape(ITEMS * mem_rows, D)
    )
    value_low = (
        jnp.einsum(
            "bhqk,bqhe->bkhe",
            prob_full.astype(jnp.bfloat16),
            grad_oc,
            preferred_element_type=jnp.float32,
        )
        .astype(jnp.bfloat16)
        .reshape(ITEMS * mem_rows, D)
    )
    grad_cq = lax.psum(query_share, "blk")
    cq_low = (grad_cq * SCALE).astype(jnp.bfloat16)
    g_cross_query = weight_grad(hidden_one.astype(jnp.bfloat16), cq_low)
    g_cq_bias = column_sum(cq_low)
    grad_h1_rows = grad_r2 + project_back(cq_low, cross_query)
    g_cross_key_dev = weight_grad(flat_mem, key_low)
    g_cross_value_dev = weight_grad(flat_mem, value_low)
    g_cv_bias_dev = column_sum(value_low)
    memory_grad = (
        (project_back(key_low, cross_key) + project_back(value_low, cross_value))
        .astype(jnp.bfloat16)
        .reshape(ITEMS, mem_rows, D)
    )
    g_cross_key, g_cross_value, g_cv_bias = lax.psum(
        (g_cross_key_dev, g_cross_value_dev, g_cv_bias_dev), "blk"
    )
    grad_r1, grad_gain1, grad_shift1 = norm1_back(grad_h1_rows)
    so_low = grad_r1.astype(jnp.bfloat16)
    g_self_out = weight_grad(self_low, so_low)
    g_so_bias = column_sum(so_low)
    grad_os = split_heads(
        project_back(so_low, self_out).astype(jnp.bfloat16).reshape(ITEMS, TGT, D)
    )
    item_index = 0
    key_grad = jnp.zeros((TGT, HEADS, HEAD), jnp.float32)
    value_grad = jnp.zeros((TGT, HEADS, HEAD), jnp.float32)
    query_blocks = []
    for row_start in range(0, TGT, block_rows):
        row_end = row_start + block_rows
        query_rows = query_self[item_index, row_start:row_end]
        key_rows = key_self[item_index, :row_end]
        scores = self_scores(query_rows, key_rows, row_start, block_rows)
        prob_full = jnp.exp(scores - lse_self[item_index][row_start // block_rows])
        grad_out = grad_os[item_index, row_start:row_end]
        row_delta = jnp.transpose(
            jnp.sum(
                grad_out.astype(jnp.float32) * self_attn[item_index, row_start:row_end], axis=-1
            )
        )
        grad_probs = jnp.einsum(
            "qhe,khe->hqk",
            grad_out,
            value_self[item_index, :row_end],
            preferred_element_type=jnp.float32,
        )
        grad_scores = (prob_full * (grad_probs - row_delta[:, :, None])).astype(jnp.bfloat16)
        query_blocks.append(
            jnp.einsum("hqk,khe->qhe", grad_scores, key_rows, preferred_element_type=jnp.float32)
        )
        key_grad = key_grad.at[:row_end].add(
            jnp.einsum("hqk,qhe->khe", grad_scores, query_rows, preferred_element_type=jnp.float32)
        )
        value_grad = value_grad.at[:row_end].add(
            jnp.einsum(
                "hqk,qhe->khe",
                prob_full.astype(jnp.bfloat16),
                grad_out,
                preferred_element_type=jnp.float32,
            )
        )
    query_items = [jnp.concatenate(query_blocks, axis=0)]
    key_items = [key_grad]
    value_items = [value_grad]
    sq_low = (jnp.stack(query_items, 0).astype(jnp.bfloat16) * jnp.bfloat16(SCALE)).reshape(
        all_rows, D
    )
    sk_low = jnp.stack(key_items, 0).astype(jnp.bfloat16).reshape(all_rows, D)
    sv_low = jnp.stack(value_items, 0).astype(jnp.bfloat16).reshape(all_rows, D)
    g_self_query = weight_grad(flat_in, sq_low)
    g_self_key = weight_grad(flat_in, sk_low)
    g_self_value = weight_grad(flat_in, sv_low)
    g_sq_bias = column_sum(sq_low)
    g_sv_bias = column_sum(sv_low)
    input_grad = (
        (
            grad_r1
            + project_back(sq_low, self_query)
            + project_back(sk_low, self_key)
            + project_back(sv_low, self_value)
        )
        .astype(jnp.bfloat16)
        .reshape(ITEMS, TGT, D)
    )
    g_self_bias = jnp.stack([g_sq_bias, g_sv_bias, g_so_bias], axis=1)
    g_cross_bias = jnp.stack([g_cq_bias, g_co_bias], axis=1)
    g_norm_gain = jnp.stack([grad_gain1, grad_gain2, grad_gain3], axis=1)
    g_norm_bias = jnp.stack([grad_shift1, grad_shift2, grad_shift3], axis=1)
    summed = (
        lax.psum_scatter(
            g_self_query.astype(jnp.bfloat16), "dp", scatter_dimension=0, tiled=True
        ).astype(jnp.float32),
        lax.psum_scatter(
            g_self_key.astype(jnp.bfloat16), "dp", scatter_dimension=0, tiled=True
        ).astype(jnp.float32),
        lax.psum_scatter(
            g_self_value.astype(jnp.bfloat16), "dp", scatter_dimension=0, tiled=True
        ).astype(jnp.float32),
        lax.psum_scatter(
            g_self_out.astype(jnp.bfloat16), "dp", scatter_dimension=0, tiled=True
        ).astype(jnp.float32),
        lax.psum_scatter(
            g_cross_query.astype(jnp.bfloat16), "dp", scatter_dimension=0, tiled=True
        ).astype(jnp.float32),
        lax.psum_scatter(
            g_cross_key.astype(jnp.bfloat16), "dp", scatter_dimension=0, tiled=True
        ).astype(jnp.float32),
        lax.psum_scatter(
            g_cross_value.astype(jnp.bfloat16), "dp", scatter_dimension=0, tiled=True
        ).astype(jnp.float32),
        lax.psum_scatter(
            g_cross_out.astype(jnp.bfloat16), "dp", scatter_dimension=0, tiled=True
        ).astype(jnp.float32),
        lax.psum_scatter(
            g_ffn_in.astype(jnp.bfloat16), "dp", scatter_dimension=0, tiled=True
        ).astype(jnp.float32),
        lax.psum_scatter(
            g_ffn_out.astype(jnp.bfloat16), "dp", scatter_dimension=0, tiled=True
        ).astype(jnp.float32),
        lax.psum_scatter(
            g_self_bias.astype(jnp.bfloat16), "dp", scatter_dimension=0, tiled=True
        ).astype(jnp.float32),
        lax.psum_scatter(
            g_cross_bias.astype(jnp.bfloat16), "dp", scatter_dimension=0, tiled=True
        ).astype(jnp.float32),
        lax.psum_scatter(
            g_cv_bias.astype(jnp.bfloat16), "dp", scatter_dimension=0, tiled=True
        ).astype(jnp.float32),
        lax.psum_scatter(
            g_norm_gain.astype(jnp.bfloat16), "dp", scatter_dimension=0, tiled=True
        ).astype(jnp.float32),
        lax.psum_scatter(
            g_norm_bias.astype(jnp.bfloat16), "dp", scatter_dimension=0, tiled=True
        ).astype(jnp.float32),
        lax.psum_scatter(
            g_ffn_in_bias.astype(jnp.bfloat16), "dp", scatter_dimension=0, tiled=True
        ).astype(jnp.float32),
        lax.psum_scatter(
            g_ffn_out_bias.astype(jnp.bfloat16), "dp", scatter_dimension=0, tiled=True
        ).astype(jnp.float32),
    )
    (
        s_query,
        s_key,
        s_value,
        s_out,
        c_query,
        c_key,
        c_value,
        c_out,
        f_in,
        f_out,
        r_self_bias,
        r_cross_bias,
        r_cv_bias,
        r_gain,
        r_shift,
        r_in_bias,
        r_out_bias,
    ) = summed
    return (
        out_rows,
        input_grad,
        memory_grad,
        s_query,
        s_key,
        s_value,
        s_out,
        r_self_bias,
        c_query,
        c_key,
        c_value,
        c_out,
        r_cross_bias,
        r_cv_bias,
        r_gain,
        r_shift,
        f_in,
        r_in_bias,
        f_out,
        r_out_bias,
    )


def solution(mesh):
    nb, ndp = mesh.shape["blk"], mesh.shape["dp"]
    body = copied_work
    if (nb, ndp) == (8, 4):
        body = functools.partial(shared_work, nb, ndp)
    return jax.shard_map(
        body,
        mesh=mesh,
        in_specs=(
            P("dp", None, None),
            P("dp", "blk", None),
            P("dp"),
            P("dp", None, None),
            P(),
            P(),
            P(),
            P(),
            P(),
            P(),
            P(),
            P(),
            P(),
            P(),
            P(),
            P(),
            P(),
            P(),
            P(),
            P(),
            P(),
        ),
        out_specs=(
            P("dp", None, None),
            P("dp", None, None),
            P("dp", "blk", None),
            P("dp", None),
            P("dp", None),
            P("dp", None),
            P("dp", None),
            P("dp", None),
            P("dp", None),
            P("dp", None),
            P("dp", None),
            P("dp", None),
            P("dp", None),
            P("dp"),
            P("dp", None),
            P("dp", None),
            P("dp", None),
            P("dp"),
            P("dp", None),
            P("dp"),
        ),
        check_vma=False,
    )
```

```python
import functools

import jax
import jax.numpy as jnp
from jax import lax
from jax.experimental import pallas as pl
from jax.experimental.pallas import tpu as pltpu
from jax.sharding import PartitionSpec as P

D = 768
HEADS = 12
HEAD = 64
FF = 3072
TGT = 1024
ITEMS = 1


NEG = -1e30
EPS = 1e-05
SCALE = 0.125
BF = jnp.bfloat16
F32 = jnp.float32
MESH = pl.DeviceIdType.MESH
VMEM = pl.BlockSpec(memory_space=pltpu.VMEM)
SMEM = pl.BlockSpec(memory_space=pltpu.SMEM)
ANY = pl.BlockSpec(memory_space=pl.ANY)
LIMIT = 62 * 2**20


def dot(a, b):
    return jnp.dot(a, b, preferred_element_type=F32)


def dot_nt(a, b):
    return lax.dot_general(a, b, (((1,), (1,)), ((), ())), preferred_element_type=F32)


def dot_tn(a, b):
    return lax.dot_general(a, b, (((0,), (0,)), ((), ())), preferred_element_type=F32)


def lanes(shape):
    return lax.broadcasted_iota(jnp.int32, shape, 1)


def norm_parts(residual):
    centered = residual - jnp.mean(residual, axis=-1, keepdims=True)
    inv = lax.rsqrt(jnp.mean(centered * centered, axis=-1, keepdims=True) + EPS)
    return centered * inv, inv


def norm_grad(gradient, normed, inv, gain):
    scaled = gradient * gain
    return (
        scaled
        - jnp.mean(scaled, axis=-1, keepdims=True)
        - normed * jnp.mean(scaled * normed, axis=-1, keepdims=True)
    ) * inv


def gelu_parts(values):
    cdf = 0.5 * (1.0 + lax.erf(values * 0.7071067811865476))
    slope = cdf + values * (jnp.exp(-0.5 * values * values) * 0.3989422804014327)
    return values * cdf, slope


def col_sum(values):
    return jnp.sum(values, axis=0, keepdims=True)


class Gather:
    def __init__(self, buf, send, recv, live=None):
        self.buf, self.send, self.recv = buf, send, recv
        self.me = lax.axis_index("blk")
        self.y, self.z = self.me % 2, self.me // 2
        self.others = (1 + self.z % 2, (2 + 3 * self.z) % 5, 3 * (1 - self.z // 2))
        self.paired = self.z + 1 - 2 * (self.z % 2)
        self.live = live
        self.inner = self.z % 3 != 0
        self.end = self.z % 3 == 0
        self.half = buf.shape[1] // 2

    def _do(self, slot, act, also=None):
        wanted = [c for c in (also, self.live and self.live(slot)) if c is not None]
        if not wanted:
            act()
        else:
            pl.when(wanted[0] if len(wanted) == 1 else jnp.logical_and(*wanted))(act)

    def _copy(self, slot, z, y, sem, recv=None, part=None):
        ref = self.buf.at[slot]
        if part is not None:
            ref = ref.at[pl.ds(part * self.half, self.half), :]
        return pltpu.make_async_remote_copy(
            src_ref=ref,
            dst_ref=ref,
            send_sem=self.send.at[sem],
            recv_sem=self.recv.at[slot if recv is None else recv],
            device_id=(lax.axis_index("dp"), z * 2 + y),
            device_id_type=MESH,
        )

    def _along(self, z):
        return self._copy(self.me, z, self.y, z)

    def _across(self, z, part=None):
        return self._copy(2 * z + self.y, self.z, 1 - self.y, 4 + z, part=part)

    def _pass_on(self, z):
        return self._copy(2 * z + self.y, self.others[1], self.y, 8 + z)

    def _mirror(self, z):
        return 2 * z + 1 - self.y

    def _pass_mirror(self):
        return self._copy(self._mirror(self.z), self.paired, self.y, 12, 8, 1)

    def _arrived(self, slot, part=None, recv=None, also=None):
        copy = self._copy(slot, self.z, 1 - self.y, 0, recv, part)
        self._do(slot, lambda: copy.wait_recv(), also)

    def _by_pair(self, n, half, whole):
        if n == 2:
            whole()
        else:
            pl.when(self.end if n == 0 else self.inner)(half)
            pl.when(self.inner if n == 0 else self.end)(whole)

    def start(self):
        def act():
            self._across(self.z).start()
            for z in self.others[:2]:
                self._along(z).start()

        self._do(self.me, act)

    def _forward(self, inner, which):
        for n in which or (0, 1, 2):
            z = self.others[n]
            slot = 2 * z + self.y
            if n == 0:
                mirror = self._mirror(self.z)
                self._arrived(mirror)
                self._do(mirror, lambda: self._pass_mirror().start())
            self._arrived(slot)
            part = 0 if n == int(inner) else None
            self._do(slot, lambda: self._across(z, part).start())
            if inner and n != 1:
                self._do(slot, lambda: self._pass_on(z).start())

    def inner_forward(self, *which):
        pl.when(self.inner)(lambda: self._forward(True, which))

    def end_forward(self, *which):
        pl.when(self.end)(lambda: self._forward(False, which))

    def finish(self):
        for n, z in enumerate(self.others):
            slot = self._mirror(z)

            def half():
                self._arrived(slot, 0)
                self._arrived(slot, 1, 8)

            self._by_pair(n, half, lambda: self._arrived(slot))

        def act():
            self._across(self.z).wait_send()
            for z in self.others[:2]:
                self._along(z).wait_send()

        self._do(self.me, act)
        self._do(self._mirror(self.z), lambda: self._pass_mirror().wait_send())
        for n, z in enumerate(self.others):
            slot = 2 * z + self.y
            self._do(
                slot,
                lambda: self._by_pair(
                    n, lambda: self._across(z, 0).wait_send(), lambda: self._across(z).wait_send()
                ),
            )
            if n != 1:
                self._do(slot, lambda: self._pass_on(z).wait_send(), self.inner)


def greet(blk_peers, dp_peers):
    dp, blk = lax.axis_index("dp"), lax.axis_index("blk")
    barrier = pltpu.get_barrier_semaphore()
    for k in range(1, blk_peers):
        pl.semaphore_signal(
            barrier, inc=1, device_id=(dp, (blk + k) % blk_peers), device_id_type=MESH
        )
    for k in range(1, dp_peers):
        pl.semaphore_signal(
            barrier, inc=1, device_id=((dp + k) % dp_peers, blk), device_id_type=MESH
        )
    pl.semaphore_wait(barrier, max(blk_peers - 1, 0) + max(dp_peers - 1, 0))


def call(body, name, ins, outs, scratch=(), collective_id=None, in_specs=None, out_specs=None):
    extra = {} if collective_id is None else {"collective_id": collective_id, "has_side_effects": True}
    return pl.pallas_call(
        body,
        out_shape=[jax.ShapeDtypeStruct(s, k) for s, k in outs],
        in_specs=in_specs or [VMEM] * len(ins),
        out_specs=out_specs or [VMEM] * len(outs),
        scratch_shapes=list(scratch),
        compiler_params=pltpu.CompilerParams(vmem_limit_bytes=LIMIT, **extra),
        name=name,
    )(*ins)


def pair_cols(p):
    return pl.ds(pl.multiple_of(p * 128, 128), 128)


def pick(own, block):
    return jnp.where(own, block, jnp.zeros_like(block))


class Refs:
    def __init__(self, names, refs):
        for name, ref in zip(names, refs, strict=True):
            setattr(self, name, ref)


def two(i):
    return pl.ds(2 * i, 2)


def rows_of(ref, i):
    return ref[two(i)].reshape(256, ref.shape[-1])


def span(i, size=256):
    return pl.ds(pl.multiple_of(i * size, size), size)


def head_col(block, h):
    return jnp.sum(jnp.where(lanes(block.shape) == h, block, 0.0), -1, keepdims=True)


def triangle(size):
    return lanes((size, size)) <= lax.broadcasted_iota(jnp.int32, (size, size), 0)


LAYER_IN = (
    "length", "mem", "x", "cot", "sq", "sk", "sv", "so_w", "wq", "wk", "wv", "wo", "wi", "wf",
    "gain", "shift", "sbias", "cbias", "vecs",
)
LAYER_OUT = ("n3_out", "input_grad", "mem_grad", "ag_o", "ag_c_o", "ag_out_o", "self_e_o", "self_l_o", "vec_out", "h1_o", "e_o")
LAYER_SCRATCH = (
    "par", "bi", "v_x", "v_sq", "v_sk", "v_sv", "v_so", "v_wq", "v_wo", "v_q", "v_k", "v_v", "v_low",
    "inv", "attn_own", "r1_own", "query", "mem_all", "low_all", "n3_all", "so_all", "co_all",
    "stats_all", "trade_src", "right", "core_e", "core_l", "chip_e", "chip_l",
    "slab_cross", "slab_in", "slab_out", "got", "got_c", "got_out", "ag_c", "ag", "ag_out", "vec", "vq", "vgot", "vall", "load_sem", "x_send", "x_recv",
    "d_send", "d_recv", "g_send", "g_recv", "v_send", "v_recv", "s_send", "s_recv",
)
GAIN, SHIFT, SBIAS, CBIAS, VBIAS, FBIAS = 0, 3, 6, 9, 11, 12


def hidden_offsets(me):
    return [pl.multiple_of(D * ((me + t) % 4) + 128 * (2 * t + me // 4), 128) for t in range(3)]


def layer_part(nb, ndp, *refs):
    r = Refs(LAYER_IN + LAYER_OUT + LAYER_SCRATCH, refs)
    dp, me = lax.axis_index("dp"), lax.axis_index("blk")
    own_rows = TGT // nb
    quarter = D // ndp
    mrows = r.mem.shape[0]
    total_rows = nb * mrows
    wide = (TGT, D)
    free = iter(range(64))

    def load(src, dst):
        copy = pltpu.make_async_copy(src, dst, r.load_sem.at[next(free)])
        copy.start()
        return copy

    def par(row):
        return r.par[row : row + 1, :]

    gathers = [
        Gather(buf, r.g_send.at[n], r.g_recv.at[n])
        for n, buf in enumerate((r.mem_all, r.low_all, r.n3_all, r.so_all, r.co_all, r.stats_all))
    ]
    g_mem, g_low, g_n3, g_so, g_co, g_stats = gathers
    g_groups = [
        Gather(buf, r.g_send.at[6 + g], r.g_recv.at[6 + g])
        for g, buf in enumerate((r.ag_c.at[0], r.ag_c.at[1], r.ag))
    ]
    g_groups.append(
        Gather(
            r.ag_out, r.g_send.at[9], r.g_recv.at[9], lambda slot: (dp - slot + nb) % 4 < 3
        )
    )

    def slab_rows(g, owner):
        if g == 2:
            return r.slab_in.at[pl.ds(pl.multiple_of(owner * quarter, 16), quarter), :]
        start = pl.multiple_of(owner * quarter + g * (quarter // 2), 16)
        return r.slab_cross.at[pl.ds(start, quarter // 2), :]

    def share(g, k):
        peer = (dp + k) % ndp
        if g == 3:
            src, dst = r.slab_out.at[(peer - me + nb) % 4], r.got_out.at[k]
        else:
            src, dst = slab_rows(g, peer), (r.got if g == 2 else r.got_c.at[g]).at[k]
        return pltpu.make_async_remote_copy(
            src_ref=src, dst_ref=dst, send_sem=r.d_send.at[g, k], recv_sem=r.d_recv.at[g, k],
            device_id=(peer, me), device_id_type=MESH,
        )

    def share_start(g):
        for k in range(1, ndp):
            share(g, k).start()

    def settle(g):
        for k in range(1, ndp):
            share(g, k).wait()
        if g == 3:
            total = r.slab_out[(dp - me + nb) % 4].astype(F32)
            for k in range(1, ndp):
                total = total + r.got_out[k].astype(F32)
            r.ag_out[me] = total.astype(BF)
        else:
            got, out = (r.got, r.ag) if g == 2 else (r.got_c.at[g], r.ag_c.at[g])
            total = slab_rows(g, dp)[...].astype(F32)
            for k in range(1, ndp):
                total = total + got[k].astype(F32)
            out[me] = total.astype(BF)
        g_groups[g].start()

    core, chip = dp % 2, dp // 2
    parts = [[None, r.core_e, r.chip_e], [None, r.core_l, r.chip_l]]

    def to_core(n, other):
        slab, core_got, _ = parts[n]
        start = pl.multiple_of((2 * other + 1 - core) * quarter, 16)
        return pltpu.make_async_remote_copy(
            src_ref=slab.at[pl.ds(start, quarter), :], dst_ref=core_got.at[other],
            send_sem=r.s_send.at[n, other], recv_sem=r.s_recv.at[n, other],
            device_id=(2 * chip + 1 - core, me), device_id_type=MESH,
        )

    def to_chip(n):
        _, core_got, chip_got = parts[n]
        return pltpu.make_async_remote_copy(
            src_ref=core_got.at[1 - chip], dst_ref=chip_got,
            send_sem=r.s_send.at[n, 2], recv_sem=r.s_recv.at[n, 2],
            device_id=(2 - 2 * chip + core, me), device_id_type=MESH,
        )

    def self_start(n):
        for other in (0, 1):
            to_core(n, other).start()

    def self_middle(n):
        slab, core_got, _ = parts[n]
        for other in (0, 1):
            to_core(n, other).wait()
        for other in (0, 1):
            @pl.loop(0, quarter // 48)
            def _(i):
                start = pl.multiple_of((2 * other + core) * quarter, 16)
                mine = slab[pl.ds(start + span(i, 48).start, 48), :].astype(F32)
                rows = span(i, 48)
                core_got[other, rows, :] = (mine + core_got[other, rows, :].astype(F32)).astype(BF)

        to_chip(n).start()

    def self_end(n):
        _, core_got, chip_got = parts[n]
        to_chip(n).wait()

        @pl.loop(0, quarter // 48)
        def _(i):
            rows = span(i, 48)
            chip_got[rows, :] = (
                chip_got[rows, :].astype(F32) + core_got[chip, rows, :].astype(F32)
            ).astype(BF)

    c_mem = load(r.mem, r.mem_all.at[me])
    c_x = load(r.x, r.v_x)
    c_qkv = [load(s, d) for s, d in ((r.sq, r.v_sq), (r.sk, r.v_sk), (r.sv, r.v_sv))]
    c_more = [load(s, d) for s, d in ((r.so_w, r.v_so), (r.wq, r.v_wq), (r.wo, r.v_wo))]
    r.par[0:3, :] = r.gain[...].astype(F32)
    r.par[3:6, :] = r.shift[...].astype(F32)
    r.par[6:9, :] = r.sbias[...].astype(F32)
    r.par[9:11, :] = r.cbias[...].astype(F32)
    r.par[11:13, :] = r.vecs[0:2, :]
    for c in range(4):
        r.bi[:, D * c : D * c + D] = r.vecs[2 + c : 3 + c, :]
    greet(nb, ndp)
    c_mem.wait()
    g_mem.start()
    c_x.wait()
    for c in c_qkv:
        c.wait()

    @pl.loop(0, 4)
    def _(i):
        rows = span(i)
        block = r.v_x[rows, :]
        r.v_q[rows, :] = ((dot(block, r.v_sq[...]) + par(SBIAS)) * SCALE).astype(BF)
        r.v_k[rows, :] = dot(block, r.v_sk[...]).astype(BF)
        r.v_v[rows, :] = (dot(block, r.v_sv[...]) + par(SBIAS + 1)).astype(BF)

    own = span(me, own_rows)
    second_own = lanes((own_rows, 128)) >= HEAD
    reach = lanes((own_rows, TGT)) - lax.broadcasted_iota(jnp.int32, (own_rows, TGT), 0)
    seen = reach <= me * own_rows

    @pl.loop(0, 6)
    def _(p):
        cols = pair_cols(p)
        found = []
        for a in (0, 1):
            head = pick(second_own == bool(a), r.v_q[own, cols])
            s = jnp.where(seen, dot_nt(head, r.v_k[:, cols]), NEG)
            e = jnp.exp(s - jnp.max(s, -1, keepdims=True))
            found.append(dot(e.astype(BF), r.v_v[:, cols]) / jnp.sum(e, -1, keepdims=True))
        r.attn_own[:, cols] = jnp.where(second_own, found[1], found[0]).astype(BF)

    g_mem.inner_forward(0)
    g_mem.end_forward(0)
    for c in c_more:
        c.wait()
    r.r1_own[...] = r.v_x[own, :].astype(F32) + dot(r.attn_own[...], r.v_so[...]) + par(SBIAS + 2)

    r.inv[...] = jnp.zeros_like(r.inv)

    def pairs(first, last, between):
        def body(ebuf, esem):
            def keep(p):
                return pltpu.make_async_copy(ebuf.at[p % 2], r.e_o.at[p], esem.at[p % 2])

            size = 256

            def one_pair(p):
                slot = ebuf.at[p % 2]
                cols = pair_cols(p)
                for i in range(TGT // size):
                    rows = slice(i * size, (i + 1) * size)
                    place = i * (i + 1) // 2
                    second = lanes((size, 128)) >= HEAD
                    found, kept = [], r.inv[rows, :]
                    for a in (0, 1):
                        head = pick(second == bool(a), r.v_q[rows, cols])
                        last = (i + 1) * size
                        s = dot_nt(head, r.v_k[0:last, cols])
                        s_diag = jnp.where(triangle(size), s[:, i * size :], NEG)
                        s = jnp.concatenate([s[:, : i * size], s_diag], 1) if i else s_diag
                        e = jnp.exp(s - jnp.max(s, -1, keepdims=True))
                        total = jnp.sum(e, -1, keepdims=True)
                        e_low = e.astype(BF)
                        for j in range(i + 1):
                            slot[a, place + j] = e_low[:, j * size : (j + 1) * size]
                        part = dot(e_low, r.v_v[0:last, cols])
                        inverse = 1.0 / total
                        found.append(part * inverse)
                        kept = jnp.where(lanes((size, 128)) == 2 * p + a, inverse, kept)
                    r.v_low[rows, cols] = jnp.where(second, found[1], found[0]).astype(BF)
                    r.inv[rows, :] = kept
                keep(p).start()

            @pl.loop(first, last)
            def _(p):
                @pl.when(p >= first + 2)
                def _():
                    keep(p - 2).wait()

                one_pair(p)
                between(p)

            for p in range(max(first, last - 2), last):
                keep(p).wait()

        pl.run_scoped(
            body, pltpu.VMEM((2, 2, 10, 256, 256), BF), pltpu.SemaphoreType.DMA((2,))
        )

    def pass_memory(p):
        pl.when(p == 0)(lambda: g_mem.inner_forward(1, 2))
        pl.when(p == 1)(lambda: g_mem.end_forward(1))

    pairs(0, 2, pass_memory)

    def row_part(wi, wf, wk, wv, key, value, probs, slope, act, attn, cotv):
        c_kv = [load(r.wk, wk), load(r.wv, wv)]
        c_wi, c_cot, c_wf = load(r.wi, wi), load(r.cot.at[own, :], cotv), load(r.wf, wf)
        n1, inv1 = norm_parts(r.r1_own[...])
        h1 = n1 * par(GAIN) + par(SHIFT)
        query = ((dot(h1.astype(BF), r.v_wq[...]) + par(CBIAS)) * SCALE).astype(BF)
        for c in c_kv:
            c.wait()
        g_mem.end_forward(2)
        g_mem.finish()

        @pl.loop(0, total_rows // 256, unroll=2)
        def _(i):
            block = rows_of(r.mem_all, i)
            key[span(i), :] = dot(block, wk[...]).astype(BF)
            value[span(i), :] = (dot(block, wv[...]) + par(VBIAS)).astype(BF)

        live = lanes((own_rows, total_rows)) < r.length[0]
        stat = jnp.zeros((own_rows, 128), F32)
        for p in range(6):
            cols = slice(128 * p, 128 * p + 128)
            found = []
            for a in (0, 1):
                head = pick(second_own == bool(a), query[:, cols])
                s = jnp.where(live, dot_nt(head, key[:, cols]), NEG)
                top = jnp.max(s, -1, keepdims=True)
                e = jnp.exp(s - top)
                total = jnp.sum(e, -1, keepdims=True)
                pr = (e * (1.0 / total)).astype(BF)
                probs[2 * p + a] = pr
                found.append(dot(pr, value[:, cols]))
                stat = jnp.where(lanes((own_rows, 128)) == 2 * p + a, top + jnp.log(total), stat)
            attn[:, cols] = jnp.where(second_own, found[1], found[0])
        low = attn[...].astype(BF)
        r.low_all[me] = low
        g_low.start()
        r2 = h1 + dot(low, r.v_wo[...]) + par(CBIAS + 1)
        n2, inv2 = norm_parts(r2)
        h2 = n2 * par(GAIN + 1) + par(SHIFT + 1)
        h2_low = h2.astype(BF)
        c_wi.wait()

        @pl.loop(0, FF // 512)
        def _(c):
            cols = span(c, 512)
            up, down = gelu_parts(dot(h2_low, wi[:, cols]) + r.bi[:, cols])
            act[:, cols] = up.astype(BF)
            slope[:, cols] = down

        c_wf.wait()
        r3 = h2 + dot(act[...], wf[...]) + par(FBIAS)
        n3, inv3 = norm_parts(r3)
        r.n3_all[me] = n3.astype(BF)
        r.stats_all[me] = jnp.where(lanes((own_rows, 128)) == HEADS, inv3, stat).T[0:16, :]
        g_stats.start()
        g_n3.start()
        g_low.inner_forward(0)
        c_cot.wait()
        g3 = cotv[...].astype(F32)
        vec = r.vec
        vec[...] = jnp.zeros_like(vec)
        vec[2:3, :] = col_sum(g3 * n3)
        vec[5:6, :] = col_sum(g3)
        grad_r3 = norm_grad(g3, n3, inv3, par(GAIN + 2))
        z_low = grad_r3.astype(BF)
        vec[9:10, :] = col_sum(z_low.astype(F32))

        @pl.loop(0, FF // 512)
        def _(c):
            cols = span(c, 512)
            act[:, cols] = (dot_nt(z_low, wf[cols, :]) * slope[:, cols]).astype(BF)

        grad_h2 = grad_r3 + dot_nt(act[...], wi[...])
        vec[1:2, :] = col_sum(grad_h2 * n2)
        vec[4:5, :] = col_sum(grad_h2)
        grad_r2 = norm_grad(grad_h2, n2, inv2, par(GAIN + 1))
        co_low = grad_r2.astype(BF)
        g_low.inner_forward(1, 2)
        g_low.end_forward(0)
        r.co_all[me] = co_low
        vec[8:9, :] = col_sum(co_low.astype(F32))
        oc = dot_nt(co_low, r.v_wo[...]).astype(BF)
        product = oc.astype(F32) * attn[...]
        for p in range(6):
            cols = slice(128 * p, 128 * p + 128)
            found = []
            for a in (0, 1):
                sel = second_own == bool(a)
                delta = jnp.sum(jnp.where(sel, product[:, cols], 0.0), -1, keepdims=True)
                dprob = dot_nt(pick(sel, oc[:, cols]), value[:, cols])
                ds = (probs[2 * p + a].astype(F32) * (dprob - delta)).astype(BF)
                found.append(dot(ds, key[:, cols]))
            r.trade_src[2, :, cols] = (
                jnp.where(second_own, found[1], found[0]).astype(BF).astype(F32) * SCALE
            ).astype(BF)
        cq_low = r.trade_src[2]
        vec[7:8, :] = col_sum(cq_low.astype(F32))
        grad_h1 = grad_r2 + dot_nt(cq_low, r.v_wq[...])
        vec[0:1, :] = col_sum(grad_h1 * n1)
        vec[3:4, :] = col_sum(grad_h1)
        so_low = norm_grad(grad_h1, n1, inv1, par(GAIN)).astype(BF)
        r.so_all[me] = so_low
        vec[6:7, :] = col_sum(so_low.astype(F32))
        g_so.start()

    memory_block = pltpu.VMEM((total_rows, D), BF)
    square = pltpu.VMEM((D, D), BF)
    pl.run_scoped(
        row_part,
        pltpu.VMEM((D, FF), BF), pltpu.VMEM((FF, D), BF), square, square, memory_block, memory_block,
        pltpu.VMEM((HEADS, own_rows, total_rows), BF),
        pltpu.VMEM((own_rows, FF), F32), pltpu.VMEM((own_rows, FF), BF),
        pltpu.VMEM((own_rows, D), F32), pltpu.VMEM((own_rows, D), BF),
    )

    def pass_rows(p):
        @pl.when(p == 2)
        def _():
            g_low.end_forward(1, 2)
            g_n3.inner_forward(0)

        @pl.when(p == 3)
        def _():
            g_n3.inner_forward(1, 2)
            g_n3.end_forward(0)

        @pl.when(p == 4)
        def _():
            g_co.start()
            g_so.inner_forward(0)
            g_n3.end_forward(1)

        @pl.when(p == 5)
        def _():
            g_so.inner_forward(1, 2)
            g_n3.end_forward(2)
            g_so.end_forward(0)

    pairs(2, 6, pass_rows)

    def hidden_scope(h2_low, z_low, act, slope, wi_own, wf_own):
        offsets = hidden_offsets(me)
        c_cot = load(r.cot, z_low)
        own_w = [
            load(r.wi.at[:, pl.ds(off, 128)], wi_own.at[:, pl.ds(128 * t, 128)])
            for t, off in enumerate(offsets)
        ] + [
            load(r.wf.at[pl.ds(off, 128), :], wf_own.at[pl.ds(128 * t, 128), :])
            for t, off in enumerate(offsets)
        ]

        def hidden_forward(r1v, h1v):
            @pl.loop(0, 4, unroll=2)
            def _(i):
                rows = span(i)
                resid = (
                    r.v_x[rows, :].astype(F32) + dot(r.v_low[rows, :], r.v_so[...]) + par(SBIAS + 2)
                )
                n1, _ = norm_parts(resid)
                h1 = n1 * par(GAIN) + par(SHIFT)
                r1v[rows, :] = h1
                h1v[rows, :] = h1.astype(BF)
                r.query[rows, :] = (
                    (dot(h1.astype(BF), r.v_wq[...]) + par(CBIAS)) * SCALE
                ).astype(BF)

            c_h1 = load(h1v, r.h1_o)
            g_stats.inner_forward()
            g_co.inner_forward(0)
            g_so.end_forward(1)
            g_low.finish()

            @pl.loop(0, 4, unroll=2)
            def _(i):
                r2 = r1v[span(i), :] + dot(rows_of(r.low_all, i), r.v_wo[...]) + par(CBIAS + 1)
                n2, _ = norm_parts(r2)
                h2_low[two(i)] = (
                    (n2 * par(GAIN + 1) + par(SHIFT + 1)).astype(BF).reshape(2, 128, D)
                )

            g_co.inner_forward(1, 2)
            g_so.end_forward(2)
            c_h1.wait()

        pl.run_scoped(hidden_forward, pltpu.VMEM(wide, F32), pltpu.VMEM(wide, BF))
        for c in own_w:
            c.wait()
        bias = jnp.concatenate([r.bi[:, pl.ds(off, 128)] for off in offsets], axis=1)

        @pl.loop(0, 4, unroll=2)
        def _(i):
            up, down = gelu_parts(dot(rows_of(h2_low, i), wi_own[...]) + bias)
            act[span(i), :] = up.astype(BF)
            slope[span(i), :] = down

        def hidden_backward():
            g_stats.end_forward()
            g_co.end_forward(0)
            g_stats.finish()
            g_n3.finish()
            c_cot.wait()

            @pl.loop(0, 4, unroll=2)
            def _(i):
                normed = rows_of(r.n3_all, i).astype(F32)
                tile = r.stats_all[two(i)]
                inv3 = jnp.concatenate(
                    [
                        jnp.concatenate([tile[b], jnp.zeros((112, 128), F32)], 0).T[:, HEADS : HEADS + 1]
                        for b in (0, 1)
                    ],
                    0,
                )
                z_low[span(i), :] = norm_grad(
                    z_low[span(i), :].astype(F32), normed, inv3, par(GAIN + 2)
                ).astype(BF)

            g_co.end_forward(1)
            for t in range(3):
                r.slab_out[t] = dot_tn(act[:, 128 * t : 128 * t + 128], z_low[...]).astype(BF)
            r.slab_out[3] = jnp.zeros_like(r.slab_out[3])
            share_start(3)

            @pl.loop(0, 4, unroll=2)
            def _(i):
                rows = span(i)
                act[rows, :] = (dot_nt(z_low[rows, :], wf_own[...]) * slope[rows, :]).astype(BF)

            g_co.end_forward(2)
            total = col_sum(act[...].astype(F32))
            for t in range(3):
                lane = pl.ds(pl.multiple_of(128 * (2 * t + me // 4), 128), 128)
                which = lax.broadcasted_iota(jnp.int32, (4, 128), 0) == (me + t) % 4
                r.vec[13:17, lane] = jnp.where(which, total[:, 128 * t : 128 * t + 128], 0.0)

            @pl.loop(0, 3)
            def _(c):
                cols = span(c)
                r.slab_in[cols, :] = dot_tn(
                    h2_low[:, :, cols].reshape(TGT, 256), act[...]
                ).astype(BF)

            share_start(2)

        hidden_backward()

    pl.run_scoped(
        hidden_scope,
        pltpu.VMEM((nb, own_rows, D), BF), pltpu.VMEM(wide, BF),
        pltpu.VMEM((TGT, 384), BF), pltpu.VMEM((TGT, 384), F32),
        pltpu.VMEM((D, 384), BF), pltpu.VMEM((384, D), BF),
    )
    c_n3 = load(r.n3_all, r.n3_out)

    def trade(k, target, origin):
        source = (target // 2 + 2) % 3
        return pltpu.make_async_remote_copy(
            src_ref=r.trade_src.at[source, :, pl.ds(pl.multiple_of((target % 2) * 384, 128), 384)],
            dst_ref=r.right.at[origin],
            send_sem=r.x_send.at[k], recv_sem=r.x_recv.at[k],
            device_id=(dp, target), device_id_type=MESH,
        )

    def inner_slot(slot):
        return jnp.logical_and(slot >= 2, slot < 6)

    def trade_start(wanted):
        for k in range(1, nb):
            target = (me + k) % nb
            pl.when(wanted(target))(lambda: trade(k, target, me).start())

    def vshare(k):
        peer = (dp + k) % ndp
        return pltpu.make_async_remote_copy(
            src_ref=r.vq.at[peer], dst_ref=r.vgot.at[k],
            send_sem=r.v_send.at[0, k], recv_sem=r.v_recv.at[0, k],
            device_id=(peer, me), device_id_type=MESH,
        )

    def vspread(k, origin):
        return pltpu.make_async_remote_copy(
            src_ref=r.vall.at[origin], dst_ref=r.vall.at[origin],
            send_sem=r.v_send.at[1, k], recv_sem=r.v_recv.at[1, k],
            device_id=(dp, (me + k) % nb), device_id_type=MESH,
        )

    def vectors_start():
        vec = r.vec[...]
        r.vq[...] = jnp.zeros_like(r.vq)
        for q in range(ndp):
            r.vq[q, 0:16, 0:quarter] = vec[0:16, quarter * q : quarter * q + quarter]
            for s in range(ndp):
                r.vq[q, 16 + s : 17 + s, 0:quarter] = vec[
                    13 + q : 14 + q, quarter * s : quarter * s + quarter
                ]
        for k in range(1, ndp):
            vshare(k).start()

    def vectors_spread():
        for k in range(1, ndp):
            vshare(k).wait()
        total = r.vq[dp]
        for k in range(1, ndp):
            total = total + r.vgot[k]
        r.vall[me] = total
        for k in range(1, nb):
            vspread(k, me).start()

    def self_part(go, gs, rights, dkt, dvt, qt, gt, slab_e, slab_l, ebuf, esem):
        parts[0][0], parts[1][0] = slab_e, slab_l
        size = 256

        def fetch(p):
            return pltpu.make_async_copy(r.e_o.at[p], ebuf.at[p % 2], esem.at[p % 2])

        fetch(0).start()
        g_so.finish()

        @pl.loop(0, 4)
        def _(i):
            go[span(i), :] = dot_nt(rows_of(r.so_all, i), r.v_so[...]).astype(BF)

        def one_pair(p):
            @pl.when(p + 1 < 6)
            def _():
                fetch(p + 1).start()

            cols = pair_cols(p)
            second = lanes((size, 128)) >= HEAD
            deltas = []
            for i in range(TGT // size):
                rows = slice(i * size, (i + 1) * size)
                invs = [head_col(r.inv[rows, :], 2 * p + a) for a in (0, 1)]
                scaled = go[rows, cols].astype(F32) * jnp.where(second, invs[1], invs[0])
                gs[rows, :] = scaled.astype(BF)
                product = scaled * r.v_low[rows, cols].astype(F32)
                deltas.append(
                    [
                        jnp.sum(jnp.where(second == bool(a), product, 0.0), -1, keepdims=True)
                        for a in (0, 1)
                    ]
                )
            qt[...] = r.v_q[:, cols].T
            gt[...] = gs[...].T
            fetch(p).wait()
            slot = ebuf.at[p % 2]
            for i in reversed(range(TGT // size)):
                rows = slice(i * size, (i + 1) * size)
                found = []
                for a in (0, 1):
                    own_g = pick(second == bool(a), gs[rows, :])
                    head = slice(HEAD * a, HEAD * a + HEAD)
                    last = (i + 1) * size
                    place = i * (i + 1) // 2
                    e = jnp.concatenate([slot[a, place + j] for j in range(i + 1)], 1)
                    dprob = dot_nt(own_g, r.v_v[0:last, cols])
                    ds = (e.astype(F32) * (dprob - deltas[i][a])).astype(BF)
                    found.append(dot(ds, r.v_k[0:last, cols]))
                    part_k = dot(qt[head, rows], ds)
                    part_v = dot(gt[head, rows], e)
                    if last == TGT:
                        dkt[head, :] = part_k
                        dvt[head, :] = part_v
                    else:
                        dkt[head, 0:last] += part_k
                        dvt[head, 0:last] += part_v
                rights[0, rows, cols] = (
                    jnp.where(second, found[1], found[0]).astype(BF).astype(F32) * SCALE
                ).astype(BF)
            rights[1, :, cols] = dkt[...].T.astype(BF)
            rights[2, :, cols] = dvt[...].T.astype(BF)
            r.vec[10:11, cols] = col_sum(rights[0, :, cols].astype(F32)) * (1.0 / nb)
            r.vec[11:12, cols] = col_sum(rights[2, :, cols].astype(F32)) * (1.0 / nb)

        square_block = pltpu.VMEM((mrows, D), BF)

        def memory_part(wk, wv, key, value, lse_t, delta_t):
            c_kv = [load(r.wk, wk), load(r.wv, wv)]

            g_co.finish()
            c_n3.wait()
            oc = r.n3_all
            member = jnp.where(
                lax.broadcasted_iota(jnp.int32, (16, D), 1) // HEAD
                == lax.broadcasted_iota(jnp.int32, (16, D), 0),
                1.0,
                0.0,
            ).astype(BF)
            for i in range(4):
                rows = slice(256 * i, 256 * i + 256)
                grad_out = dot_nt(rows_of(r.co_all, i), r.v_wo[...]).astype(BF)
                oc[two(i)] = grad_out.reshape(2, 128, D)
                product = grad_out.astype(F32) * rows_of(r.low_all, i).astype(F32)
                big = product.astype(BF)
                small = (product - big.astype(F32)).astype(BF)
                delta_t[:, rows] = dot_nt(member, big) + dot_nt(member, small)
                lse_t[:, rows] = jnp.concatenate([r.stats_all[2 * i], r.stats_all[2 * i + 1]], 1)
            for c in c_kv:
                c.wait()
            key[...] = dot(r.mem_all[me], wk[...]).astype(BF)
            value[...] = (dot(r.mem_all[me], wv[...]) + par(VBIAS)).astype(BF)
            self_middle(0)
            position = me * mrows + lax.broadcasted_iota(jnp.int32, (mrows, 1), 0)
            live = position < r.length[0]
            second = lanes((mrows, 128)) >= HEAD

            @pl.loop(0, 6)
            def _(p):
                cols = pair_cols(p)
                found_k, found_v = [], []
                for a in (0, 1):
                    sel = second == bool(a)
                    s = dot_nt(pick(sel, key[:, cols]), r.query[:, cols])
                    pr = jnp.where(live, jnp.exp(s - lse_t[pl.ds(2 * p + a, 1), :]), 0.0)
                    dprob = dot_nt(pick(sel, value[:, cols]), oc[:, :, cols].reshape(TGT, 128))
                    ds = (pr * (dprob - delta_t[pl.ds(2 * p + a, 1), :])).astype(BF)
                    found_k.append(dot(ds, r.query[:, cols]))
                    found_v.append(dot(pr.astype(BF), oc[:, :, cols].reshape(TGT, 128)))
                r.trade_src[0, :, cols] = jnp.where(second, found_k[1], found_k[0]).astype(BF)
                r.trade_src[1, :, cols] = jnp.where(second, found_v[1], found_v[0]).astype(BF)

            c_h1.start()
            trade_start(inner_slot)
            dk, dv = r.trade_src[0], r.trade_src[1]
            r.mem_grad[...] = (dot_nt(dk, wk[...]) + dot_nt(dv, wv[...])).astype(BF)
            r.vec[12:13, :] = col_sum(dv.astype(F32))

        half = pl.ds(pl.multiple_of((me % 2) * 384, 128), 384)

        c_h1 = pltpu.make_async_copy(r.h1_o, r.query, r.load_sem.at[next(free)])

        def form_cross():
            @pl.when(me % 5 != 1)
            def _():
                r.right[me] = r.trade_src[(me // 2 + 2) % 3, :, half]
                for k in range(1, nb):
                    trade(k, (me + k) % nb, (me + nb - k) % nb).wait_recv()

            @pl.when(me % 5 == 1)
            def _():
                r.right[...] = r.co_all[:, :, half]

            def product(left):
                @pl.loop(0, 3)
                def _(c):
                    r.slab_cross[span(c), :] = dot_tn(
                        left(span(c)), r.right[...].reshape(TGT, 384)
                    ).astype(BF)

            c_h1.wait()
            pl.when(inner_slot(me))(
                lambda: product(lambda cols: r.mem_all[:, :, cols].reshape(TGT, 256))
            )
            pl.when(me % 7 == 0)(lambda: product(lambda cols: r.query[:, cols]))
            pl.when(me % 5 == 1)(
                lambda: product(lambda cols: r.low_all[:, :, cols].reshape(TGT, 256))
            )
            share_start(0)
            share_start(1)

        def self_slab(n):
            slab = parts[n][0]

            @pl.loop(0, 3)
            def _(c):
                rows = span(c)
                for weight in range(3):
                    slab[rows, 384 * weight : 384 * weight + 384] = dot_tn(
                        r.v_x[:, rows], rights[weight, :, 384 * n : 384 * n + 384]
                    ).astype(BF)
                if n == 0:
                    slab[rows, 1152:] = dot_tn(
                        r.v_low[:, rows], r.so_all[...].reshape(TGT, D)
                    ).astype(BF)

            self_start(n)

        def run_memory():
            pl.run_scoped(
                memory_part,
                square, square, square_block, square_block,
                pltpu.VMEM((16, TGT), F32), pltpu.VMEM((16, TGT), F32),
            )

        @pl.loop(0, 6)
        def _(p):
            pl.when(p == 1)(lambda: trade_start(lambda slot: slot % 7 == 0))

            pl.when(p == 2)(lambda: settle(3))

            @pl.when(p == 3)
            def _():
                self_slab(0)
                settle(2)
                run_memory()
                g_groups[3].inner_forward()
                g_groups[3].end_forward(0)

            @pl.when(p == 4)
            def _():
                g_groups[3].end_forward(1, 2)
                g_groups[2].inner_forward(0)

            @pl.when(p == 5)
            def _():
                form_cross()
                g_groups[2].inner_forward(1, 2)
                g_groups[2].end_forward(0)

            one_pair(p)

        self_slab(1)
        vectors_start()
        settle(0)
        settle(1)
        g_groups[2].end_forward(1, 2)
        self_middle(1)

        @pl.loop(0, 4)
        def _(i):
            rows = span(i)
            sq, sk, sv = rights[0, rows, :], rights[1, rows, :], rights[2, rows, :]
            go[rows, :] = (
                rows_of(r.so_all, i).astype(F32)
                + dot_nt(sq, r.v_sq[...])
                + dot_nt(sk, r.v_sk[...])
                + dot_nt(sv, r.v_sv[...])
            ).astype(BF)

            pl.when(i == 1)(lambda: g_groups[0].inner_forward(0))

            @pl.when(i == 3)
            def _():
                g_groups[0].inner_forward(1, 2)
                g_groups[1].inner_forward(0)

        c_grad = load(go, r.input_grad)
        g_groups[0].end_forward(0)
        g_groups[1].inner_forward(1, 2)
        vectors_spread()
        g_groups[0].end_forward(1, 2)
        g_groups[1].end_forward()
        c_grad.wait()


    pl.run_scoped(
        self_part,
        pltpu.VMEM(wide, BF), pltpu.VMEM((TGT, 128), BF), pltpu.VMEM((3,) + wide, BF),
        pltpu.VMEM((128, TGT), F32), pltpu.VMEM((128, TGT), F32),
        pltpu.VMEM((128, TGT), BF), pltpu.VMEM((128, TGT), BF),
        pltpu.VMEM((D, 1920), BF), pltpu.VMEM((D, 1152), BF),
        pltpu.VMEM((2, 2, 10, 256, 256), BF), pltpu.SemaphoreType.DMA((2,)),
    )

    outs = []

    def collect(g, src, dst):
        g_groups[g].finish()
        outs.append(load(src, dst))

    collect(3, r.ag_out, r.ag_out_o)
    collect(2, r.ag, r.ag_o)
    self_end(0)
    outs.append(load(r.chip_e, r.self_e_o))
    self_end(1)
    outs.append(load(r.chip_l, r.self_l_o))
    for g in (0, 1):
        collect(g, r.ag_c.at[g], r.ag_c_o.at[g])
    for k in range(1, nb):
        vspread(k, (me + nb - k) % nb).wait_recv()
    total = r.vall[0]
    for b in range(1, nb):
        total = total + r.vall[b]
    r.vec_out[...] = total
    for k in range(1, nb):
        target = (me + k) % nb
        pl.when(target % 5 != 1)(lambda: trade(k, target, me).wait_send())
        vspread(k, me).wait_send()
    for c in outs:
        c.wait()


FINISH_IN = (
    "n3", "grad_in", "mem_in", "ag", "ag_c", "ag_out", "self_e", "self_l", "vec", "gain", "shift",
)
FINISH_OUT = (
    "out", "input_grad", "mem_grad", "s_q", "s_k", "s_v", "s_o", "c_k", "c_v", "c_q", "c_o", "f_in",
    "f_out", "self_bias", "cross_bias", "cv", "d_gain", "d_shift", "in_bias", "out_bias",
)
FINISH_SCRATCH = ("v_e", "v_l", "v_ag", "v_c", "v_ag_out", "v_n3", "v_f", "v_in", "v_out", "v_y", "v_grad", "v_mem", "v_small", "v_wide", "sem")


def finish_part(nb, ndp, *refs):
    r = Refs(FINISH_IN + FINISH_OUT + FINISH_SCRATCH, refs)
    dp = lax.axis_index("dp")
    quarter = D // ndp
    free = iter(range(40))

    def move(src, dst):
        copy = pltpu.make_async_copy(src, dst, r.sem.at[next(free)])
        copy.start()
        return copy

    c_self = [move(r.self_e, r.v_e), move(r.self_l, r.v_l)]
    c_ag = [move(r.ag_c, r.v_c), move(r.ag, r.v_ag)]
    c_out, c_n3 = move(r.ag_out, r.v_ag_out), move(r.n3, r.v_n3)
    c_grad, c_mem = move(r.grad_in, r.v_grad), move(r.mem_in, r.v_mem)
    done = []
    vec = r.vec
    smalls = (
        (r.self_bias, (10, 11, 6)), (r.cross_bias, (7, 8)), (r.d_gain, (0, 1, 2)),
        (r.d_shift, (3, 4, 5)), (r.cv, (12,)), (r.out_bias, (9,)),
    )
    for m, (ref, rows) in enumerate(smalls):
        for n, row in enumerate(rows):
            r.v_small[m, n : n + 1, :] = vec[row : row + 1, 0:quarter]
        done.append(move(r.v_small.at[m, pl.ds(0, len(rows))], ref))
    for n in range(ndp):
        r.v_wide[:, quarter * n : quarter * n + quarter] = vec[16 + n : 17 + n, 0:quarter]
    done.append(move(r.v_wide, r.in_bias))
    for c in c_self:
        c.wait()

    @pl.loop(0, quarter // 48)
    def _(i):
        rows = span(i, 48)
        for n in range(3):
            cols = slice(384 * n, 384 * n + 384)
            r.v_f[n, rows, 0:384] = r.v_e[rows, cols].astype(F32)
            r.v_f[n, rows, 384:] = r.v_l[rows, cols].astype(F32)
        r.v_f[3, rows, :] = r.v_e[rows, 1152:].astype(F32)

    for n, dst in enumerate((r.s_q, r.s_k, r.s_v, r.s_o)):
        done.append(move(r.v_f.at[n], dst))
    c_ag[0].wait()

    @pl.loop(0, quarter // 48)
    def _(i):
        rows = span(i, 48)
        for b, n in enumerate((4, 7, 5, 5, 6, 6, 7, 4)):
            half = slice(384 * (b % 2), 384 * (b % 2) + 384)
            r.v_f[n, rows, half] = r.v_c[i // 2, b, span(i % 2, 48), :].astype(F32)

    for n, dst in enumerate((r.c_q, r.c_k, r.c_v, r.c_o)):
        done.append(move(r.v_f.at[4 + n], dst))
    c_grad.wait()
    c_mem.wait()
    done += [move(r.v_grad, r.input_grad), move(r.v_mem, r.mem_grad)]
    c_ag[1].wait()

    @pl.loop(0, quarter // 48)
    def _(i):
        rows = span(i, 48)
        for b in range(nb):
            for t in range(3):
                col = D * ((b + t) % 4) + 128 * (2 * t + b // 4)
                r.v_in[rows, col : col + 128] = r.v_ag[
                    b, rows, 128 * t : 128 * t + 128
                ].astype(F32)

    done.append(move(r.v_in, r.f_in))
    c_out.wait()

    @pl.loop(0, nb)
    def _(b):
        t = (dp - b + nb) % 4

        @pl.when(t < 3)
        def _():
            place = pl.ds(pl.multiple_of(128 * (2 * t + b // 4), 128), 128)
            r.v_out[place, :] = r.v_ag_out[b].astype(F32)

    done.append(move(r.v_out, r.f_out))
    c_n3.wait()
    gain, shift = r.gain[...].astype(F32)[2:3, :], r.shift[...].astype(F32)[2:3, :]

    @pl.loop(0, nb)
    def _(b):
        r.v_y[b] = (r.v_n3[b].astype(F32) * gain + shift).astype(BF)

    done.append(move(r.v_y, r.out))
    for c in done:
        c.wait()


def shared_work(
    nb, ndp,
    inputs, memory, lengths, cotangent, self_query, self_key, self_value, self_out, self_bias,
    cross_query, cross_key, cross_value, cross_out, cross_bias, cross_value_bias,
    norm_gain, norm_bias, ffn_in, ffn_in_bias, ffn_out, ffn_out_bias,
):
    own_rows = TGT // nb
    x, mem, cot = inputs[0], memory[0], cotangent[0]
    mrows = mem.shape[0]
    quarter = D // ndp
    gain, shift = norm_gain.T, norm_bias.T
    vecs = (
        jnp.concatenate([cross_value_bias, ffn_out_bias, ffn_in_bias]).reshape(6, D).astype(F32)
    )
    wide, own, square, block = (TGT, D), (own_rows, D), (D, D), (nb, own_rows, D)
    dma = pltpu.SemaphoreType.DMA
    vm = pltpu.VMEM
    n3, grad_in, mem_grad, ag, ag_c, ag_out, self_e, self_l, vec, _, _ = call(
        functools.partial(layer_part, nb, ndp),
        "layer_part",
        (lengths, mem, x, cot, self_query, self_key, self_value, self_out, cross_query, cross_key,
         cross_value, cross_out, ffn_in, ffn_out, gain, shift, self_bias.T, cross_bias.T, vecs),
        [(block, BF), (wide, BF), ((mrows, D), BF), ((nb, quarter, 384), BF),
         ((2, nb, quarter // 2, 384), BF), ((nb, 128, D), BF), ((quarter, 1920), BF), ((quarter, 1152), BF), ((24, 256), F32), (wide, BF), ((6, 2, 10, 256, 256), BF)],
        [vm((16, D), F32), vm((1, FF), F32), vm(wide, BF)]
        + [vm(square, BF)] * 6
        + [vm(wide, BF)] * 4
        + [vm((TGT, 128), F32), vm(own, BF), vm(own, F32), vm(wide, BF), vm((nb, mrows, D), BF)]
        + [vm(block, BF)] * 4
        + [vm((nb, 16, own_rows), F32), vm((3, own_rows, D), BF), vm((nb, own_rows, 384), BF)]
        + [vm((2, quarter, 1920), BF), vm((2, quarter, 1152), BF),
           vm((quarter, 1920), BF), vm((quarter, 1152), BF)]
        + [vm((D, 384), BF)] * 2
        + [vm((4, 128, D), BF), vm((ndp, quarter, 384), BF), vm((2, ndp, quarter // 2, 384), BF),
           vm((ndp, 128, D), BF), vm((2, nb, quarter // 2, 384), BF), vm((nb, quarter, 384), BF),
           vm((nb, 128, D), BF),
           vm((24, D), F32), vm((ndp, 24, 256), F32), vm((ndp, 24, 256), F32), vm((nb, 24, 256), F32)]
        + [dma((64,)), dma((nb,)), dma((nb,)), dma((4, ndp)), dma((4, ndp)), dma((10, 16)),
           dma((10, 16)), dma((2, nb)), dma((2, nb)), dma((2, 3)), dma((2, 3))],
        collective_id=0,
        in_specs=[SMEM] + [ANY] * 13 + [VMEM] * 5,
        out_specs=[ANY] * 2 + [VMEM] + [ANY] * 5 + [VMEM] + [ANY] * 2,
    )
    weight = ((quarter, D), F32)
    (
        out, input_grad, memory_grad, s_q, s_k, s_v, s_o, c_k, c_v, c_q, c_o, f_in, f_out,
        g_self_bias, g_cross_bias, g_cv, g_gain, g_shift, g_in_bias, g_out_bias,
    ) = call(
        functools.partial(finish_part, nb, ndp),
        "finish_part",
        (n3, grad_in, mem_grad, ag, ag_c, ag_out, self_e, self_l, vec, gain, shift),
        [(block, BF), (wide, BF), ((mrows, D), BF)]
        + [weight] * 8
        + [((quarter, FF), F32), ((FF // ndp, D), F32), ((3, quarter), F32), ((2, quarter), F32),
           ((1, quarter), F32), ((3, quarter), F32), ((3, quarter), F32), ((1, FF // ndp), F32),
           ((1, quarter), F32)],
        [vm((quarter, 1920), BF), vm((quarter, 1152), BF), vm((nb, quarter, 384), BF),
         vm((2, nb, quarter // 2, 384), BF),
         vm((nb, 128, D), BF), vm(block, BF),
         vm((8, quarter, D), F32), vm((quarter, FF), F32), vm((FF // ndp, D), F32), vm(block, BF),
         vm(wide, BF), vm((mrows, D), BF), vm((6, 8, quarter), F32), vm((1, FF // ndp), F32),
         dma((40,))],
        in_specs=[ANY] * 8 + [VMEM] * 3,
        out_specs=[ANY] * 20,
    )
    return (
        out.reshape(1, TGT, D), input_grad[None], memory_grad[None],
        s_q, s_k, s_v, s_o, g_self_bias.T, c_q, c_k, c_v, c_o, g_cross_bias.T, g_cv.reshape(quarter),
        g_gain.T, g_shift.T, f_in, g_in_bias.reshape(FF // ndp), f_out, g_out_bias.reshape(quarter),
    )


def merged(array, axis, join):
    gathered = jax.tree.map(
        lambda a, kind: lax.all_gather(a.astype(kind), axis), array, (jnp.bfloat16, jnp.bfloat16)
    )

    def take(source):
        return jax.tree.map(
            lambda a, own: lax.dynamic_index_in_dim(a, source, 0, False).astype(own.dtype),
            gathered,
            array,
        )

    return lax.fori_loop(
        1, lax.axis_size(axis), lambda source, state: join(state, take(source)), take(0)
    )


def layer_norm(residual, gain_col, shift_col):
    average = jnp.mean(residual, axis=-1, keepdims=True)
    centered = residual - average
    variance = jnp.mean(centered * centered, axis=-1, keepdims=True)
    return centered * lax.rsqrt(variance + EPS) * gain_col + shift_col


def exact_gelu(values):
    return jax.nn.gelu(values, approximate=False)


def project(left_side, weight):
    return jnp.dot(left_side, weight, preferred_element_type=jnp.float32)


def project_back(gradient, weight):
    return lax.dot_general(
        gradient, weight, (((1,), (1,)), ((), ())), preferred_element_type=jnp.float32
    )


def weight_grad(left_side, gradient):
    return lax.dot_general(
        left_side, gradient, (((0,), (0,)), ((), ())), preferred_element_type=jnp.float32
    )


def column_sum(gradient):
    return jnp.sum(gradient.astype(jnp.float32), axis=0)


def split_heads(values):
    return values.reshape(values.shape[:-1] + (HEADS, HEAD))


def combine_totals(earlier, latter):
    top_a, sum_a = earlier
    top_b, sum_b = latter
    top_score = jnp.maximum(top_a, top_b)
    return (top_score, sum_a * jnp.exp(top_a - top_score) + sum_b * jnp.exp(top_b - top_score))


def self_scores(query_rows, key_rows, row_start, block_rows):
    scores = jnp.einsum("qhe,khe->hqk", query_rows, key_rows, preferred_element_type=jnp.float32)
    row_pos = row_start + jnp.arange(block_rows)[:, None]
    col_pos = jnp.arange(key_rows.shape[0])[None, :]
    return jnp.where((col_pos <= row_pos)[None], scores, NEG)


def copied_work(
    inputs,
    memory,
    lengths,
    cotangent,
    self_query,
    self_key,
    self_value,
    self_out,
    self_bias,
    cross_query,
    cross_key,
    cross_value,
    cross_out,
    cross_bias,
    cross_value_bias,
    norm_gain,
    norm_bias,
    ffn_in,
    ffn_in_bias,
    ffn_out,
    ffn_out_bias,
):
    all_rows = ITEMS * TGT
    block_rows = min(512, TGT)
    mem_rows = memory.shape[1]
    self_bias_f = self_bias.astype(jnp.float32)
    cross_bias_f = cross_bias.astype(jnp.float32)
    gains = norm_gain.astype(jnp.float32)
    shifts = norm_bias.astype(jnp.float32)
    flat_in = inputs.reshape(all_rows, D)
    query_self = split_heads(
        ((project(flat_in, self_query) + self_bias_f[:, 0]) * SCALE)
        .astype(jnp.bfloat16)
        .reshape(ITEMS, TGT, D)
    )
    key_self = split_heads(project(flat_in, self_key).astype(jnp.bfloat16).reshape(ITEMS, TGT, D))
    value_self = split_heads(
        (project(flat_in, self_value) + self_bias_f[:, 1])
        .astype(jnp.bfloat16)
        .reshape(ITEMS, TGT, D)
    )
    item_index = 0
    attn_blocks = []
    lse_blocks = []
    for row_start in range(0, TGT, block_rows):
        row_end = row_start + block_rows
        scores = self_scores(
            query_self[item_index, row_start:row_end],
            key_self[item_index, :row_end],
            row_start,
            block_rows,
        )
        top_score = jnp.max(scores, axis=-1, keepdims=True)
        log_total = top_score + jnp.log(
            jnp.sum(jnp.exp(scores - top_score), axis=-1, keepdims=True)
        )
        probs_low = jnp.exp(scores - log_total).astype(jnp.bfloat16)
        attn_blocks.append(
            jnp.einsum(
                "hqk,khe->qhe",
                probs_low,
                value_self[item_index, :row_end],
                preferred_element_type=jnp.float32,
            )
        )
        lse_blocks.append(log_total)
    attn_items = [jnp.concatenate(attn_blocks, axis=0)]
    lse_self = [lse_blocks]
    self_attn = jnp.stack(attn_items, axis=0)
    self_low = self_attn.astype(jnp.bfloat16).reshape(all_rows, D)
    resid_one = flat_in.astype(jnp.float32) + project(self_low, self_out) + self_bias_f[:, 2]
    hidden_one, norm1_back = jax.vjp(layer_norm, resid_one, gains[:, 0], shifts[:, 0])
    hidden_low = hidden_one.astype(jnp.bfloat16)
    query_cross = split_heads(
        ((project(hidden_low, cross_query) + cross_bias_f[:, 0]) * SCALE)
        .astype(jnp.bfloat16)
        .reshape(ITEMS, TGT, D)
    )
    flat_mem = memory.reshape(ITEMS * mem_rows, D)
    key_cross = split_heads(
        project(flat_mem, cross_key).astype(jnp.bfloat16).reshape(ITEMS, mem_rows, D)
    )
    value_cross = split_heads(
        (project(flat_mem, cross_value) + cross_value_bias.astype(jnp.float32))
        .astype(jnp.bfloat16)
        .reshape(ITEMS, mem_rows, D)
    )
    position = lax.axis_index("blk") * mem_rows + jnp.arange(mem_rows)
    live_mask = position[None, :] < lengths[:, None]

    def cross_scores():
        raw_scores = jnp.einsum(
            "bqhe,bkhe->bhqk", query_cross, key_cross, preferred_element_type=jnp.float32
        )
        return jnp.where(live_mask[:, None, None, :], raw_scores, NEG)

    scores = cross_scores()
    top_local = jnp.max(scores, axis=-1)
    sum_local = jnp.sum(jnp.exp(scores - top_local[..., None]), axis=-1)
    top_all, sum_all = merged((top_local, sum_local), "blk", combine_totals)
    cross_lse = top_all + jnp.log(sum_all)
    probs_low = jnp.exp(scores - cross_lse[..., None]).astype(jnp.bfloat16)
    share_out = jnp.einsum(
        "bhqk,bkhe->bqhe", probs_low, value_cross, preferred_element_type=jnp.float32
    ).reshape(all_rows, D)
    cot_flat = cotangent.reshape(all_rows, D)
    attn_rows = lax.psum(share_out, "blk")
    cross_low = attn_rows.astype(jnp.bfloat16)
    resid_two = hidden_one + project(cross_low, cross_out) + cross_bias_f[:, 1]
    hidden_two, norm2_back = jax.vjp(layer_norm, resid_two, gains[:, 1], shifts[:, 1])
    second_low = hidden_two.astype(jnp.bfloat16)
    pre_act = project(second_low, ffn_in) + ffn_in_bias.astype(jnp.float32)
    activated, gelu_back = jax.vjp(exact_gelu, pre_act)
    act_low = activated.astype(jnp.bfloat16)
    resid_three = hidden_two + project(act_low, ffn_out) + ffn_out_bias.astype(jnp.float32)
    result, norm3_back = jax.vjp(layer_norm, resid_three, gains[:, 2], shifts[:, 2])
    result_low = result.astype(jnp.bfloat16)
    grad_r3, grad_gain3, grad_shift3 = norm3_back(cot_flat.astype(jnp.float32))
    z_low = grad_r3.astype(jnp.bfloat16)
    g_ffn_out = weight_grad(act_low, z_low)
    g_ffn_out_bias = column_sum(z_low)
    (grad_pre,) = gelu_back(project_back(z_low, ffn_out))
    pre_low = grad_pre.astype(jnp.bfloat16)
    g_ffn_in = weight_grad(second_low, pre_low)
    g_ffn_in_bias = column_sum(pre_low)
    grad_h2 = grad_r3 + project_back(pre_low, ffn_in)
    grad_r2, grad_gain2, grad_shift2 = norm2_back(grad_h2)
    co_low = grad_r2.astype(jnp.bfloat16)
    g_cross_out = weight_grad(cross_low, co_low)
    g_co_bias = column_sum(co_low)
    oc_low = project_back(co_low, cross_out).astype(jnp.bfloat16)
    out_rows = result_low.reshape(ITEMS, TGT, D)
    grad_oc = split_heads(oc_low.reshape(ITEMS, TGT, D))
    cross_delta = jnp.transpose(
        jnp.sum(
            grad_oc.astype(jnp.float32) * split_heads(attn_rows.reshape(ITEMS, TGT, D)), axis=-1
        ),
        (0, 2, 1),
    )
    scores = cross_scores()
    prob_full = jnp.exp(scores - cross_lse[..., None])
    grad_probs = jnp.einsum(
        "bqhe,bkhe->bhqk", grad_oc, value_cross, preferred_element_type=jnp.float32
    )
    grad_scores = (prob_full * (grad_probs - cross_delta[..., None])).astype(jnp.bfloat16)
    query_share = jnp.einsum(
        "bhqk,bkhe->bqhe", grad_scores, key_cross, preferred_element_type=jnp.float32
    ).reshape(all_rows, D)
    key_low = (
        jnp.einsum("bhqk,bqhe->bkhe", grad_scores, query_cross, preferred_element_type=jnp.float32)
        .astype(jnp.bfloat16)
        .reshape(ITEMS * mem_rows, D)
    )
    value_low = (
        jnp.einsum(
            "bhqk,bqhe->bkhe",
            prob_full.astype(jnp.bfloat16),
            grad_oc,
            preferred_element_type=jnp.float32,
        )
        .astype(jnp.bfloat16)
        .reshape(ITEMS * mem_rows, D)
    )
    grad_cq = lax.psum(query_share, "blk")
    cq_low = (grad_cq * SCALE).astype(jnp.bfloat16)
    g_cross_query = weight_grad(hidden_one.astype(jnp.bfloat16), cq_low)
    g_cq_bias = column_sum(cq_low)
    grad_h1_rows = grad_r2 + project_back(cq_low, cross_query)
    g_cross_key_dev = weight_grad(flat_mem, key_low)
    g_cross_value_dev = weight_grad(flat_mem, value_low)
    g_cv_bias_dev = column_sum(value_low)
    memory_grad = (
        (project_back(key_low, cross_key) + project_back(value_low, cross_value))
        .astype(jnp.bfloat16)
        .reshape(ITEMS, mem_rows, D)
    )
    g_cross_key, g_cross_value, g_cv_bias = lax.psum(
        (g_cross_key_dev, g_cross_value_dev, g_cv_bias_dev), "blk"
    )
    grad_r1, grad_gain1, grad_shift1 = norm1_back(grad_h1_rows)
    so_low = grad_r1.astype(jnp.bfloat16)
    g_self_out = weight_grad(self_low, so_low)
    g_so_bias = column_sum(so_low)
    grad_os = split_heads(
        project_back(so_low, self_out).astype(jnp.bfloat16).reshape(ITEMS, TGT, D)
    )
    item_index = 0
    key_grad = jnp.zeros((TGT, HEADS, HEAD), jnp.float32)
    value_grad = jnp.zeros((TGT, HEADS, HEAD), jnp.float32)
    query_blocks = []
    for row_start in range(0, TGT, block_rows):
        row_end = row_start + block_rows
        query_rows = query_self[item_index, row_start:row_end]
        key_rows = key_self[item_index, :row_end]
        scores = self_scores(query_rows, key_rows, row_start, block_rows)
        prob_full = jnp.exp(scores - lse_self[item_index][row_start // block_rows])
        grad_out = grad_os[item_index, row_start:row_end]
        row_delta = jnp.transpose(
            jnp.sum(
                grad_out.astype(jnp.float32) * self_attn[item_index, row_start:row_end], axis=-1
            )
        )
        grad_probs = jnp.einsum(
            "qhe,khe->hqk",
            grad_out,
            value_self[item_index, :row_end],
            preferred_element_type=jnp.float32,
        )
        grad_scores = (prob_full * (grad_probs - row_delta[:, :, None])).astype(jnp.bfloat16)
        query_blocks.append(
            jnp.einsum("hqk,khe->qhe", grad_scores, key_rows, preferred_element_type=jnp.float32)
        )
        key_grad = key_grad.at[:row_end].add(
            jnp.einsum("hqk,qhe->khe", grad_scores, query_rows, preferred_element_type=jnp.float32)
        )
        value_grad = value_grad.at[:row_end].add(
            jnp.einsum(
                "hqk,qhe->khe",
                prob_full.astype(jnp.bfloat16),
                grad_out,
                preferred_element_type=jnp.float32,
            )
        )
    query_items = [jnp.concatenate(query_blocks, axis=0)]
    key_items = [key_grad]
    value_items = [value_grad]
    sq_low = (jnp.stack(query_items, 0).astype(jnp.bfloat16) * jnp.bfloat16(SCALE)).reshape(
        all_rows, D
    )
    sk_low = jnp.stack(key_items, 0).astype(jnp.bfloat16).reshape(all_rows, D)
    sv_low = jnp.stack(value_items, 0).astype(jnp.bfloat16).reshape(all_rows, D)
    g_self_query = weight_grad(flat_in, sq_low)
    g_self_key = weight_grad(flat_in, sk_low)
    g_self_value = weight_grad(flat_in, sv_low)
    g_sq_bias = column_sum(sq_low)
    g_sv_bias = column_sum(sv_low)
    input_grad = (
        (
            grad_r1
            + project_back(sq_low, self_query)
            + project_back(sk_low, self_key)
            + project_back(sv_low, self_value)
        )
        .astype(jnp.bfloat16)
        .reshape(ITEMS, TGT, D)
    )
    g_self_bias = jnp.stack([g_sq_bias, g_sv_bias, g_so_bias], axis=1)
    g_cross_bias = jnp.stack([g_cq_bias, g_co_bias], axis=1)
    g_norm_gain = jnp.stack([grad_gain1, grad_gain2, grad_gain3], axis=1)
    g_norm_bias = jnp.stack([grad_shift1, grad_shift2, grad_shift3], axis=1)
    summed = (
        lax.psum_scatter(
            g_self_query.astype(jnp.bfloat16), "dp", scatter_dimension=0, tiled=True
        ).astype(jnp.float32),
        lax.psum_scatter(
            g_self_key.astype(jnp.bfloat16), "dp", scatter_dimension=0, tiled=True
        ).astype(jnp.float32),
        lax.psum_scatter(
            g_self_value.astype(jnp.bfloat16), "dp", scatter_dimension=0, tiled=True
        ).astype(jnp.float32),
        lax.psum_scatter(
            g_self_out.astype(jnp.bfloat16), "dp", scatter_dimension=0, tiled=True
        ).astype(jnp.float32),
        lax.psum_scatter(
            g_cross_query.astype(jnp.bfloat16), "dp", scatter_dimension=0, tiled=True
        ).astype(jnp.float32),
        lax.psum_scatter(
            g_cross_key.astype(jnp.bfloat16), "dp", scatter_dimension=0, tiled=True
        ).astype(jnp.float32),
        lax.psum_scatter(
            g_cross_value.astype(jnp.bfloat16), "dp", scatter_dimension=0, tiled=True
        ).astype(jnp.float32),
        lax.psum_scatter(
            g_cross_out.astype(jnp.bfloat16), "dp", scatter_dimension=0, tiled=True
        ).astype(jnp.float32),
        lax.psum_scatter(
            g_ffn_in.astype(jnp.bfloat16), "dp", scatter_dimension=0, tiled=True
        ).astype(jnp.float32),
        lax.psum_scatter(
            g_ffn_out.astype(jnp.bfloat16), "dp", scatter_dimension=0, tiled=True
        ).astype(jnp.float32),
        lax.psum_scatter(
            g_self_bias.astype(jnp.bfloat16), "dp", scatter_dimension=0, tiled=True
        ).astype(jnp.float32),
        lax.psum_scatter(
            g_cross_bias.astype(jnp.bfloat16), "dp", scatter_dimension=0, tiled=True
        ).astype(jnp.float32),
        lax.psum_scatter(
            g_cv_bias.astype(jnp.bfloat16), "dp", scatter_dimension=0, tiled=True
        ).astype(jnp.float32),
        lax.psum_scatter(
            g_norm_gain.astype(jnp.bfloat16), "dp", scatter_dimension=0, tiled=True
        ).astype(jnp.float32),
        lax.psum_scatter(
            g_norm_bias.astype(jnp.bfloat16), "dp", scatter_dimension=0, tiled=True
        ).astype(jnp.float32),
        lax.psum_scatter(
            g_ffn_in_bias.astype(jnp.bfloat16), "dp", scatter_dimension=0, tiled=True
        ).astype(jnp.float32),
        lax.psum_scatter(
            g_ffn_out_bias.astype(jnp.bfloat16), "dp", scatter_dimension=0, tiled=True
        ).astype(jnp.float32),
    )
    (
        s_query,
        s_key,
        s_value,
        s_out,
        c_query,
        c_key,
        c_value,
        c_out,
        f_in,
        f_out,
        r_self_bias,
        r_cross_bias,
        r_cv_bias,
        r_gain,
        r_shift,
        r_in_bias,
        r_out_bias,
    ) = summed
    return (
        out_rows,
        input_grad,
        memory_grad,
        s_query,
        s_key,
        s_value,
        s_out,
        r_self_bias,
        c_query,
        c_key,
        c_value,
        c_out,
        r_cross_bias,
        r_cv_bias,
        r_gain,
        r_shift,
        f_in,
        r_in_bias,
        f_out,
        r_out_bias,
    )


def solution(mesh):
    nb, ndp = mesh.shape["blk"], mesh.shape["dp"]
    body = copied_work
    if (nb, ndp) == (8, 4):
        body = functools.partial(shared_work, nb, ndp)
    return jax.shard_map(
        body,
        mesh=mesh,
        in_specs=(
            P("dp", None, None),
            P("dp", "blk", None),
            P("dp"),
            P("dp", None, None),
            P(),
            P(),
            P(),
            P(),
            P(),
            P(),
            P(),
            P(),
            P(),
            P(),
            P(),
            P(),
            P(),
            P(),
            P(),
            P(),
            P(),
        ),
        out_specs=(
            P("dp", None, None),
            P("dp", None, None),
            P("dp", "blk", None),
            P("dp", None),
            P("dp", None),
            P("dp", None),
            P("dp", None),
            P("dp", None),
            P("dp", None),
            P("dp", None),
            P("dp", None),
            P("dp", None),
            P("dp", None),
            P("dp"),
            P("dp", None),
            P("dp", None),
            P("dp", None),
            P("dp"),
            P("dp", None),
            P("dp"),
        ),
        check_vma=False,
    )
```
